32 devices in a mesh: groups: 2 (over x), cell: 16 (over z, y, core).
Axes of the slice: x: 2, y: 2, z: 4, core: 2. Of those that a mesh axis runs over, the one named last changes fastest.
Arguments:
- atoms: bfloat16 [1024, 49, 128], P(('groups', 'cell')), parts along dimension 0, may hold values from -6 to 6
- frames: bfloat16 [4096, 235], P(('groups', 'cell')), parts along dimension 0, may hold values from -4 to 4
- w_zero: bfloat16 [896, 896], replicated, may hold values from -0.1875 to 0.1875
- w_one: bfloat16 [2, 768, 768], replicated, may hold values from -0.15625 to 0.15625
- w_two: bfloat16 [2, 640, 640], replicated, may hold values from -0.15625 to 0.15625
- cotangent: bfloat16 [1024, 49, 128], P(('groups', 'cell')), parts along dimension 0, may hold values from -6 to 6
- ghost_rows: int32 [512], P(('groups', 'cell')), parts along dimension 0, may hold values from 0 to 31
- send_rows: int32 [512], P(('groups', 'cell')), parts along dimension 0, may hold values from 0 to 47
- recv_rows: int32 [512], P(('groups', 'cell')), parts along dimension 0, may hold values from 0 to 31
- edge_src: int32 [4096], P(('groups', 'cell')), parts along dimension 0, may hold values from 0 to 63
- edge_tgt: int32 [4096], P(('groups', 'cell')), parts along dimension 0, may hold values from 0 to 48, as said below
Outputs:
- update: bfloat16 [1024, 49, 128], P(('groups', 'cell')), parts along dimension 0
- atom_grads: bfloat16 [1024, 49, 128], P(('groups', 'cell')), parts along dimension 0
The draws below stay inside these ranges and needn't reach their ends.
There are 2 independent parts, one for each index of `groups`. The reference program is written for one: setup_inputs(seed, part) draws one part's arguments, and reference() takes and returns one part's arrays. A program takes and returns all parts, laid end to end along the dimension named above; an argument that names none is the same for every part. Nothing has to cross between parts.
Inputs may be any that keep to these rules, and one draw needn't show every extreme that they name: `ghost_rows`: the first 8 entries of a slab's block name its atoms that slab d-1 holds as ghosts, the last 8 those that slab d+1 holds; slabs wrap around. `send_rows`: entry d + s of slab c's block is the row of c's extended table that device d receives as its source row from c in slot s. `recv_rows`: entry d + s of slab c's block is c's atom that device d's target row 32 + c + s stands for. `edge_src`: indexes the device's source table: its extended table, then the received rows ordered by sender. `edge_tgt`: below 32: an own atom; from 32: the received target slot c + s; the largest value marks a padding edge. On each device the padding edges fill whole trailing blocks of 64; in every draw some device has all 2 blocks live and some other device only one.
All inputs are finite; a program needn't handle non-finite values.
Results may differ from the reference program's by a relative error of at most 0.0064.
Values may be sent and summed in bfloat16 or wider, within the bound.
No kernel may reach another device: no remote copies, remote signals or barrier semaphores. Data moves between devices by JAX's collectives and lax.ppermute only.
A program may use at most 64 MiB of HBM per device.

```python
import jax
import jax.numpy as jnp
import numpy as np
from jax import lax

CHANNELS = 128
LMAX = 6
A_DEV = 32
BLK_DEV = 2
SLOT = 1
EDGE = 64
GHOST = 8
COEF = 49
FRAME = 235
ZERO_W = 896
ONE_W = 768
TWO_W = 640
ATOMS = 512
EDGES = 2048
LISTS = 256
GHOSTS_ALL = 256
N_CELL = 16


def frame_scale():
    scales = []
    for degree in range(LMAX + 1):
        extent = min(degree, 2)
        scales = scales + [(2 * degree + 1) ** (-0.5)] * ((2 * extent + 1) * (2 * degree + 1))
    return np.array(scales, np.float32)


def draw_frames(key, part):
    key = jax.random.fold_in(key, 3)
    base = jnp.clip(jax.random.normal(key, (EDGES, FRAME), jnp.float32), -4.0, 4.0)
    return (base * jnp.asarray(frame_scale())[None, :]).astype(jnp.bfloat16)


def draw_edge_tgt(key, part):
    key = jax.random.fold_in(key, 7)
    key_live, key_full, key_thin, key_rows = jax.random.split(key, 4)
    devices = jnp.arange(N_CELL, dtype=jnp.int32)
    live = jax.random.randint(key_live, (N_CELL,), 1, BLK_DEV + 1)
    full_at = jax.random.randint(key_full, (), 0, N_CELL)
    thin_at = (full_at + 1 + jax.random.randint(key_thin, (), 0, N_CELL - 1)) % N_CELL
    live = jnp.where(devices == full_at, BLK_DEV, live)
    live = jnp.where(devices == thin_at, 1, live)
    picked = jax.random.randint(key_rows, (N_CELL, BLK_DEV, EDGE), 0, A_DEV + N_CELL * SLOT)
    blocks = jnp.arange(BLK_DEV, dtype=jnp.int32)[None, :, None]
    result = jnp.where(blocks < live[:, None, None], picked, A_DEV + N_CELL * SLOT)
    return result.reshape(-1).astype(jnp.int32)


def place_ends(values, key, low, largest):
    longest = values.shape.index(max(values.shape))
    spots = []
    for shift in (0, 1):
        where = [jax.random.randint(jax.random.fold_in(key, axis), (), 0, length) for axis, length in enumerate(values.shape)]
        where[longest] = (where[longest] + shift) % values.shape[longest]
        spots.append(tuple(where))
    return values.at[spots[0]].set(low).at[spots[1]].set(largest)


def shard_levels(own_key, shape, cuts, low, high):
    level, own = 1.0, jax.random.fold_in(own_key, 6)
    for position, blocks in cuts:
        heights = jnp.exp(jax.random.uniform(jax.random.fold_in(own, position), (blocks,), jnp.float32, low / len(cuts), high / len(cuts)))
        level = level * jnp.repeat(heights, shape[position] // blocks).reshape([-1 if axis == position else 1 for axis in range(len(shape))])
    return level


def gaussian(rng, dims, deviation, limit, cuts=(), held_as=jnp.bfloat16):
    level = shard_levels(rng, dims, cuts, -0.22, 0.18) if cuts else 1.0
    values = jax.random.normal(rng, dims, jnp.float32) * deviation * level
    return jnp.minimum(jnp.maximum(values, -limit), limit).astype(held_as)


def setup_inputs(seed: int = 0, part: int = 0) -> dict:
    key_list = jax.random.split(jax.random.key(seed), 12)
    part_keys = jax.random.split(jax.random.fold_in(key_list[11], part), 12)
    atoms = gaussian(part_keys[0], (ATOMS, COEF, CHANNELS), 1.0, 6.0, ((0, 16),))
    frames = draw_frames(jax.random.fold_in(jax.random.fold_in(key_list[11], part), 71), part)
    w_zero = gaussian(key_list[2], (ZERO_W, ZERO_W), ZERO_W ** -0.5, 0.1875)
    w_one = gaussian(key_list[3], (2, ONE_W, ONE_W), (2 * ONE_W) ** -0.5, 0.15625)
    w_two = gaussian(key_list[4], (2, TWO_W, TWO_W), (2 * TWO_W) ** -0.5, 0.15625)
    cotangent = gaussian(part_keys[5], (ATOMS, COEF, CHANNELS), 1.0, 6.0, ((0, 16),))
    ghost_rows = place_ends(jax.random.randint(part_keys[6], (GHOSTS_ALL,), 0, A_DEV), jax.random.fold_in(part_keys[6], 1), 0, A_DEV - 1).astype(jnp.int32)
    send_rows = place_ends(jax.random.randint(part_keys[7], (LISTS,), 0, A_DEV + 2 * GHOST), jax.random.fold_in(part_keys[7], 1), 0, (A_DEV + 2 * GHOST) - 1).astype(jnp.int32)
    recv_rows = place_ends(jax.random.randint(part_keys[8], (LISTS,), 0, A_DEV), jax.random.fold_in(part_keys[8], 1), 0, A_DEV - 1).astype(jnp.int32)
    edge_src = place_ends(jax.random.randint(part_keys[9], (EDGES,), 0, A_DEV + 2 * GHOST + N_CELL * SLOT), jax.random.fold_in(part_keys[9], 1), 0, (A_DEV + 2 * GHOST + N_CELL * SLOT) - 1).astype(jnp.int32)
    edge_tgt = draw_edge_tgt(jax.random.fold_in(jax.random.fold_in(key_list[11], part), 71), part)
    return dict(atoms=atoms, frames=frames, w_zero=w_zero, w_one=w_one, w_two=w_two, cotangent=cotangent, ghost_rows=ghost_rows, send_rows=send_rows, recv_rows=recv_rows, edge_src=edge_src, edge_tgt=edge_tgt)


def frame_layout():
    layout = []
    offset = 0
    for degree in range(LMAX + 1):
        extent = min(degree, 2)
        layout.append((degree, degree * degree, 2 * degree + 1, extent, offset))
        offset = offset + (2 * extent + 1) * (2 * degree + 1)
    return layout


def turn_in(coeffs, frames):
    groups = ([], [], [], [], [])
    for degree, anchor, span_size, extent, offset in frame_layout():
        frame_block = frames[:, offset:offset + (2 * extent + 1) * span_size].reshape(-1, 2 * extent + 1, span_size)
        turned = jnp.einsum("eam,emc->eac", frame_block.astype(jnp.float32), coeffs[:, anchor:anchor + span_size].astype(jnp.float32))
        groups[0].append(turned[:, extent])
        if extent >= 1:
            groups[1].append(turned[:, extent + 1])
            groups[2].append(turned[:, extent - 1])
        if extent >= 2:
            groups[3].append(turned[:, extent + 2])
            groups[4].append(turned[:, extent - 2])
    return tuple(jnp.stack(member, axis=1) for member in groups)


def turn_out(parts, frames):
    pieces = []
    for degree, anchor, span_size, extent, offset in frame_layout():
        frame_block = frames[:, offset:offset + (2 * extent + 1) * span_size].reshape(-1, 2 * extent + 1, span_size)
        column = []
        if extent >= 2:
            column.append(parts[4][:, degree - 2])
        if extent >= 1:
            column.append(parts[2][:, degree - 1])
        column.append(parts[0][:, degree])
        if extent >= 1:
            column.append(parts[1][:, degree - 1])
        if extent >= 2:
            column.append(parts[3][:, degree - 2])
        stacked = jnp.stack(column, axis=1)
        pieces.append(jnp.einsum("eam,eac->emc", frame_block.astype(jnp.float32), stacked.astype(jnp.float32)))
    return jnp.concatenate(pieces, axis=1)


def product(left, right):
    return jnp.dot(left, right, preferred_element_type=jnp.float32)


def product_t(left, right):
    return lax.dot_general(left, right, (((1,), (1,)), ((), ())), preferred_element_type=jnp.float32)


def mix(members, w_zero, w_one, w_two):
    edge_count = members[0].shape[0]
    flattened = [member.reshape(edge_count, -1) for member in members]
    zero_out = product(flattened[0], w_zero)
    plus_one = product(flattened[1], w_one[0]) - product(flattened[2], w_one[1])
    minus_one = product(flattened[2], w_one[0]) + product(flattened[1], w_one[1])
    plus_two = product(flattened[3], w_two[0]) - product(flattened[4], w_two[1])
    minus_two = product(flattened[4], w_two[0]) + product(flattened[3], w_two[1])
    results = (zero_out, plus_one, minus_one, plus_two, minus_two)
    return tuple(result.reshape(member.shape) for result, member in zip(results, members))


def mix_back(members, w_zero, w_one, w_two):
    edge_count = members[0].shape[0]
    flattened = [member.reshape(edge_count, -1) for member in members]
    zero_in = product_t(flattened[0], w_zero)
    plus_one = product_t(flattened[1], w_one[0]) + product_t(flattened[2], w_one[1])
    minus_one = product_t(flattened[2], w_one[0]) - product_t(flattened[1], w_one[1])
    plus_two = product_t(flattened[3], w_two[0]) + product_t(flattened[4], w_two[1])
    minus_two = product_t(flattened[4], w_two[0]) - product_t(flattened[3], w_two[1])
    results = (zero_in, plus_one, minus_one, plus_two, minus_two)
    return tuple(result.reshape(member.shape) for result, member in zip(results, members))


def gate(preact):
    scale = jax.nn.sigmoid(preact[0][:, 0])
    return tuple(member * scale[:, None, :] for member in preact)


def gate_back(preact, upstream):
    scale = jax.nn.sigmoid(preact[0][:, 0])
    slope = scale * (1.0 - scale)
    total = sum(jnp.sum(above * below, axis=1) for above, below in zip(upstream, preact))
    lowered = [member * scale[:, None, :] for member in upstream]
    lowered[0] = lowered[0].at[:, 0].add(total * slope)
    return tuple(lowered)


def device_work(source_table, grad_table, frames, sources, targets, w_zero, w_one, w_two):
    picked = source_table[sources]
    rotated = tuple(member.astype(jnp.bfloat16) for member in turn_in(picked, frames))
    preact = mix(rotated, w_zero, w_one, w_two)
    gated = tuple(member.astype(jnp.bfloat16) for member in gate(preact))
    message = turn_out(gated, frames)
    summed = jnp.zeros((grad_table.shape[0],) + message.shape[1:], jnp.float32).at[targets].add(message)
    upstream = turn_in(grad_table[targets], frames)
    lowered = tuple(member.astype(jnp.bfloat16) for member in gate_back(preact, upstream))
    mixed_back = tuple(member.astype(jnp.bfloat16) for member in mix_back(lowered, w_zero, w_one, w_two))
    edge_grad = turn_out(mixed_back, frames)
    gathered = jnp.zeros((source_table.shape[0],) + edge_grad.shape[1:], jnp.float32).at[sources].add(edge_grad)
    return summed, gathered


def rounded(values):
    return lax.optimization_barrier(values.astype(jnp.bfloat16)).astype(jnp.float32)


def reference(atoms, frames, w_zero, w_one, w_two, cotangent, ghost_rows, send_rows, recv_rows, edge_src, edge_tgt):
    owned = atoms.reshape(N_CELL, A_DEV, COEF, CHANNELS)
    upstream_all = cotangent.reshape(N_CELL, A_DEV, COEF, CHANNELS)
    ghost_ids = ghost_rows.reshape(N_CELL, 2 * GHOST)
    packs = jax.vmap(lambda table_rows, index_rows: table_rows[index_rows])(owned, ghost_ids)
    from_prev = jnp.roll(packs[:, GHOST:], 1, axis=0)
    from_next = jnp.roll(packs[:, :GHOST], -1, axis=0)
    extended = jnp.concatenate([owned, from_prev, from_next], axis=1)
    sends = send_rows.reshape(N_CELL, N_CELL, SLOT)
    recvs = recv_rows.reshape(N_CELL, N_CELL, SLOT)
    frame_all = frames.reshape(N_CELL, -1, FRAME)
    sources = edge_src.reshape(N_CELL, -1)
    targets = edge_tgt.reshape(N_CELL, -1)
    senders = jnp.arange(N_CELL, dtype=jnp.int32)
    zero_row = jnp.zeros((1, COEF, CHANNELS), jnp.bfloat16)

    def visit_device(totals, device):
        update_acc, grad_acc = totals
        incoming = extended[senders[:, None], sends[:, device]].reshape(-1, COEF, CHANNELS)
        incoming_grad = upstream_all[senders[:, None], recvs[:, device]].reshape(-1, COEF, CHANNELS)
        source_table = jnp.concatenate([extended[device], incoming], axis=0)
        grad_table = jnp.concatenate([upstream_all[device], incoming_grad, zero_row], axis=0)
        summed, gathered = device_work(source_table, grad_table, frame_all[device], sources[device], targets[device], w_zero, w_one, w_two)
        update_acc = update_acc.at[device].add(summed[:A_DEV])
        remote = rounded(summed[A_DEV:A_DEV + N_CELL * SLOT]).reshape(N_CELL, SLOT, COEF, CHANNELS)
        update_acc = update_acc.at[senders[:, None], recvs[:, device]].add(remote)
        grad_acc = grad_acc.at[device].add(gathered[:A_DEV + 2 * GHOST])
        remote_grad = rounded(gathered[A_DEV + 2 * GHOST:]).reshape(N_CELL, SLOT, COEF, CHANNELS)
        grad_acc = grad_acc.at[senders[:, None], sends[:, device]].add(remote_grad)
        return (update_acc, grad_acc), None

    start = (jnp.zeros((N_CELL, A_DEV, COEF, CHANNELS), jnp.float32),
             jnp.zeros((N_CELL, A_DEV + 2 * GHOST, COEF, CHANNELS), jnp.float32))
    (update_acc, grad_acc), unused = lax.scan(visit_device, start, senders)
    update = update_acc.astype(jnp.bfloat16).reshape(ATOMS, COEF, CHANNELS)
    ghost_back = rounded(grad_acc[:, A_DEV:])
    grads_prev = jnp.roll(ghost_back[:, GHOST:], 1, axis=0)
    grads_next = jnp.roll(ghost_back[:, :GHOST], -1, axis=0)
    arriving = jnp.concatenate([grads_prev, grads_next], axis=1)
    own_grad = jax.vmap(lambda base_rows, index_rows, value_rows: base_rows.at[index_rows].add(value_rows))(grad_acc[:, :A_DEV], ghost_ids, arriving)
    atom_grads = own_grad.astype(jnp.bfloat16).reshape(ATOMS, COEF, CHANNELS)
    return update, atom_grads
```

```python
import jax
import jax.numpy as jnp
from jax import lax
from jax.experimental import pallas as pl
from jax.experimental.pallas import tpu as pltpu
from jax.sharding import PartitionSpec as P

LMAX = 6
COEF = (LMAX + 1) ** 2
LANES = 128
PIECE = 104
VMEM_LIMIT = 56 * 1024 * 1024
F32 = jnp.float32
BF16 = jnp.bfloat16


def frame_layout():
    layout = []
    offset = 0
    for degree in range(LMAX + 1):
        extent = min(degree, 2)
        layout.append((degree, degree * degree, 2 * degree + 1, extent, offset))
        offset = offset + (2 * extent + 1) * (2 * degree + 1)
    return layout


def group_places():
    places = {}
    block = 0
    for order in (0, 1, -1, 2, -2):
        for degree in range(abs(order), LMAX + 1):
            places[(degree, order)] = block
            block += 1
    return places


PLACES = group_places()
ROT = len(PLACES)
N0, N1, N2 = LMAX + 1, LMAX, LMAX - 1


def lanes(block, count=1):
    return slice(block * LANES, (block + count) * LANES)


def column(row):
    n = row.shape[1]
    first = lax.broadcasted_iota(jnp.int32, (n, n), 0)
    second = lax.broadcasted_iota(jnp.int32, (n, n), 1)
    picked = jnp.where(first == second, row, 0).astype(F32)
    return jnp.sum(picked, axis=1, keepdims=True).astype(jnp.int32)


def pick_rows(row, count, start=0):
    n = row.shape[1]
    rows = lax.broadcasted_iota(jnp.int32, (n, count), 1) + start
    return (column(row) == rows).astype(F32).astype(BF16)


def sum_rows(row, count, start=0):
    n = row.shape[1]
    rows = lax.broadcasted_iota(jnp.int32, (count, n), 0) + start
    return (row == rows).astype(F32).astype(BF16)


def dot(left, right):
    return jnp.dot(left, right, preferred_element_type=F32)


def dot_t(left, right):
    return lax.dot_general(left, right, (((1,), (1,)), ((), ())), preferred_element_type=F32)


def both(first, second):
    return jnp.concatenate([first.astype(F32), second.astype(F32)], axis=0).astype(BF16)


def pack_kernel(ghost_ref, atoms_ref, down_ref, up_ref):
    width = down_ref.shape[1]
    onehot = pick_rows(ghost_ref[...], atoms_ref.shape[1])
    for m in range(COEF):
        rows = dot(onehot, atoms_ref[m])
        down_ref[m] = rows[:width].astype(BF16)
        up_ref[m] = rows[width:].astype(BF16)


def send_kernel(send_ref, recv_ref, atoms_ref, prev_ref, next_ref, cot_ref, out_ref, wide):
    own = atoms_ref.shape[1]
    slots = send_ref.shape[1]
    ghosts = 2 * prev_ref.shape[1]
    from_own = pick_rows(send_ref[...], own)
    from_ghost = pick_rows(send_ref[...], ghosts, own)
    from_cot = pick_rows(recv_ref[...], own)
    for m in range(COEF):
        rows = dot(from_own, atoms_ref[m]) + dot(from_ghost, both(prev_ref[m], next_ref[m]))
        wide[pl.ds(m, slots, stride=PIECE), :] = rows
        wide[pl.ds(COEF + m, slots, stride=PIECE), :] = dot(from_cot, cot_ref[m])
    for m in range(2 * COEF, PIECE):
        wide[pl.ds(m, slots, stride=PIECE), :] = jnp.zeros((slots, LANES), F32)
    out_ref[...] = wide[...].astype(BF16)


def edge_kernel(
    src_ref, tgt_ref, frames_ref, atoms_ref, prev_ref, next_ref, cot_ref, recv_ref,
    w_zero_hbm, w_one_hbm, w_two_hbm,
    out_ref, own_sum_ref, own_grad_ref, ghost_grad_ref,
    w_zero, w_one, w_two, sems, wide, table, target, xs, us, spread, fwd0, fwd1, fwd2, ups, pre, msg,
):
    own = atoms_ref.shape[1]
    ghosts = 2 * prev_ref.shape[1]
    edges = src_ref.shape[1]
    ext = own + ghosts
    slots = table.shape[0] - ext
    copies = [
        pltpu.make_async_copy(w_zero_hbm, w_zero, sems.at[0]),
        pltpu.make_async_copy(w_one_hbm, w_one, sems.at[1]),
        pltpu.make_async_copy(w_two_hbm, w_two, sems.at[2]),
    ]
    for copy in copies:
        copy.start()

    wide[...] = recv_ref[...].astype(F32)
    for m in range(COEF):
        table[0:own, lanes(m)] = atoms_ref[m]
        table[own:ext, lanes(m)] = both(prev_ref[m], next_ref[m])
        table[ext:, lanes(m)] = wide[pl.ds(m, slots, stride=PIECE), :].astype(BF16)
        target[0:own, lanes(m)] = cot_ref[m]
        target[own:, lanes(m)] = wide[pl.ds(COEF + m, slots, stride=PIECE), :].astype(BF16)

    pick_src = pick_rows(src_ref[...], ext + slots)
    pick_tgt = pick_rows(tgt_ref[...], own + slots)
    for l in range(LMAX + 1):
        span = lanes(l * l, 2 * l + 1)
        xs[:, span] = dot(pick_src, table[:, span])
        us[:, span] = dot(pick_tgt, target[:, span])

    def rotate(step, carry):
        at = pl.ds(pl.multiple_of(step * 16, 16), 16)
        minus = pl.ds(pl.multiple_of(step * 16 + edges, 16), 16)
        block = frames_ref[at, :].astype(F32)
        for degree, anchor, span, extent, offset in frame_layout():
            orders = range(-extent, extent + 1)
            acc = [None] * len(orders)
            bcc = [None] * len(orders)
            for m in range(span):
                x = xs[at, lanes(anchor + m)]
                u = us[at, lanes(anchor + m)]
                for i in range(len(orders)):
                    k = offset + i * span + m
                    f = jnp.broadcast_to(block[:, k : k + 1], (16, LANES))
                    spread[k, at, :] = f
                    acc[i] = f * x if m == 0 else acc[i] + f * x
                    bcc[i] = f * u if m == 0 else bcc[i] + f * u
            for i, order in enumerate(orders):
                value = acc[i].astype(BF16)
                if order == 0:
                    fwd0[at, lanes(degree)] = value
                elif abs(order) == 1:
                    fwd1[at if order > 0 else minus, lanes(degree - 1)] = value
                else:
                    fwd2[at if order > 0 else minus, lanes(degree - 2)] = value
                ups[at, lanes(PLACES[(degree, order)])] = bcc[i]
        return carry

    lax.fori_loop(0, edges // 16, rotate, 0)

    for copy in copies:
        copy.wait()

    def mixed(product, sign):
        top, low = slice(0, edges), slice(edges, 2 * edges)
        pre[:, lanes(0, N0)] = product(fwd0[...], w_zero[...])
        real = product(fwd1[...], w_one[0])
        imag = product(fwd1[...], w_one[1])
        pre[:, lanes(N0, N1)] = real[top] - sign * imag[low]
        pre[:, lanes(N0 + N1, N1)] = real[low] + sign * imag[top]
        real = product(fwd2[...], w_two[0])
        imag = product(fwd2[...], w_two[1])
        pre[:, lanes(N0 + 2 * N1, N2)] = real[top] - sign * imag[low]
        pre[:, lanes(N0 + 2 * N1 + N2, N2)] = real[low] + sign * imag[top]

    mixed(dot, 1.0)

    def gating(step, carry):
        at = pl.ds(pl.multiple_of(step * 16, 16), 16)
        minus = pl.ds(pl.multiple_of(step * 16 + edges, 16), 16)
        scale = jax.nn.sigmoid(pre[at, lanes(0)])
        total = None
        for block in range(ROT):
            y = pre[at, lanes(block)]
            v = ups[at, lanes(block)]
            total = y * v if total is None else total + y * v
            pre[at, lanes(block)] = y * scale
        slope = scale * (1.0 - scale)
        for (degree, order), block in PLACES.items():
            value = ups[at, lanes(block)] * scale
            if block == 0:
                value = value + total * slope
            value = value.astype(BF16)
            if order == 0:
                fwd0[at, lanes(degree)] = value
            elif abs(order) == 1:
                fwd1[at if order > 0 else minus, lanes(degree - 1)] = value
            else:
                fwd2[at if order > 0 else minus, lanes(degree - 2)] = value
        return carry

    lax.fori_loop(0, edges // 16, gating, 0)

    def turn_out(step, carry):
        at = pl.ds(pl.multiple_of(step * 16, 16), 16)
        for degree, anchor, span, extent, offset in frame_layout():
            orders = range(-extent, extent + 1)
            parts = [pre[at, lanes(PLACES[(degree, order)])] for order in orders]
            for m in range(span):
                value = None
                for i in range(len(orders)):
                    term = spread[offset + i * span + m, at, :] * parts[i]
                    value = term if value is None else value + term
                msg[at, lanes(anchor + m)] = value.astype(BF16)
        return carry

    def summed(row, count, place, own_out, ghost_out):
        onehot = sum_rows(row, count)
        for l in range(LMAX + 1):
            anchor, span = l * l, 2 * l + 1
            sums = dot(onehot, msg[:, lanes(anchor, span)])
            for m in range(span):
                own_out[anchor + m] = sums[0:own, lanes(m)]
                if ghost_out is not None:
                    ghost_out[anchor + m] = sums[own:ext, lanes(m)]
                wide[pl.ds(place + anchor + m, slots, stride=PIECE), :] = sums[count - slots :, lanes(m)]

    lax.fori_loop(0, edges // 16, turn_out, 0)
    summed(tgt_ref[...], own + slots, 0, own_sum_ref, None)
    mixed(dot_t, -1.0)
    lax.fori_loop(0, edges // 16, turn_out, 0)
    summed(src_ref[...], ext + slots, COEF, own_grad_ref, ghost_grad_ref)
    for m in range(2 * COEF, PIECE):
        wide[pl.ds(m, slots, stride=PIECE), :] = jnp.zeros((slots, LANES), F32)
    out_ref[...] = wide[...].astype(BF16)


def ghost_kernel(own, send_ref, back_ref, ghost_grad_ref, prev_ref, next_ref, wide):
    slots = send_ref.shape[1]
    ghosts = ghost_grad_ref.shape[1]
    wide[...] = back_ref[...].astype(F32)
    onehot = sum_rows(send_ref[...], ghosts, own)
    for m in range(COEF):
        back = wide[pl.ds(COEF + m, slots, stride=PIECE), :].astype(BF16)
        rows = ghost_grad_ref[m] + dot(onehot, back)
        prev_ref[m] = rows[: ghosts // 2].astype(BF16)
        next_ref[m] = rows[ghosts // 2 :].astype(BF16)


def own_kernel(send_ref, recv_ref, back_ref, own_sum_ref, own_grad_ref, update_ref, grad_ref, wide):
    slots = send_ref.shape[1]
    own = own_sum_ref.shape[1]
    wide[...] = back_ref[...].astype(F32)
    from_tgt = sum_rows(recv_ref[...], own)
    from_src = sum_rows(send_ref[...], own)
    for m in range(COEF):
        back = wide[pl.ds(m, slots, stride=PIECE), :].astype(BF16)
        update_ref[m] = (own_sum_ref[m] + dot(from_tgt, back)).astype(BF16)
        back = wide[pl.ds(COEF + m, slots, stride=PIECE), :].astype(BF16)
        grad_ref[m] = own_grad_ref[m] + dot(from_src, back)


def last_kernel(ghost_ref, grad_ref, before_ref, after_ref, out_ref):
    onehot = sum_rows(ghost_ref[...], grad_ref.shape[1])
    for m in range(COEF):
        out_ref[m] = (grad_ref[m] + dot(onehot, both(before_ref[m], after_ref[m]))).astype(BF16)


def shape(*dims, dtype=BF16):
    return jax.ShapeDtypeStruct(dims, dtype)


def call(kernel, out_shape, scratch=(), hbm=(), flops=0, moved=0, inputs=()):
    specs = [
        pl.BlockSpec(memory_space=pl.ANY if i in hbm else pltpu.VMEM) for i in range(len(inputs))
    ]
    return pl.pallas_call(
        kernel,
        out_shape=out_shape,
        in_specs=specs,
        out_specs=jax.tree.map(lambda _: pl.BlockSpec(memory_space=pltpu.VMEM), out_shape),
        scratch_shapes=scratch,
        compiler_params=pltpu.CompilerParams(vmem_limit_bytes=VMEM_LIMIT),
        cost_estimate=pl.CostEstimate(flops=flops, bytes_accessed=moved, transcendentals=0),
    )(*inputs)


def local(
    atoms,
    frames,
    w_zero,
    w_one,
    w_two,
    cotangent,
    ghost_rows,
    send_rows,
    recv_rows,
    edge_src,
    edge_tgt,
):
    own = atoms.shape[0]
    half = ghost_rows.shape[0] // 2
    slots = send_rows.shape[0]
    edges = edge_src.shape[0]
    ext = own + 2 * half
    cells = lax.axis_size("cell")
    up = [(i, (i + 1) % cells) for i in range(cells)]
    down = [(j, i) for i, j in up]
    atoms_t = jnp.transpose(atoms, (1, 0, 2))
    cot_t = jnp.transpose(cotangent, (1, 0, 2))
    ghost_l, send_l, recv_l, src_l, tgt_l = (
        row.reshape(1, -1) for row in (ghost_rows, send_rows, recv_rows, edge_src, edge_tgt)
    )
    pack = shape(COEF, half, LANES)
    bundle = shape(slots * PIECE, LANES)
    wide = pltpu.VMEM((slots * PIECE, LANES), F32)
    exchange = lambda x: lax.all_to_all(x, "cell", 0, 0, tiled=True)

    to_down, to_up = call(pack_kernel, (pack, pack), moved=1 << 20, inputs=(ghost_l, atoms_t))
    from_prev = lax.ppermute(to_up, "cell", up)
    from_next = lax.ppermute(to_down, "cell", down)
    outgoing = call(
        send_kernel, bundle, (wide,), moved=1 << 20,
        inputs=(send_l, recv_l, atoms_t, from_prev, from_next, cot_t),
    )
    received = exchange(outgoing)
    weights = [pltpu.VMEM(w.shape, BF16) for w in (w_zero, w_one, w_two)]
    partial, own_sum, own_grad, ghost_grad = call(
        edge_kernel,
        (
            bundle,
            shape(COEF, own, LANES, dtype=F32),
            shape(COEF, own, LANES, dtype=F32),
            shape(COEF, 2 * half, LANES, dtype=F32),
        ),
        weights
        + [
            pltpu.SemaphoreType.DMA((3,)),
            wide,
            pltpu.VMEM((ext + slots, COEF * LANES), BF16),
            pltpu.VMEM((own + slots, COEF * LANES), BF16),
            pltpu.VMEM((edges, COEF * LANES), F32),
            pltpu.VMEM((edges, COEF * LANES), F32),
            pltpu.VMEM((frames.shape[1], edges, LANES), F32),
            pltpu.VMEM((edges, N0 * LANES), BF16),
            pltpu.VMEM((2 * edges, N1 * LANES), BF16),
            pltpu.VMEM((2 * edges, N2 * LANES), BF16),
            pltpu.VMEM((edges, ROT * LANES), F32),
            pltpu.VMEM((edges, ROT * LANES), F32),
            pltpu.VMEM((edges, COEF * LANES), BF16),
        ],
        hbm=(8, 9, 10),
        flops=5 << 30,
        moved=8 << 20,
        inputs=(src_l, tgt_l, frames, atoms_t, from_prev, from_next, cot_t, received, w_zero, w_one, w_two),
    )
    returned = exchange(partial)
    to_prev, to_next = call(
        lambda *refs: ghost_kernel(own, *refs), (pack, pack), (wide,), moved=1 << 20,
        inputs=(send_l, returned, ghost_grad),
    )
    after = lax.ppermute(to_prev, "cell", down)
    before = lax.ppermute(to_next, "cell", up)
    update, grad = call(
        own_kernel,
        (shape(COEF, own, LANES), shape(COEF, own, LANES, dtype=F32)), (wide,), moved=3 << 20,
        inputs=(send_l, recv_l, returned, own_sum, own_grad),
    )
    atom_grads = call(
        last_kernel, shape(COEF, own, LANES), moved=2 << 20,
        inputs=(ghost_l, grad, before, after),
    )
    return jnp.transpose(update, (1, 0, 2)), jnp.transpose(atom_grads, (1, 0, 2))


def solution(mesh):
    whole = P(("groups", "cell"))
    return jax.shard_map(
        local,
        mesh=mesh,
        in_specs=(whole, whole, P(), P(), P()) + (whole,) * 6,
        out_specs=(whole, whole),
        check_vma=False,
    )
```

```python
import jax
import jax.numpy as jnp
from jax import lax
from jax.experimental import pallas as pl
from jax.experimental.pallas import tpu as pltpu
from jax.sharding import PartitionSpec as P

LMAX = 6
COEF = (LMAX + 1) ** 2
LANES = 128
PIECE = 104
NOTE = 2 * COEF
ROWS = 16
MIB = 1024 * 1024
FULL = 56
F32 = jnp.float32
BF16 = jnp.bfloat16


def frame_layout():
    layout = []
    offset = 0
    for degree in range(LMAX + 1):
        extent = min(degree, 2)
        layout.append((degree, degree * degree, 2 * degree + 1, extent, offset))
        offset = offset + (2 * extent + 1) * (2 * degree + 1)
    return layout


def group_places():
    places = {}
    block = 0
    for order in (0, 1, -1, 2, -2):
        for degree in range(abs(order), LMAX + 1):
            places[(degree, order)] = block
            block += 1
    return places


PLACES = group_places()
ROT = len(PLACES)
N0, N1, N2 = LMAX + 1, LMAX, LMAX - 1


def lanes(block, count=1):
    return slice(block * LANES, (block + count) * LANES)


def column(row):
    n = row.shape[1]
    first = lax.broadcasted_iota(jnp.int32, (n, n), 0)
    second = lax.broadcasted_iota(jnp.int32, (n, n), 1)
    picked = jnp.where(first == second, row, 0).astype(F32)
    return jnp.sum(picked, axis=1, keepdims=True).astype(jnp.int32)


def pick_rows(row, count, start=0):
    n = row.shape[1]
    rows = lax.broadcasted_iota(jnp.int32, (n, count), 1) + start
    return (column(row) == rows).astype(F32).astype(BF16)


def sum_rows(row, count, start=0):
    n = row.shape[1]
    rows = lax.broadcasted_iota(jnp.int32, (count, n), 0) + start
    return (row == rows).astype(F32).astype(BF16)


def dot(left, right):
    return jnp.dot(left, right, preferred_element_type=F32)


def dot_t(left, right):
    return lax.dot_general(left, right, (((1,), (1,)), ((), ())), preferred_element_type=F32)


def start(sems, *pairs):
    copies = [pltpu.make_async_copy(*pair, sems.at[i]) for i, pair in enumerate(pairs)]
    for copy in copies:
        copy.start()
    return copies


def load(sems, *pairs):
    for copy in start(sems, *pairs):
        copy.wait()


def both(first, second):
    return jnp.concatenate([first.astype(F32), second.astype(F32)], axis=0).astype(BF16)


def pack_kernel(ghost_hbm, atoms_hbm, down_ref, up_ref, ghost_ref, atoms_ref, sems):
    load(sems, (ghost_hbm, ghost_ref), (atoms_hbm, atoms_ref))
    width = down_ref.shape[1]
    onehot = pick_rows(ghost_ref[...], atoms_ref.shape[1])
    for m in range(COEF):
        rows = dot(onehot, atoms_ref[m])
        down_ref[m] = rows[:width].astype(BF16)
        up_ref[m] = rows[width:].astype(BF16)


def own_send_kernel(
    send_hbm, recv_hbm, atoms_hbm, cot_hbm, out_ref, send_ref, recv_ref, atoms_ref, cot_ref, wide, sems
):
    load(sems, (send_hbm, send_ref), (recv_hbm, recv_ref), (atoms_hbm, atoms_ref), (cot_hbm, cot_ref))
    own = atoms_ref.shape[1]
    slots = send_ref.shape[1]
    from_own = pick_rows(send_ref[...], own)
    from_cot = pick_rows(recv_ref[...], own)
    for m in range(COEF):
        wide[pl.ds(m, slots, stride=PIECE), :] = dot(from_own, atoms_ref[m])
        wide[pl.ds(COEF + m, slots, stride=PIECE), :] = dot(from_cot, cot_ref[m])
    index = jnp.broadcast_to(column(send_ref[...]).astype(F32), (slots, LANES))
    for m in range(2 * COEF, PIECE):
        wide[pl.ds(m, slots, stride=PIECE), :] = index if m == NOTE else jnp.zeros_like(index)
    out_ref[...] = wide[...].astype(BF16)


def send_kernel(own, part_ref, prev_ref, next_ref, out_ref, wide):
    slots = part_ref.shape[0] // PIECE
    ghosts = 2 * prev_ref.shape[1]
    wide[...] = part_ref[...].astype(F32)
    asked = wide[pl.ds(NOTE, slots, stride=PIECE), 0:1].astype(jnp.int32)
    onehot = (asked == lax.broadcasted_iota(jnp.int32, (slots, ghosts), 1) + own).astype(F32).astype(BF16)
    for m in range(COEF):
        at = pl.ds(m, slots, stride=PIECE)
        wide[at, :] = wide[at, :] + dot(onehot, both(prev_ref[m], next_ref[m]))
    out_ref[...] = wide[...].astype(BF16)


def along(block, k):
    return jnp.broadcast_to(block[:, k : k + 1], (block.shape[0], LANES)).astype(F32)


def fill_spread(turned, spread, step):
    block = turned[pl.ds(pl.multiple_of(step * ROWS, ROWS), ROWS), :]
    for k in range(turned.shape[1]):
        spread[step, k] = along(block, k)


def store_rotated(values, order, degree, refs, step, edges):
    at = pl.ds(pl.multiple_of(step * ROWS, ROWS), ROWS)
    if order < 0:
        at = pl.ds(pl.multiple_of(step * ROWS + edges, ROWS), ROWS)
    refs[abs(order)][at, lanes(degree - abs(order))] = values.astype(BF16)


def remote_marks(src, tgt, own, ext, slots):
    return src >= ext, (tgt >= own) & (tgt < own + slots)


def local_kernel(
    src_ref, tgt_ref, frames_ref, atoms_ref, prev_ref, next_ref, cot_ref,
    turned, fwd0, fwd1, fwd2, ups, src_out, tgt_out,
    table, target, xs, us, slots,
):
    own = atoms_ref.shape[1]
    ext = table.shape[0]
    edges = src_ref.shape[1]
    src, tgt = src_ref[...], tgt_ref[...]

    far_src, far_tgt = remote_marks(src, tgt, own, ext, slots)
    kind = jnp.where(far_src, jnp.where(far_tgt, 1, 0), jnp.where(far_tgt, 2, 3))
    key = kind * edges + lax.broadcasted_iota(jnp.int32, (1, edges), 1)
    before = (column(key) < key).astype(F32)
    rank = jnp.sum(before, axis=0, keepdims=True).astype(jnp.int32)
    place = column(rank) == lax.broadcasted_iota(jnp.int32, (edges, edges), 1)

    def reorder(row):
        spots = jnp.where(place, column(row), 0).astype(F32)
        return jnp.sum(spots, axis=0, keepdims=True).astype(jnp.int32)

    src, tgt = reorder(src), reorder(tgt)
    src_out[...] = src
    tgt_out[...] = tgt
    turned[...] = dot(sum_rows(rank, edges), frames_ref[...]).astype(BF16)

    for m in range(COEF):
        table[0:own, lanes(m)] = atoms_ref[m]
        table[own:ext, lanes(m)] = both(prev_ref[m], next_ref[m])
        target[:, lanes(m)] = cot_ref[m]
    pick_src = pick_rows(src, ext)
    pick_tgt = pick_rows(tgt, own)
    for l in range(LMAX + 1):
        span = lanes(l * l, 2 * l + 1)
        xs[:, span] = dot(pick_src, table[:, span])
        us[:, span] = dot(pick_tgt, target[:, span])

    def rotate(step, carry):
        at = pl.ds(pl.multiple_of(step * ROWS, ROWS), ROWS)
        block = turned[at, :]
        for degree, anchor, span, extent, offset in frame_layout():
            orders = range(-extent, extent + 1)
            acc = [None] * len(orders)
            bcc = [None] * len(orders)
            for m in range(span):
                x = xs[at, lanes(anchor + m)]
                u = us[at, lanes(anchor + m)]
                for i in range(len(orders)):
                    k = offset + i * span + m
                    f = along(block, k)
                    acc[i] = f * x if m == 0 else acc[i] + f * x
                    bcc[i] = f * u if m == 0 else bcc[i] + f * u
            for i, order in enumerate(orders):
                store_rotated(acc[i], order, degree, (fwd0, fwd1, fwd2), step, edges)
                ups[at, lanes(PLACES[(degree, order)])] = bcc[i]
        return carry

    lax.fori_loop(0, edges // ROWS, rotate, 0)


def turn_out(spread, parts_of, msg, step):
    at = pl.ds(pl.multiple_of(step * ROWS, ROWS), ROWS)
    for degree, anchor, span, extent, offset in frame_layout():
        orders = range(-extent, extent + 1)
        parts = parts_of(at, degree, orders)
        for m in range(span):
            value = None
            for i in range(len(orders)):
                term = spread[step, offset + i * span + m] * parts[i]
                value = term if value is None else value + term
            msg[at, lanes(anchor + m)] = value.astype(BF16)


def gated_parts(pre):
    def parts(at, degree, orders):
        scale = jax.nn.sigmoid(pre[at, lanes(0)])
        return [pre[at, lanes(PLACES[(degree, order)])] * scale for order in orders]

    return parts


def plain_parts(ref):
    return lambda at, degree, orders: [ref[at, lanes(PLACES[(degree, order)])] for order in orders]


def loop(low, high, body):
    def step(i, carry):
        body(i)
        return carry

    lax.fori_loop(low, high, step, 0)


def edge_kernel(
    own, ext,
    src_hbm, tgt_hbm, recv_hbm, turned_hbm, near0, near1, near2, near_ups, zero_hbm, one_hbm, two_hbm,
    out_ref, pre_hbm, back_hbm,
    src_ref, tgt_ref, recv_ref, turned, fwd0, fwd1, fwd2, ups, w_zero, w_one, w_two,
    wide, table, target, pick_s, pick_t, pre, back, msg, spread, sems, sems_out,
):
    first_in = start(
        sems, (src_hbm, src_ref), (tgt_hbm, tgt_ref), (recv_hbm, recv_ref),
        (turned_hbm, turned), (near0, fwd0), (near1, fwd1), (near2, fwd2),
        (zero_hbm, w_zero), (near_ups, ups), (one_hbm, w_one), (two_hbm, w_two),
    )
    edges = src_ref.shape[1]
    slots = table.shape[0]
    groups = edges // ROWS
    msg[...] = jnp.zeros(msg.shape, BF16)
    for copy in first_in[:2]:
        copy.wait()
    src, tgt = src_ref[...], tgt_ref[...]
    far_src, far_tgt = remote_marks(src, tgt, own, ext, slots)
    count = lambda mask: jnp.sum(mask.astype(F32)).astype(jnp.int32)
    n_src = count(far_src)
    first = count(far_src & jnp.logical_not(far_tgt))
    last = count(far_src | far_tgt)
    src_end = (n_src + ROWS - 1) // ROWS
    tgt_start, tgt_end = first // ROWS, (last + ROWS - 1) // ROWS

    pick_s[...] = pick_rows(src, slots, ext)
    pick_t[...] = pick_rows(tgt, slots, own)
    for copy in first_in[2:4]:
        copy.wait()
    wide[...] = recv_ref[...].astype(F32)
    for m in range(COEF):
        table[:, lanes(m)] = wide[pl.ds(m, slots, stride=PIECE), :].astype(BF16)
        target[:, lanes(m)] = wide[pl.ds(COEF + m, slots, stride=PIECE), :].astype(BF16)

    def rotate(step, pick, far, add):
        at = pl.ds(pl.multiple_of(step * ROWS, ROWS), ROWS)
        onehot = pick[at, :]
        for degree, anchor, span, extent, offset in frame_layout():
            orders = range(-extent, extent + 1)
            acc = [None] * len(orders)
            rows = dot(onehot, far[:, lanes(anchor, span)])
            for m in range(span):
                for i in range(len(orders)):
                    term = spread[step, offset + i * span + m] * rows[:, lanes(m)]
                    acc[i] = term if m == 0 else acc[i] + term
            for i, order in enumerate(orders):
                add(acc[i], order, degree, step)

    def add_ups(value, order, degree, step):
        at = pl.ds(pl.multiple_of(step * ROWS, ROWS), ROWS)
        spot = lanes(PLACES[(degree, order)])
        ups[at, spot] = ups[at, spot] + value

    def add_fwd(value, order, degree, step):
        at = pl.ds(pl.multiple_of(step * ROWS, ROWS), ROWS)
        if order < 0:
            at = pl.ds(pl.multiple_of(step * ROWS + edges, ROWS), ROWS)
        ref, spot = (fwd0, fwd1, fwd2)[abs(order)], lanes(degree - abs(order))
        ref[at, spot] = (ref[at, spot].astype(F32) + value).astype(BF16)

    def store_fwd(value, order, degree, step):
        store_rotated(value, order, degree, (fwd0, fwd1, fwd2), step, edges)

    loop(0, jnp.maximum(src_end, tgt_end), lambda step: fill_spread(turned, spread, step))
    for copy in first_in[4:7]:
        copy.wait()
    loop(0, src_end, lambda step: rotate(step, pick_s, table, add_fwd))
    for copy in first_in[7:9]:
        copy.wait()
    loop(tgt_start, tgt_end, lambda step: rotate(step, pick_t, target, add_ups))
    for copy in first_in[9:]:
        copy.wait()

    def mixed(product, sign, to):
        top, low = slice(0, edges), slice(edges, 2 * edges)
        to[:, lanes(0, N0)] = product(fwd0[...], w_zero[...])
        real = product(fwd1[...], w_one[0])
        imag = product(fwd1[...], w_one[1])
        to[:, lanes(N0, N1)] = real[top] - sign * imag[low]
        to[:, lanes(N0 + N1, N1)] = real[low] + sign * imag[top]
        real = product(fwd2[...], w_two[0])
        imag = product(fwd2[...], w_two[1])
        to[:, lanes(N0 + 2 * N1, N2)] = real[top] - sign * imag[low]
        to[:, lanes(N0 + 2 * N1 + N2, N2)] = real[low] + sign * imag[top]

    mixed(dot, 1.0, pre)
    pre_out, = start(sems_out, (pre, pre_hbm))

    def gating(step):
        at = pl.ds(pl.multiple_of(step * ROWS, ROWS), ROWS)
        scale = jax.nn.sigmoid(pre[at, lanes(0)])
        total = None
        for (degree, order), block in PLACES.items():
            above = ups[at, lanes(block)]
            below = pre[at, lanes(block)] * above
            total = below if total is None else total + below
            if block:
                store_fwd(above * scale, order, degree, step)
        first_row = ups[at, lanes(0)] * scale + total * (scale * (1.0 - scale))
        store_fwd(first_row, 0, 0, step)

    loop(0, groups, gating)

    def far_sums(row, start, place):
        onehot = sum_rows(row, slots, start)
        for l in range(LMAX + 1):
            anchor, span = l * l, 2 * l + 1
            sums = dot(onehot, msg[:, lanes(anchor, span)])
            for m in range(span):
                wide[pl.ds(place + anchor + m, slots, stride=PIECE), :] = sums[:, lanes(m)]

    loop(tgt_start, tgt_end, lambda step: turn_out(spread, gated_parts(pre), msg, step))
    far_sums(tgt, own, 0)
    mixed(dot_t, -1.0, back)
    back_out = pltpu.make_async_copy(back, back_hbm, sems_out.at[1])
    back_out.start()
    loop(0, src_end, lambda step: turn_out(spread, plain_parts(back), msg, step))
    far_sums(src, ext, COEF)
    for m in range(2 * COEF, PIECE):
        wide[pl.ds(m, slots, stride=PIECE), :] = jnp.zeros((slots, LANES), F32)
    out_ref[...] = wide[...].astype(BF16)
    pre_out.wait()
    back_out.wait()


def near_kernel(
    src_ref, tgt_ref, turned, pre, back, own_sum_ref, own_grad_ref, ghost_grad_ref, msg, spread
):
    edges = src_ref.shape[1]
    own = own_sum_ref.shape[1]
    ext = own + ghost_grad_ref.shape[1]

    def sums(onehot, store):
        for l in range(LMAX + 1):
            anchor, span = l * l, 2 * l + 1
            rows = dot(onehot, msg[:, lanes(anchor, span)])
            for m in range(span):
                store(anchor + m, rows[:, lanes(m)])

    def store_sum(m, rows):
        own_sum_ref[m] = rows

    def store_grad(m, rows):
        own_grad_ref[m] = rows[:own]
        ghost_grad_ref[m] = rows[own:]

    loop(0, edges // ROWS, lambda step: fill_spread(turned, spread, step))
    loop(0, edges // ROWS, lambda step: turn_out(spread, gated_parts(pre), msg, step))
    sums(sum_rows(tgt_ref[...], own), store_sum)
    loop(0, edges // ROWS, lambda step: turn_out(spread, plain_parts(back), msg, step))
    sums(sum_rows(src_ref[...], ext), store_grad)


def ghost_kernel(own, send_ref, back_ref, ghost_grad_ref, prev_ref, next_ref, wide):
    slots = send_ref.shape[1]
    ghosts = ghost_grad_ref.shape[1]
    wide[...] = back_ref[...].astype(F32)
    onehot = sum_rows(send_ref[...], ghosts, own)
    for m in range(COEF):
        back = wide[pl.ds(COEF + m, slots, stride=PIECE), :].astype(BF16)
        rows = ghost_grad_ref[m] + dot(onehot, back)
        prev_ref[m] = rows[: ghosts // 2].astype(BF16)
        next_ref[m] = rows[ghosts // 2 :].astype(BF16)


def own_kernel(send_ref, recv_ref, back_ref, own_sum_ref, own_grad_ref, update_ref, grad_ref, wide):
    slots = send_ref.shape[1]
    own = own_sum_ref.shape[1]
    wide[...] = back_ref[...].astype(F32)
    from_tgt = sum_rows(recv_ref[...], own)
    from_src = sum_rows(send_ref[...], own)
    for m in range(COEF):
        back = wide[pl.ds(m, slots, stride=PIECE), :].astype(BF16)
        update_ref[m] = (own_sum_ref[m] + dot(from_tgt, back)).astype(BF16)
        back = wide[pl.ds(COEF + m, slots, stride=PIECE), :].astype(BF16)
        grad_ref[m] = own_grad_ref[m] + dot(from_src, back)


def last_kernel(ghost_ref, grad_ref, before_ref, after_ref, out_ref):
    onehot = sum_rows(ghost_ref[...], grad_ref.shape[1])
    for m in range(COEF):
        out_ref[m] = (grad_ref[m] + dot(onehot, both(before_ref[m], after_ref[m]))).astype(BF16)


def shape(*dims, dtype=BF16):
    return jax.ShapeDtypeStruct(dims, dtype)


def call(kernel, out_shape, scratch=(), limit=12, hbm=(), hbm_out=(), cost=(0, 0), inputs=()):
    specs = [
        pl.BlockSpec(memory_space=pltpu.HBM if i in hbm else pltpu.VMEM) for i in range(len(inputs))
    ]
    return pl.pallas_call(
        kernel,
        out_shape=out_shape,
        in_specs=specs,
        out_specs=jax.tree.map(
            lambda s: pl.BlockSpec(memory_space=pltpu.HBM if s in hbm_out else pltpu.VMEM), out_shape
        ),
        scratch_shapes=scratch,
        compiler_params=pltpu.CompilerParams(vmem_limit_bytes=limit * MIB),
        cost_estimate=pl.CostEstimate(flops=cost[0], bytes_accessed=cost[1], transcendentals=0),
    )(*inputs)


def local(
    atoms,
    frames,
    w_zero,
    w_one,
    w_two,
    cotangent,
    ghost_rows,
    send_rows,
    recv_rows,
    edge_src,
    edge_tgt,
):
    own = atoms.shape[0]
    half = ghost_rows.shape[0] // 2
    slots = send_rows.shape[0]
    edges = edge_src.shape[0]
    ext = own + 2 * half
    cells = lax.axis_size("cell")
    up = [(i, (i + 1) % cells) for i in range(cells)]
    down = [(j, i) for i, j in up]
    atoms_t = jnp.transpose(atoms, (1, 0, 2))
    cot_t = jnp.transpose(cotangent, (1, 0, 2))
    ghost_l, send_l, recv_l, src_l, tgt_l = (
        row.reshape(1, -1) for row in (ghost_rows, send_rows, recv_rows, edge_src, edge_tgt)
    )
    pack = shape(COEF, half, LANES)
    bundle = shape(slots * PIECE, LANES)
    wide = pltpu.VMEM((slots * PIECE, LANES), F32)
    rows = pltpu.VMEM((COEF, own, LANES), BF16)
    index = shape(1, edges, dtype=jnp.int32)
    coefs = lambda n, dtype: shape(edges, n * LANES, dtype=dtype)
    scratch = lambda s: pltpu.VMEM(s.shape, s.dtype)
    short = lambda x: pltpu.VMEM(x.shape, jnp.int32)
    exchange = lambda x: lax.all_to_all(x, "cell", 0, 0, tiled=True)
    mixing = [coefs(N0, BF16), shape(2 * edges, N1 * LANES), shape(2 * edges, N2 * LANES)]
    every = coefs(COEF, F32)
    turned = coefs(ROT, F32)

    to_down, to_up = call(
        pack_kernel, (pack, pack), (short(ghost_l), rows, pltpu.SemaphoreType.DMA((2,))),
        hbm=(0, 1), cost=(0, MIB), inputs=(ghost_l, atoms_t),
    )
    from_prev = lax.ppermute(to_up, "cell", up)
    from_next = lax.ppermute(to_down, "cell", down)
    part = call(
        own_send_kernel, bundle,
        (short(send_l), short(recv_l), rows, rows, wide, pltpu.SemaphoreType.DMA((4,))),
        limit=FULL, hbm=(0, 1, 2, 3), cost=(0, 3 * MIB), inputs=(send_l, recv_l, atoms_t, cot_t),
    )
    outgoing = call(
        lambda *refs: send_kernel(own, *refs), bundle, (wide,), cost=(0, MIB),
        inputs=(part, from_prev, from_next),
    )
    received = exchange(outgoing)
    spread = pltpu.VMEM((edges // ROWS, frames.shape[1], ROWS, LANES), F32)
    near = call(
        lambda *refs: local_kernel(*refs, slots),
        [shape(*frames.shape)] + mixing + [turned, index, index],
        [
            pltpu.VMEM((ext, COEF * LANES), BF16),
            pltpu.VMEM((own, COEF * LANES), BF16),
            scratch(every),
            scratch(every),
        ],
        cost=(1 << 31, 24 * MIB), limit=FULL,
        inputs=(src_l, tgt_l, frames, atoms_t, from_prev, from_next, cot_t),
    )
    frames_p, near0, near1, near2, near_ups, src_p, tgt_p = near
    far_rows = pltpu.VMEM((slots, COEF * LANES), BF16)
    pick = pltpu.VMEM((edges, slots), BF16)
    inputs = (
        src_p, tgt_p, received, frames_p, near0, near1, near2, near_ups, w_zero, w_one, w_two
    )
    partial, pre, back = call(
        lambda *refs: edge_kernel(own, ext, *refs),
        (bundle, turned, turned),
        [scratch(x) for x in inputs]
        + [wide, far_rows, far_rows, pick, pick, scratch(turned), scratch(turned)]
        + [
            scratch(coefs(COEF, BF16)),
            spread,
            pltpu.SemaphoreType.DMA((len(inputs),)),
            pltpu.SemaphoreType.DMA((2,)),
        ],
        cost=(3 << 30, 24 * MIB), limit=FULL, hbm=range(len(inputs)), hbm_out=(turned,),
        inputs=inputs,
    )
    returned = exchange(partial)
    own_sum, own_grad, ghost_grad = call(
        near_kernel,
        (
            shape(COEF, own, LANES, dtype=F32),
            shape(COEF, own, LANES, dtype=F32),
            shape(COEF, 2 * half, LANES, dtype=F32),
        ),
        [scratch(coefs(COEF, BF16)), spread],
        cost=(1 << 30, 20 * MIB), limit=28,
        inputs=(src_p, tgt_p, frames_p, pre, back),
    )
    to_prev, to_next = call(
        lambda *refs: ghost_kernel(own, *refs), (pack, pack), (wide,), cost=(0, MIB),
        inputs=(send_l, returned, ghost_grad),
    )
    after = lax.ppermute(to_prev, "cell", down)
    before = lax.ppermute(to_next, "cell", up)
    update, grad = call(
        own_kernel,
        (shape(COEF, own, LANES), shape(COEF, own, LANES, dtype=F32)), (wide,), cost=(0, 3 * MIB),
        inputs=(send_l, recv_l, returned, own_sum, own_grad),
    )
    atom_grads = call(
        last_kernel, shape(COEF, own, LANES), cost=(0, 2 * MIB),
        inputs=(ghost_l, grad, before, after),
    )
    return jnp.transpose(update, (1, 0, 2)), jnp.transpose(atom_grads, (1, 0, 2))


def solution(mesh):
    whole = P(("groups", "cell"))
    return jax.shard_map(
        local,
        mesh=mesh,
        in_specs=(whole, whole, P(), P(), P()) + (whole,) * 6,
        out_specs=(whole, whole),
        check_vma=False,
    )
```

```python
import jax
import jax.numpy as jnp
from jax import lax
from jax.experimental import pallas as pl
from jax.experimental.pallas import tpu as pltpu
from jax.sharding import PartitionSpec as P

LMAX = 6
COEF = (LMAX + 1) ** 2
LANES = 128
PIECE = 104
NOTE = 2 * COEF
ROWS = 16
MIB = 1024 * 1024
F32 = jnp.float32
BF16 = jnp.bfloat16


def frame_layout():
    layout = []
    offset = 0
    for degree in range(LMAX + 1):
        extent = min(degree, 2)
        layout.append((degree, degree * degree, 2 * degree + 1, extent, offset))
        offset = offset + (2 * extent + 1) * (2 * degree + 1)
    return layout


def group_places():
    places = {}
    block = 0
    for order in (0, 1, -1, 2, -2):
        for degree in range(abs(order), LMAX + 1):
            places[(degree, order)] = block
            block += 1
    return places


PLACES = group_places()
ROT = len(PLACES)
N0, N1, N2 = LMAX + 1, LMAX, LMAX - 1


def lanes(block, count=1):
    return slice(block * LANES, (block + count) * LANES)


def column(row):
    n = row.shape[1]
    first = lax.broadcasted_iota(jnp.int32, (n, n), 0)
    second = lax.broadcasted_iota(jnp.int32, (n, n), 1)
    picked = jnp.where(first == second, row, 0).astype(F32)
    return jnp.sum(picked, axis=1, keepdims=True).astype(jnp.int32)


def pick_rows(row, count, start=0):
    n = row.shape[1]
    rows = lax.broadcasted_iota(jnp.int32, (n, count), 1) + start
    return (column(row) == rows).astype(F32).astype(BF16)


def sum_rows(row, count, start=0):
    n = row.shape[1]
    rows = lax.broadcasted_iota(jnp.int32, (count, n), 0) + start
    return (row == rows).astype(F32).astype(BF16)


def dot(left, right):
    return jnp.dot(left, right, preferred_element_type=F32)


def dot_t(left, right):
    return lax.dot_general(left, right, (((1,), (1,)), ((), ())), preferred_element_type=F32)


def start(sems, *pairs):
    copies = [pltpu.make_async_copy(*pair, sems.at[i]) for i, pair in enumerate(pairs)]
    for copy in copies:
        copy.start()
    return copies


def load(sems, *pairs):
    for copy in start(sems, *pairs):
        copy.wait()


def both(first, second):
    return jnp.concatenate([first.astype(F32), second.astype(F32)], axis=0).astype(BF16)


def pack_kernel(ghost_hbm, atoms_hbm, down_ref, up_ref, ghost_ref, atoms_ref, sems):
    width = down_ref.shape[1]
    steps = sems.shape[0] - 1
    cuts = [COEF * i // steps for i in range(steps + 1)]
    spans = [pl.ds(low, high - low) for low, high in zip(cuts, cuts[1:])]
    copies = start(
        sems, (ghost_hbm, ghost_ref), *((atoms_hbm.at[span], atoms_ref.at[span]) for span in spans)
    )
    copies[0].wait()
    onehot = pick_rows(ghost_ref[...], atoms_ref.shape[1])
    for i in range(steps):
        copies[1 + i].wait()
        for m in range(cuts[i], cuts[i + 1]):
            rows = dot(onehot, atoms_ref[m])
            down_ref[m] = rows[:width].astype(BF16)
            up_ref[m] = rows[width:].astype(BF16)


def own_send_kernel(
    send_hbm, recv_hbm, atoms_hbm, cot_hbm, out_ref, send_ref, recv_ref, atoms_ref, cot_ref, wide, sems
):
    load(sems, (send_hbm, send_ref), (recv_hbm, recv_ref), (atoms_hbm, atoms_ref), (cot_hbm, cot_ref))
    own = atoms_ref.shape[1]
    slots = send_ref.shape[1]
    from_own = pick_rows(send_ref[...], own)
    from_cot = pick_rows(recv_ref[...], own)
    for m in range(COEF):
        wide[pl.ds(m, slots, stride=PIECE), :] = dot(from_own, atoms_ref[m])
        wide[pl.ds(COEF + m, slots, stride=PIECE), :] = dot(from_cot, cot_ref[m])
    index = jnp.broadcast_to(column(send_ref[...]).astype(F32), (slots, LANES))
    for m in range(2 * COEF, PIECE):
        wide[pl.ds(m, slots, stride=PIECE), :] = index if m == NOTE else jnp.zeros_like(index)
    out_ref[...] = wide[...].astype(BF16)


def send_kernel(own, part_ref, prev_ref, next_ref, out_ref, wide, extra):
    slots = part_ref.shape[0] // PIECE
    ghosts = 2 * prev_ref.shape[1]
    wide[...] = part_ref[...].astype(F32)
    extra[...] = jnp.zeros(extra.shape, F32)
    asked = wide[pl.ds(NOTE, slots, stride=PIECE), 0:1].astype(jnp.int32)
    onehot = (asked == lax.broadcasted_iota(jnp.int32, (slots, ghosts), 1) + own).astype(F32).astype(BF16)
    for m in range(COEF):
        extra[pl.ds(m, slots, stride=PIECE), :] = dot(onehot, both(prev_ref[m], next_ref[m]))
    out_ref[...] = (wide[...] + extra[...]).astype(BF16)


def along(block, k):
    return jnp.broadcast_to(block[:, k : k + 1], (block.shape[0], LANES)).astype(F32)


def fill_spread(turned, spread, step):
    block = turned[pl.ds(pl.multiple_of(step * ROWS, ROWS), ROWS), :]
    for k in range(turned.shape[1]):
        spread[step, k] = along(block, k)


def store_rotated(values, order, degree, refs, step, edges):
    at = pl.ds(pl.multiple_of(step * ROWS, ROWS), ROWS)
    if order < 0:
        at = pl.ds(pl.multiple_of(step * ROWS + edges, ROWS), ROWS)
    refs[abs(order)][at, lanes(degree - abs(order))] = values.astype(BF16)


def remote_marks(src, tgt, own, ext, slots):
    return src >= ext, (tgt >= own) & (tgt < own + slots)


def local_kernel(
    src_ref, tgt_ref, frames_ref, atoms_ref, prev_ref, next_ref, cot_ref,
    near0, near1, near2, near_ups, turned, src_out, tgt_out,
    fwd0, fwd1, fwd2, ups, table, target, xs, us, sems, slots,
):
    own = atoms_ref.shape[1]
    ext = table.shape[0]
    edges = src_ref.shape[1]
    src, tgt = src_ref[...], tgt_ref[...]

    far_src, far_tgt = remote_marks(src, tgt, own, ext, slots)
    kind = jnp.where(far_src, jnp.where(far_tgt, 1, 0), jnp.where(far_tgt, 2, 3))
    key = kind * edges + lax.broadcasted_iota(jnp.int32, (1, edges), 1)
    before = (column(key) < key).astype(F32)
    rank = jnp.sum(before, axis=0, keepdims=True).astype(jnp.int32)
    place = column(rank) == lax.broadcasted_iota(jnp.int32, (edges, edges), 1)

    def reorder(row):
        spots = jnp.where(place, column(row), 0).astype(F32)
        return jnp.sum(spots, axis=0, keepdims=True).astype(jnp.int32)

    src, tgt = reorder(src), reorder(tgt)
    src_out[...] = src
    tgt_out[...] = tgt
    turned[...] = dot(sum_rows(rank, edges), frames_ref[...]).astype(BF16)

    for m in range(COEF):
        table[0:own, lanes(m)] = atoms_ref[m]
        table[own:ext, lanes(m)] = both(prev_ref[m], next_ref[m])
        target[:, lanes(m)] = cot_ref[m]
    pick_src = pick_rows(src, ext)
    pick_tgt = pick_rows(tgt, own)
    for l in range(LMAX + 1):
        span = lanes(l * l, 2 * l + 1)
        xs[:, span] = dot(pick_src, table[:, span])
        us[:, span] = dot(pick_tgt, target[:, span])

    def rotate(step, carry):
        at = pl.ds(pl.multiple_of(step * ROWS, ROWS), ROWS)
        block = turned[at, :]
        for degree, anchor, span, extent, offset in frame_layout():
            orders = range(-extent, extent + 1)
            acc = [None] * len(orders)
            bcc = [None] * len(orders)
            for m in range(span):
                x = xs[at, lanes(anchor + m)]
                u = us[at, lanes(anchor + m)]
                for i in range(len(orders)):
                    k = offset + i * span + m
                    f = along(block, k)
                    acc[i] = f * x if m == 0 else acc[i] + f * x
                    bcc[i] = f * u if m == 0 else bcc[i] + f * u
            for i, order in enumerate(orders):
                store_rotated(acc[i], order, degree, (fwd0, fwd1, fwd2), step, edges)
                ups[at, lanes(PLACES[(degree, order)])] = bcc[i]
        return carry

    lax.fori_loop(0, edges // ROWS, rotate, 0)
    load(sems, (fwd0, near0), (fwd1, near1), (fwd2, near2), (ups, near_ups))


def turn_out(spread, rows, msg, step):
    at = pl.ds(pl.multiple_of(step * ROWS, ROWS), ROWS)
    for degree, anchor, span, extent, offset in frame_layout():
        orders = range(-extent, extent + 1)
        parts = [rows[at, lanes(PLACES[(degree, order)])].astype(F32) for order in orders]
        for m in range(span):
            value = None
            for i in range(len(orders)):
                term = spread[step, offset + i * span + m] * parts[i]
                value = term if value is None else value + term
            msg[at, lanes(anchor + m)] = value.astype(BF16)


def loop(low, high, body):
    def step(i, carry):
        body(i)
        return carry

    lax.fori_loop(low, high, step, 0)


def edge_kernel(
    own, ext,
    recv_ref, src_ref, tgt_ref, turned, near0, near1, near2, near_ups, zero_hbm, one_hbm, two_hbm,
    out_ref, gated_hbm, back_hbm,
    fwd0, fwd1, fwd2, ups, w_zero, w_one, w_two,
    wide, table, target, pick_s, pick_t, pre, gated, back, msg, spread, sems, sems_out,
):
    first_in = start(
        sems, (near0, fwd0), (near1, fwd1), (near2, fwd2),
        (zero_hbm, w_zero), (one_hbm, w_one), (two_hbm, w_two), (near_ups, ups),
    )
    edges = src_ref.shape[1]
    slots = table.shape[0]
    groups = edges // ROWS
    msg[...] = jnp.zeros(msg.shape, BF16)
    src, tgt = src_ref[...], tgt_ref[...]
    far_src, far_tgt = remote_marks(src, tgt, own, ext, slots)
    count = lambda mask: jnp.sum(mask.astype(F32)).astype(jnp.int32)
    n_src = count(far_src)
    first = count(far_src & jnp.logical_not(far_tgt))
    last = count(far_src | far_tgt)
    src_end = (n_src + ROWS - 1) // ROWS
    tgt_start, tgt_end = first // ROWS, (last + ROWS - 1) // ROWS

    pick_s[...] = pick_rows(src, slots, ext)
    pick_t[...] = pick_rows(tgt, slots, own)
    wide[...] = recv_ref[...].astype(F32)
    for m in range(COEF):
        table[:, lanes(m)] = wide[pl.ds(m, slots, stride=PIECE), :].astype(BF16)
        target[:, lanes(m)] = wide[pl.ds(COEF + m, slots, stride=PIECE), :].astype(BF16)

    def rotate(step, pick, far, add):
        at = pl.ds(pl.multiple_of(step * ROWS, ROWS), ROWS)
        onehot = pick[at, :]
        for degree, anchor, span, extent, offset in frame_layout():
            orders = range(-extent, extent + 1)
            acc = [None] * len(orders)
            rows = dot(onehot, far[:, lanes(anchor, span)])
            for m in range(span):
                for i in range(len(orders)):
                    term = spread[step, offset + i * span + m] * rows[:, lanes(m)]
                    acc[i] = term if m == 0 else acc[i] + term
            for i, order in enumerate(orders):
                add(acc[i], order, degree, step)

    def add_ups(value, order, degree, step):
        at = pl.ds(pl.multiple_of(step * ROWS, ROWS), ROWS)
        spot = lanes(PLACES[(degree, order)])
        ups[at, spot] = ups[at, spot] + value

    def add_fwd(value, order, degree, step):
        at = pl.ds(pl.multiple_of(step * ROWS, ROWS), ROWS)
        if order < 0:
            at = pl.ds(pl.multiple_of(step * ROWS + edges, ROWS), ROWS)
        ref, spot = (fwd0, fwd1, fwd2)[abs(order)], lanes(degree - abs(order))
        ref[at, spot] = (ref[at, spot].astype(F32) + value).astype(BF16)

    def store_fwd(value, order, degree, step):
        store_rotated(value, order, degree, (fwd0, fwd1, fwd2), step, edges)

    loop(0, jnp.maximum(src_end, tgt_end), lambda step: fill_spread(turned, spread, step))
    for copy in first_in[:3]:
        copy.wait()
    loop(0, src_end, lambda step: rotate(step, pick_s, table, add_fwd))

    def mixed(product, sign, to, ready):
        top, low = slice(0, edges), slice(edges, 2 * edges)
        ready(0)
        to[:, lanes(0, N0)] = product(fwd0[...], w_zero[...]).astype(to.dtype)
        ready(1)
        real = product(fwd1[...], w_one[0])
        imag = product(fwd1[...], w_one[1])
        to[:, lanes(N0, N1)] = (real[top] - sign * imag[low]).astype(to.dtype)
        to[:, lanes(N0 + N1, N1)] = (real[low] + sign * imag[top]).astype(to.dtype)
        ready(2)
        real = product(fwd2[...], w_two[0])
        imag = product(fwd2[...], w_two[1])
        to[:, lanes(N0 + 2 * N1, N2)] = (real[top] - sign * imag[low]).astype(to.dtype)
        to[:, lanes(N0 + 2 * N1 + N2, N2)] = (real[low] + sign * imag[top]).astype(to.dtype)

    mixed(dot, 1.0, pre, lambda i: first_in[3 + i].wait())
    first_in[6].wait()
    loop(tgt_start, tgt_end, lambda step: rotate(step, pick_t, target, add_ups))

    def gating(step):
        at = pl.ds(pl.multiple_of(step * ROWS, ROWS), ROWS)
        scale = jax.nn.sigmoid(pre[at, lanes(0)])
        total = None
        for (degree, order), block in PLACES.items():
            above = ups[at, lanes(block)]
            below = pre[at, lanes(block)] * above
            total = below if total is None else total + below
            gated[at, lanes(block)] = (pre[at, lanes(block)] * scale).astype(BF16)
            if block:
                store_fwd(above * scale, order, degree, step)
        first_row = ups[at, lanes(0)] * scale + total * (scale * (1.0 - scale))
        store_fwd(first_row, 0, 0, step)

    loop(0, groups, gating)
    gated_out, = start(sems_out, (gated, gated_hbm))

    def far_sums(row, start, place):
        onehot = sum_rows(row, slots, start)
        for l in range(LMAX + 1):
            anchor, span = l * l, 2 * l + 1
            sums = dot(onehot, msg[:, lanes(anchor, span)])
            for m in range(span):
                wide[pl.ds(place + anchor + m, slots, stride=PIECE), :] = sums[:, lanes(m)]

    loop(tgt_start, tgt_end, lambda step: turn_out(spread, gated, msg, step))
    far_sums(tgt, own, 0)
    mixed(dot_t, -1.0, back, lambda i: None)
    back_out = pltpu.make_async_copy(back, back_hbm, sems_out.at[1])
    back_out.start()
    loop(0, src_end, lambda step: turn_out(spread, back, msg, step))
    far_sums(src, ext, COEF)
    for m in range(2 * COEF, PIECE):
        wide[pl.ds(m, slots, stride=PIECE), :] = jnp.zeros((slots, LANES), F32)
    out_ref[...] = wide[...].astype(BF16)
    gated_out.wait()
    back_out.wait()


def near_kernel(
    src_ref, tgt_ref, turned, gated, back, own_sum_ref, own_grad_ref, ghost_grad_ref, msg, spread
):
    edges = src_ref.shape[1]
    own = own_sum_ref.shape[1]
    ext = own + ghost_grad_ref.shape[1]

    def sums(onehot, store):
        for l in range(LMAX + 1):
            anchor, span = l * l, 2 * l + 1
            rows = dot(onehot, msg[:, lanes(anchor, span)])
            for m in range(span):
                store(anchor + m, rows[:, lanes(m)])

    def store_sum(m, rows):
        own_sum_ref[m] = rows

    def store_grad(m, rows):
        own_grad_ref[m] = rows[:own]
        ghost_grad_ref[m] = rows[own:]

    loop(0, edges // ROWS, lambda step: fill_spread(turned, spread, step))
    loop(0, edges // ROWS, lambda step: turn_out(spread, gated, msg, step))
    sums(sum_rows(tgt_ref[...], own), store_sum)
    loop(0, edges // ROWS, lambda step: turn_out(spread, back, msg, step))
    sums(sum_rows(src_ref[...], ext), store_grad)


def ghost_kernel(own, send_ref, back_ref, ghost_grad_ref, prev_ref, next_ref, wide):
    slots = send_ref.shape[1]
    ghosts = ghost_grad_ref.shape[1]
    wide[...] = back_ref[...].astype(F32)
    onehot = sum_rows(send_ref[...], ghosts, own)
    for m in range(COEF):
        back = wide[pl.ds(COEF + m, slots, stride=PIECE), :].astype(BF16)
        rows = ghost_grad_ref[m] + dot(onehot, back)
        prev_ref[m] = rows[: ghosts // 2].astype(BF16)
        next_ref[m] = rows[ghosts // 2 :].astype(BF16)


def own_kernel(send_ref, recv_ref, back_ref, own_sum_ref, own_grad_ref, update_ref, grad_ref, wide):
    slots = send_ref.shape[1]
    own = own_sum_ref.shape[1]
    wide[...] = back_ref[...].astype(F32)
    from_tgt = sum_rows(recv_ref[...], own)
    from_src = sum_rows(send_ref[...], own)
    for m in range(COEF):
        back = wide[pl.ds(m, slots, stride=PIECE), :].astype(BF16)
        update_ref[m] = (own_sum_ref[m] + dot(from_tgt, back)).astype(BF16)
        back = wide[pl.ds(COEF + m, slots, stride=PIECE), :].astype(BF16)
        grad_ref[m] = own_grad_ref[m] + dot(from_src, back)


def last_kernel(ghost_ref, grad_ref, before_ref, after_ref, out_ref):
    onehot = sum_rows(ghost_ref[...], grad_ref.shape[1])
    for m in range(COEF):
        out_ref[m] = (grad_ref[m] + dot(onehot, both(before_ref[m], after_ref[m]))).astype(BF16)


def shape(*dims, dtype=BF16):
    return jax.ShapeDtypeStruct(dims, dtype)


def call(kernel, out_shape, scratch=(), limit=12, hbm=(), hbm_out=(), cost=(0, 0), inputs=()):
    specs = [
        pl.BlockSpec(memory_space=pltpu.HBM if i in hbm else pltpu.VMEM) for i in range(len(inputs))
    ]
    inputs = [
        pltpu.with_memory_space_constraint(x, pltpu.HBM) if i in hbm else x
        for i, x in enumerate(inputs)
    ]
    return pl.pallas_call(
        kernel,
        out_shape=jax.tree.map(
            lambda s: pltpu.HBM(s.shape, s.dtype) if s in hbm_out else s, out_shape
        ),
        in_specs=specs,
        out_specs=jax.tree.map(
            lambda s: pl.BlockSpec(memory_space=pltpu.HBM if s in hbm_out else pltpu.VMEM), out_shape
        ),
        scratch_shapes=scratch,
        compiler_params=pltpu.CompilerParams(vmem_limit_bytes=limit * MIB),
        cost_estimate=pl.CostEstimate(flops=cost[0], bytes_accessed=cost[1], transcendentals=0),
    )(*inputs)


def local(
    atoms,
    frames,
    w_zero,
    w_one,
    w_two,
    cotangent,
    ghost_rows,
    send_rows,
    recv_rows,
    edge_src,
    edge_tgt,
):
    own = atoms.shape[0]
    half = ghost_rows.shape[0] // 2
    slots = send_rows.shape[0]
    edges = edge_src.shape[0]
    ext = own + 2 * half
    cells = lax.axis_size("cell")
    up = [(i, (i + 1) % cells) for i in range(cells)]
    down = [(j, i) for i, j in up]
    atoms_t = jnp.transpose(atoms, (1, 0, 2))
    cot_t = jnp.transpose(cotangent, (1, 0, 2))
    ghost_l, send_l, recv_l, src_l, tgt_l = (
        row.reshape(1, -1) for row in (ghost_rows, send_rows, recv_rows, edge_src, edge_tgt)
    )
    pack = shape(COEF, half, LANES)
    bundle = shape(slots * PIECE, LANES)
    wide = pltpu.VMEM((slots * PIECE, LANES), F32)
    rows = pltpu.VMEM((COEF, own, LANES), BF16)
    index = shape(1, edges, dtype=jnp.int32)
    coefs = lambda n, dtype: shape(edges, n * LANES, dtype=dtype)
    scratch = lambda s: pltpu.VMEM(s.shape, s.dtype)
    short = lambda x: pltpu.VMEM(x.shape, jnp.int32)
    exchange = lambda x: lax.all_to_all(x, "cell", 0, 0, tiled=True)
    mixing = [coefs(N0, BF16), shape(2 * edges, N1 * LANES), shape(2 * edges, N2 * LANES)]
    every = coefs(COEF, F32)
    turned = coefs(ROT, F32)
    rounded = coefs(ROT, BF16)

    to_down, to_up = call(
        pack_kernel, (pack, pack), (short(ghost_l), rows, pltpu.SemaphoreType.DMA((5,))),
        hbm=(0, 1), cost=(0, MIB), inputs=(ghost_l, atoms_t),
    )
    from_prev = lax.ppermute(to_up, "cell", up)
    from_next = lax.ppermute(to_down, "cell", down)
    part = call(
        own_send_kernel, bundle,
        (short(send_l), short(recv_l), rows, rows, wide, pltpu.SemaphoreType.DMA((4,))),
        hbm=(0, 1, 2, 3), cost=(0, 3 * MIB), inputs=(send_l, recv_l, atoms_t, cot_t),
    )
    outgoing = call(
        lambda *refs: send_kernel(own, *refs), bundle, (wide, wide), cost=(0, MIB),
        inputs=(part, from_prev, from_next),
    )
    received = exchange(outgoing)
    spread = pltpu.VMEM((edges // ROWS, frames.shape[1], ROWS, LANES), F32)
    results = mixing + [turned]
    near = call(
        lambda *refs: local_kernel(*refs, slots),
        results + [shape(*frames.shape), index, index],
        [scratch(x) for x in results]
        + [
            pltpu.VMEM((ext, COEF * LANES), BF16),
            pltpu.VMEM((own, COEF * LANES), BF16),
            scratch(every),
            scratch(every),
            pltpu.SemaphoreType.DMA((len(results),)),
        ],
        cost=(1 << 31, 24 * MIB), limit=24, hbm_out=results,
        inputs=(src_l, tgt_l, frames, atoms_t, from_prev, from_next, cot_t),
    )
    near0, near1, near2, near_ups, frames_p, src_p, tgt_p = near
    far_rows = pltpu.VMEM((slots, COEF * LANES), BF16)
    pick = pltpu.VMEM((edges, slots), BF16)
    inputs = (
        received, src_p, tgt_p, frames_p, near0, near1, near2, near_ups, w_zero, w_one, w_two
    )
    partial, gated, back = call(
        lambda *refs: edge_kernel(own, ext, *refs),
        (bundle, rounded, rounded),
        [scratch(x) for x in inputs[4:]]
        + [wide, far_rows, far_rows, pick, pick, scratch(turned), scratch(rounded), scratch(rounded)]
        + [
            scratch(coefs(COEF, BF16)),
            spread,
            pltpu.SemaphoreType.DMA((len(inputs),)),
            pltpu.SemaphoreType.DMA((2,)),
        ],
        cost=(3 << 30, 24 * MIB), limit=44, hbm=range(4, len(inputs)), hbm_out=(rounded,),
        inputs=inputs,
    )
    returned = exchange(partial)
    own_sum, own_grad, ghost_grad = call(
        near_kernel,
        (
            shape(COEF, own, LANES, dtype=F32),
            shape(COEF, own, LANES, dtype=F32),
            shape(COEF, 2 * half, LANES, dtype=F32),
        ),
        [scratch(coefs(COEF, BF16)), spread],
        cost=(1 << 30, 20 * MIB), limit=28,
        inputs=(src_p, tgt_p, frames_p, gated, back),
    )
    to_prev, to_next = call(
        lambda *refs: ghost_kernel(own, *refs), (pack, pack), (wide,), cost=(0, MIB),
        inputs=(send_l, returned, ghost_grad),
    )
    after = lax.ppermute(to_prev, "cell", down)
    before = lax.ppermute(to_next, "cell", up)
    update, grad = call(
        own_kernel,
        (shape(COEF, own, LANES), shape(COEF, own, LANES, dtype=F32)), (wide,), cost=(0, 3 * MIB),
        inputs=(send_l, recv_l, returned, own_sum, own_grad),
    )
    atom_grads = call(
        last_kernel, shape(COEF, own, LANES), cost=(0, 2 * MIB),
        inputs=(ghost_l, grad, before, after),
    )
    return jnp.transpose(update, (1, 0, 2)), jnp.transpose(atom_grads, (1, 0, 2))


def solution(mesh):
    whole = P(("groups", "cell"))
    return jax.shard_map(
        local,
        mesh=mesh,
        in_specs=(whole, whole, P(), P(), P()) + (whole,) * 6,
        out_specs=(whole, whole),
        check_vma=False,
    )
```

```python
import jax
import jax.numpy as jnp
from jax import lax
from jax.experimental import pallas as pl
from jax.experimental.pallas import tpu as pltpu
from jax.sharding import PartitionSpec as P

LMAX = 6
COEF = (LMAX + 1) ** 2
LANES = 128
PIECE = 104
NOTE = 2 * COEF
ROWS = 16
MIB = 1024 * 1024
F32 = jnp.float32
BF16 = jnp.bfloat16


def frame_layout():
    layout = []
    offset = 0
    for degree in range(LMAX + 1):
        extent = min(degree, 2)
        layout.append((degree, degree * degree, 2 * degree + 1, extent, offset))
        offset = offset + (2 * extent + 1) * (2 * degree + 1)
    return layout


def group_places():
    places = {}
    block = 0
    for order in (0, 1, -1, 2, -2):
        for degree in range(abs(order), LMAX + 1):
            places[(degree, order)] = block
            block += 1
    return places


PLACES = group_places()
ROT = len(PLACES)
N0, N1, N2 = LMAX + 1, LMAX, LMAX - 1


def lanes(block, count=1):
    return slice(block * LANES, (block + count) * LANES)


def column(row):
    n = row.shape[1]
    first = lax.broadcasted_iota(jnp.int32, (n, n), 0)
    second = lax.broadcasted_iota(jnp.int32, (n, n), 1)
    picked = jnp.where(first == second, row, 0).astype(F32)
    return jnp.sum(picked, axis=1, keepdims=True).astype(jnp.int32)


def pick_rows(row, count, start=0):
    n = row.shape[1]
    rows = lax.broadcasted_iota(jnp.int32, (n, count), 1) + start
    return (column(row) == rows).astype(F32).astype(BF16)


def sum_rows(row, count, start=0):
    n = row.shape[1]
    rows = lax.broadcasted_iota(jnp.int32, (count, n), 0) + start
    return (row == rows).astype(F32).astype(BF16)


def dot(left, right):
    return jnp.dot(left, right, preferred_element_type=F32)


def dot_t(left, right):
    return lax.dot_general(left, right, (((1,), (1,)), ((), ())), preferred_element_type=F32)


def start(sems, *pairs):
    copies = [pltpu.make_async_copy(*pair, sems.at[i]) for i, pair in enumerate(pairs)]
    for copy in copies:
        copy.start()
    return copies


def load(sems, *pairs):
    for copy in start(sems, *pairs):
        copy.wait()


def both(first, second):
    return jnp.concatenate([first.astype(F32), second.astype(F32)], axis=0).astype(BF16)


def pack_kernel(ghost_hbm, atoms_hbm, down_ref, up_ref, ghost_ref, atoms_ref, sems):
    width = down_ref.shape[1]
    steps = sems.shape[0] - 1
    cuts = [COEF * i // steps for i in range(steps + 1)]
    spans = [pl.ds(low, high - low) for low, high in zip(cuts, cuts[1:])]
    copies = start(
        sems, (ghost_hbm, ghost_ref), *((atoms_hbm.at[span], atoms_ref.at[span]) for span in spans)
    )
    copies[0].wait()
    onehot = pick_rows(ghost_ref[...], atoms_ref.shape[1])
    for i in range(steps):
        copies[1 + i].wait()
        for m in range(cuts[i], cuts[i + 1]):
            rows = dot(onehot, atoms_ref[m])
            down_ref[m] = rows[:width].astype(BF16)
            up_ref[m] = rows[width:].astype(BF16)


def own_send_kernel(
    send_hbm, recv_hbm, atoms_hbm, cot_hbm, out_ref, send_ref, recv_ref, atoms_ref, cot_ref, wide, sems
):
    load(sems, (send_hbm, send_ref), (recv_hbm, recv_ref), (atoms_hbm, atoms_ref), (cot_hbm, cot_ref))
    own = atoms_ref.shape[1]
    slots = send_ref.shape[1]
    from_own = pick_rows(send_ref[...], own)
    from_cot = pick_rows(recv_ref[...], own)
    for m in range(COEF):
        wide[pl.ds(m, slots, stride=PIECE), :] = dot(from_own, atoms_ref[m])
        wide[pl.ds(COEF + m, slots, stride=PIECE), :] = dot(from_cot, cot_ref[m])
    index = jnp.broadcast_to(column(send_ref[...]).astype(F32), (slots, LANES))
    for m in range(2 * COEF, PIECE):
        wide[pl.ds(m, slots, stride=PIECE), :] = index if m == NOTE else jnp.zeros_like(index)
    out_ref[...] = wide[...].astype(BF16)


def send_kernel(own, part_ref, prev_ref, next_ref, out_ref, wide, extra):
    slots = part_ref.shape[0] // PIECE
    ghosts = 2 * prev_ref.shape[1]
    wide[...] = part_ref[...].astype(F32)
    extra[...] = jnp.zeros(extra.shape, F32)
    asked = wide[pl.ds(NOTE, slots, stride=PIECE), 0:1].astype(jnp.int32)
    onehot = (asked == lax.broadcasted_iota(jnp.int32, (slots, ghosts), 1) + own).astype(F32).astype(BF16)
    for m in range(COEF):
        extra[pl.ds(m, slots, stride=PIECE), :] = dot(onehot, both(prev_ref[m], next_ref[m]))
    out_ref[...] = (wide[...] + extra[...]).astype(BF16)


def along(block, k):
    return jnp.broadcast_to(block[:, k : k + 1], (block.shape[0], LANES)).astype(F32)


def fill_spread(turned, spread, step):
    block = turned[pl.ds(pl.multiple_of(step * ROWS, ROWS), ROWS), :]
    for k in range(turned.shape[1]):
        spread[step, k] = along(block, k)


def store_rotated(values, order, degree, refs, step, edges):
    at = pl.ds(pl.multiple_of(step * ROWS, ROWS), ROWS)
    if order < 0:
        at = pl.ds(pl.multiple_of(step * ROWS + edges, ROWS), ROWS)
    refs[abs(order)][at, lanes(degree - abs(order))] = values.astype(BF16)


def remote_marks(src, tgt, own, ext, slots):
    return src >= ext, (tgt >= own) & (tgt < own + slots)


def local_kernel(
    src_ref, tgt_ref, frames_ref, atoms_ref, prev_ref, next_ref, cot_ref,
    near0, near1, near2, near_ups, turned, src_out, tgt_out,
    fwd0, fwd1, fwd2, ups, table, target, xs, us, sems, slots,
):
    own = atoms_ref.shape[1]
    ext = table.shape[0]
    edges = src_ref.shape[1]
    src, tgt = src_ref[...], tgt_ref[...]

    far_src, far_tgt = remote_marks(src, tgt, own, ext, slots)
    kind = jnp.where(far_src, jnp.where(far_tgt, 1, 0), jnp.where(far_tgt, 2, 3))
    key = kind * edges + lax.broadcasted_iota(jnp.int32, (1, edges), 1)
    before = (column(key) < key).astype(F32)
    rank = jnp.sum(before, axis=0, keepdims=True).astype(jnp.int32)
    place = column(rank) == lax.broadcasted_iota(jnp.int32, (edges, edges), 1)

    def reorder(row):
        spots = jnp.where(place, column(row), 0).astype(F32)
        return jnp.sum(spots, axis=0, keepdims=True).astype(jnp.int32)

    src, tgt = reorder(src), reorder(tgt)
    src_out[...] = src
    tgt_out[...] = tgt
    turned[...] = dot(sum_rows(rank, edges), frames_ref[...]).astype(BF16)

    for m in range(COEF):
        table[0:own, lanes(m)] = atoms_ref[m]
        table[own:ext, lanes(m)] = both(prev_ref[m], next_ref[m])
        target[:, lanes(m)] = cot_ref[m]
    pick_src = pick_rows(src, ext)
    pick_tgt = pick_rows(tgt, own)
    for l in range(LMAX + 1):
        span = lanes(l * l, 2 * l + 1)
        xs[:, span] = dot(pick_src, table[:, span])
        us[:, span] = dot(pick_tgt, target[:, span])

    def rotate(step, carry):
        at = pl.ds(pl.multiple_of(step * ROWS, ROWS), ROWS)
        block = turned[at, :]
        for degree, anchor, span, extent, offset in frame_layout():
            orders = range(-extent, extent + 1)
            acc = [None] * len(orders)
            bcc = [None] * len(orders)
            for m in range(span):
                x = xs[at, lanes(anchor + m)]
                u = us[at, lanes(anchor + m)]
                for i in range(len(orders)):
                    k = offset + i * span + m
                    f = along(block, k)
                    acc[i] = f * x if m == 0 else acc[i] + f * x
                    bcc[i] = f * u if m == 0 else bcc[i] + f * u
            for i, order in enumerate(orders):
                store_rotated(acc[i], order, degree, (fwd0, fwd1, fwd2), step, edges)
                ups[at, lanes(PLACES[(degree, order)])] = bcc[i]
        return carry

    lax.fori_loop(0, edges // ROWS, rotate, 0)
    load(sems, (fwd0, near0), (fwd1, near1), (fwd2, near2), (ups, near_ups))


def turn_out(spread, rows, msg, step):
    at = pl.ds(pl.multiple_of(step * ROWS, ROWS), ROWS)
    for degree, anchor, span, extent, offset in frame_layout():
        orders = range(-extent, extent + 1)
        parts = [rows[at, lanes(PLACES[(degree, order)])].astype(F32) for order in orders]
        for m in range(span):
            value = None
            for i in range(len(orders)):
                term = spread[step, offset + i * span + m] * parts[i]
                value = term if value is None else value + term
            msg[at, lanes(anchor + m)] = value.astype(BF16)


def loop(low, high, body):
    def step(i, carry):
        body(i)
        return carry

    lax.fori_loop(low, high, step, 0)


def edge_kernel(
    own, ext,
    recv_ref, src_ref, tgt_ref, turned, near0, near1, near2, near_ups, zero_hbm, one_hbm, two_hbm,
    out_ref, gated_hbm, back_hbm,
    fwd0, fwd1, fwd2, ups, w_zero, w_one, w_two,
    wide, table, target, xs, us, pre, gated, back, msg, spread, sems, sems_out,
):
    first_in = start(
        sems, (near0, fwd0), (near1, fwd1), (near2, fwd2),
        (zero_hbm, w_zero), (one_hbm, w_one), (two_hbm, w_two),
    )
    edges = src_ref.shape[1]
    slots = table.shape[0]
    groups = edges // ROWS
    msg[...] = jnp.zeros(msg.shape, BF16)
    src, tgt = src_ref[...], tgt_ref[...]
    far_src, far_tgt = remote_marks(src, tgt, own, ext, slots)
    count = lambda mask: jnp.sum(mask.astype(F32)).astype(jnp.int32)
    n_src = count(far_src)
    first = count(far_src & jnp.logical_not(far_tgt))
    last = count(far_src | far_tgt)
    src_end = (n_src + ROWS - 1) // ROWS
    tgt_start, tgt_end = first // ROWS, (last + ROWS - 1) // ROWS

    pick_src = pick_rows(src, slots, ext)
    pick_tgt = pick_rows(tgt, slots, own)
    wide[...] = recv_ref[...].astype(F32)
    for m in range(COEF):
        table[:, lanes(m)] = wide[pl.ds(m, slots, stride=PIECE), :].astype(BF16)
        target[:, lanes(m)] = wide[pl.ds(COEF + m, slots, stride=PIECE), :].astype(BF16)

    for l in range(LMAX + 1):
        span = lanes(l * l, 2 * l + 1)
        xs[:, span] = dot(pick_src, table[:, span])
        us[:, span] = dot(pick_tgt, target[:, span])

    def rotate(step, far, add):
        at = pl.ds(pl.multiple_of(step * ROWS, ROWS), ROWS)
        for degree, anchor, span, extent, offset in frame_layout():
            orders = range(-extent, extent + 1)
            acc = [None] * len(orders)
            for m in range(span):
                row = far[at, lanes(anchor + m)]
                for i in range(len(orders)):
                    term = spread[step, offset + i * span + m] * row
                    acc[i] = term if m == 0 else acc[i] + term
            for i, order in enumerate(orders):
                add(acc[i], order, degree, step)

    def add_ups(value, order, degree, step):
        at = pl.ds(pl.multiple_of(step * ROWS, ROWS), ROWS)
        spot = lanes(PLACES[(degree, order)])
        ups[at, spot] = ups[at, spot] + value

    def add_fwd(value, order, degree, step):
        at = pl.ds(pl.multiple_of(step * ROWS, ROWS), ROWS)
        if order < 0:
            at = pl.ds(pl.multiple_of(step * ROWS + edges, ROWS), ROWS)
        ref, spot = (fwd0, fwd1, fwd2)[abs(order)], lanes(degree - abs(order))
        ref[at, spot] = (ref[at, spot].astype(F32) + value).astype(BF16)

    def store_fwd(value, order, degree, step):
        store_rotated(value, order, degree, (fwd0, fwd1, fwd2), step, edges)

    loop(0, jnp.maximum(src_end, tgt_end), lambda step: fill_spread(turned, spread, step))
    for copy in first_in[:3]:
        copy.wait()
    ups_in = pltpu.make_async_copy(near_ups, ups, sems.at[6])
    ups_in.start()
    loop(0, src_end, lambda step: rotate(step, xs, add_fwd))

    def mixed(product, sign, to, ready):
        top, low = slice(0, edges), slice(edges, 2 * edges)
        ready(0)
        to[:, lanes(0, N0)] = product(fwd0[...], w_zero[...]).astype(to.dtype)
        ready(1)
        real = product(fwd1[...], w_one[0])
        imag = product(fwd1[...], w_one[1])
        to[:, lanes(N0, N1)] = (real[top] - sign * imag[low]).astype(to.dtype)
        to[:, lanes(N0 + N1, N1)] = (real[low] + sign * imag[top]).astype(to.dtype)
        ready(2)
        real = product(fwd2[...], w_two[0])
        imag = product(fwd2[...], w_two[1])
        to[:, lanes(N0 + 2 * N1, N2)] = (real[top] - sign * imag[low]).astype(to.dtype)
        to[:, lanes(N0 + 2 * N1 + N2, N2)] = (real[low] + sign * imag[top]).astype(to.dtype)

    mixed(dot, 1.0, pre, lambda i: first_in[3 + i].wait())
    ups_in.wait()
    loop(tgt_start, tgt_end, lambda step: rotate(step, us, add_ups))

    def gating(step):
        at = pl.ds(pl.multiple_of(step * ROWS, ROWS), ROWS)
        scale = jax.nn.sigmoid(pre[at, lanes(0)])
        total = None
        for (degree, order), block in PLACES.items():
            above = ups[at, lanes(block)]
            below = pre[at, lanes(block)] * above
            total = below if total is None else total + below
            gated[at, lanes(block)] = (pre[at, lanes(block)] * scale).astype(BF16)
            if block:
                store_fwd(above * scale, order, degree, step)
        first_row = ups[at, lanes(0)] * scale + total * (scale * (1.0 - scale))
        store_fwd(first_row, 0, 0, step)

    loop(0, groups, gating)
    gated_out, = start(sems_out, (gated, gated_hbm))

    def far_sums(row, start, place):
        onehot = sum_rows(row, slots, start)
        for l in range(LMAX + 1):
            anchor, span = l * l, 2 * l + 1
            sums = dot(onehot, msg[:, lanes(anchor, span)])
            for m in range(span):
                wide[pl.ds(place + anchor + m, slots, stride=PIECE), :] = sums[:, lanes(m)]

    loop(tgt_start, tgt_end, lambda step: turn_out(spread, gated, msg, step))
    far_sums(tgt, own, 0)
    mixed(dot_t, -1.0, back, lambda i: None)
    back_out = pltpu.make_async_copy(back, back_hbm, sems_out.at[1])
    back_out.start()
    loop(0, src_end, lambda step: turn_out(spread, back, msg, step))
    far_sums(src, ext, COEF)
    for m in range(2 * COEF, PIECE):
        wide[pl.ds(m, slots, stride=PIECE), :] = jnp.zeros((slots, LANES), F32)
    out_ref[...] = wide[...].astype(BF16)
    gated_out.wait()
    back_out.wait()


def near_kernel(
    src_ref, tgt_ref, turned, gated, back, own_sum_ref, own_grad_ref, ghost_grad_ref, msg, spread
):
    edges = src_ref.shape[1]
    own = own_sum_ref.shape[1]
    ext = own + ghost_grad_ref.shape[1]

    def sums(onehot, store):
        for l in range(LMAX + 1):
            anchor, span = l * l, 2 * l + 1
            rows = dot(onehot, msg[:, lanes(anchor, span)])
            for m in range(span):
                store(anchor + m, rows[:, lanes(m)])

    def store_sum(m, rows):
        own_sum_ref[m] = rows

    def store_grad(m, rows):
        own_grad_ref[m] = rows[:own]
        ghost_grad_ref[m] = rows[own:]

    loop(0, edges // ROWS, lambda step: fill_spread(turned, spread, step))
    loop(0, edges // ROWS, lambda step: turn_out(spread, gated, msg, step))
    sums(sum_rows(tgt_ref[...], own), store_sum)
    loop(0, edges // ROWS, lambda step: turn_out(spread, back, msg, step))
    sums(sum_rows(src_ref[...], ext), store_grad)


def ghost_kernel(own, send_ref, back_ref, ghost_grad_ref, prev_ref, next_ref, wide):
    slots = send_ref.shape[1]
    ghosts = ghost_grad_ref.shape[1]
    wide[...] = back_ref[...].astype(F32)
    onehot = sum_rows(send_ref[...], ghosts, own)
    for m in range(COEF):
        back = wide[pl.ds(COEF + m, slots, stride=PIECE), :].astype(BF16)
        rows = ghost_grad_ref[m] + dot(onehot, back)
        prev_ref[m] = rows[: ghosts // 2].astype(BF16)
        next_ref[m] = rows[ghosts // 2 :].astype(BF16)


def own_kernel(send_ref, recv_ref, back_ref, own_sum_ref, own_grad_ref, update_ref, grad_ref, wide):
    slots = send_ref.shape[1]
    own = own_sum_ref.shape[1]
    wide[...] = back_ref[...].astype(F32)
    from_tgt = sum_rows(recv_ref[...], own)
    from_src = sum_rows(send_ref[...], own)
    for m in range(COEF):
        back = wide[pl.ds(m, slots, stride=PIECE), :].astype(BF16)
        update_ref[m] = (own_sum_ref[m] + dot(from_tgt, back)).astype(BF16)
        back = wide[pl.ds(COEF + m, slots, stride=PIECE), :].astype(BF16)
        grad_ref[m] = own_grad_ref[m] + dot(from_src, back)


def last_kernel(ghost_ref, grad_ref, before_ref, after_ref, out_ref):
    onehot = sum_rows(ghost_ref[...], grad_ref.shape[1])
    for m in range(COEF):
        out_ref[m] = (grad_ref[m] + dot(onehot, both(before_ref[m], after_ref[m]))).astype(BF16)


def shape(*dims, dtype=BF16):
    return jax.ShapeDtypeStruct(dims, dtype)


def call(kernel, out_shape, scratch=(), limit=12, hbm=(), hbm_out=(), cost=(0, 0), inputs=()):
    specs = [
        pl.BlockSpec(memory_space=pltpu.HBM if i in hbm else pltpu.VMEM) for i in range(len(inputs))
    ]
    inputs = [
        pltpu.with_memory_space_constraint(x, pltpu.HBM) if i in hbm else x
        for i, x in enumerate(inputs)
    ]
    return pl.pallas_call(
        kernel,
        out_shape=jax.tree.map(
            lambda s: pltpu.HBM(s.shape, s.dtype) if s in hbm_out else s, out_shape
        ),
        in_specs=specs,
        out_specs=jax.tree.map(
            lambda s: pl.BlockSpec(memory_space=pltpu.HBM if s in hbm_out else pltpu.VMEM), out_shape
        ),
        scratch_shapes=scratch,
        compiler_params=pltpu.CompilerParams(vmem_limit_bytes=limit * MIB),
        cost_estimate=pl.CostEstimate(flops=cost[0], bytes_accessed=cost[1], transcendentals=0),
    )(*inputs)


def local(
    atoms,
    frames,
    w_zero,
    w_one,
    w_two,
    cotangent,
    ghost_rows,
    send_rows,
    recv_rows,
    edge_src,
    edge_tgt,
):
    own = atoms.shape[0]
    half = ghost_rows.shape[0] // 2
    slots = send_rows.shape[0]
    edges = edge_src.shape[0]
    ext = own + 2 * half
    cells = lax.axis_size("cell")
    up = [(i, (i + 1) % cells) for i in range(cells)]
    down = [(j, i) for i, j in up]
    atoms_t = jnp.transpose(atoms, (1, 0, 2))
    cot_t = jnp.transpose(cotangent, (1, 0, 2))
    ghost_l, send_l, recv_l, src_l, tgt_l = (
        row.reshape(1, -1) for row in (ghost_rows, send_rows, recv_rows, edge_src, edge_tgt)
    )
    pack = shape(COEF, half, LANES)
    bundle = shape(slots * PIECE, LANES)
    wide = pltpu.VMEM((slots * PIECE, LANES), F32)
    rows = pltpu.VMEM((COEF, own, LANES), BF16)
    index = shape(1, edges, dtype=jnp.int32)
    coefs = lambda n, dtype: shape(edges, n * LANES, dtype=dtype)
    scratch = lambda s: pltpu.VMEM(s.shape, s.dtype)
    short = lambda x: pltpu.VMEM(x.shape, jnp.int32)
    exchange = lambda x: lax.all_to_all(x, "cell", 0, 0, tiled=True)
    mixing = [coefs(N0, BF16), shape(2 * edges, N1 * LANES), shape(2 * edges, N2 * LANES)]
    every = coefs(COEF, F32)
    turned = coefs(ROT, F32)
    rounded = coefs(ROT, BF16)

    to_down, to_up = call(
        pack_kernel, (pack, pack), (short(ghost_l), rows, pltpu.SemaphoreType.DMA((2,))),
        hbm=(0, 1), cost=(0, MIB), inputs=(ghost_l, atoms_t),
    )
    from_prev = lax.ppermute(to_up, "cell", up)
    from_next = lax.ppermute(to_down, "cell", down)
    part = call(
        own_send_kernel, bundle,
        (short(send_l), short(recv_l), rows, rows, wide, pltpu.SemaphoreType.DMA((4,))),
        hbm=(0, 1, 2, 3), cost=(0, 3 * MIB), inputs=(send_l, recv_l, atoms_t, cot_t),
    )
    outgoing = call(
        lambda *refs: send_kernel(own, *refs), bundle, (wide, wide), cost=(0, MIB),
        inputs=(part, from_prev, from_next),
    )
    received = exchange(outgoing)
    spread = pltpu.VMEM((edges // ROWS, frames.shape[1], ROWS, LANES), F32)
    results = mixing + [turned]
    near = call(
        lambda *refs: local_kernel(*refs, slots),
        results + [shape(*frames.shape), index, index],
        [scratch(x) for x in results]
        + [
            pltpu.VMEM((ext, COEF * LANES), BF16),
            pltpu.VMEM((own, COEF * LANES), BF16),
            scratch(every),
            scratch(every),
            pltpu.SemaphoreType.DMA((len(results),)),
        ],
        cost=(1 << 31, 24 * MIB), limit=24, hbm_out=results,
        inputs=(src_l, tgt_l, frames, atoms_t, from_prev, from_next, cot_t),
    )
    near0, near1, near2, near_ups, frames_p, src_p, tgt_p = near
    far_rows = pltpu.VMEM((slots, COEF * LANES), BF16)
    inputs = (
        received, src_p, tgt_p, frames_p, near0, near1, near2, near_ups, w_zero, w_one, w_two
    )
    partial, gated, back = call(
        lambda *refs: edge_kernel(own, ext, *refs),
        (bundle, rounded, rounded),
        [scratch(x) for x in inputs[4:]]
        + [wide, far_rows, far_rows, scratch(every), scratch(every), scratch(turned), scratch(rounded), scratch(rounded)]
        + [
            scratch(coefs(COEF, BF16)),
            spread,
            pltpu.SemaphoreType.DMA((len(inputs),)),
            pltpu.SemaphoreType.DMA((2,)),
        ],
        cost=(3 << 30, 24 * MIB), limit=44, hbm=range(4, len(inputs)), hbm_out=(rounded,),
        inputs=inputs,
    )
    returned = exchange(partial)
    own_sum, own_grad, ghost_grad = call(
        near_kernel,
        (
            shape(COEF, own, LANES, dtype=F32),
            shape(COEF, own, LANES, dtype=F32),
            shape(COEF, 2 * half, LANES, dtype=F32),
        ),
        [scratch(coefs(COEF, BF16)), spread],
        cost=(1 << 30, 20 * MIB), limit=28,
        inputs=(src_p, tgt_p, frames_p, gated, back),
    )
    to_prev, to_next = call(
        lambda *refs: ghost_kernel(own, *refs), (pack, pack), (wide,), cost=(0, MIB),
        inputs=(send_l, returned, ghost_grad),
    )
    after = lax.ppermute(to_prev, "cell", down)
    before = lax.ppermute(to_next, "cell", up)
    update, grad = call(
        own_kernel,
        (shape(COEF, own, LANES), shape(COEF, own, LANES, dtype=F32)), (wide,), cost=(0, 3 * MIB),
        inputs=(send_l, recv_l, returned, own_sum, own_grad),
    )
    atom_grads = call(
        last_kernel, shape(COEF, own, LANES), cost=(0, 2 * MIB),
        inputs=(ghost_l, grad, before, after),
    )
    return jnp.transpose(update, (1, 0, 2)), jnp.transpose(atom_grads, (1, 0, 2))


def solution(mesh):
    whole = P(("groups", "cell"))
    return jax.shard_map(
        local,
        mesh=mesh,
        in_specs=(whole, whole, P(), P(), P()) + (whole,) * 6,
        out_specs=(whole, whole),
        check_vma=False,
    )
```

```python
import jax
import jax.numpy as jnp
from jax import lax
from jax.experimental import pallas as pl
from jax.experimental.pallas import tpu as pltpu
from jax.sharding import PartitionSpec as P

LMAX = 6
COEF = (LMAX + 1) ** 2
LANES = 128
PIECE = 104
NOTE = 2 * COEF
ROWS = 16
MIB = 1024 * 1024
F32 = jnp.float32
BF16 = jnp.bfloat16


def frame_layout():
    layout = []
    offset = 0
    for degree in range(LMAX + 1):
        extent = min(degree, 2)
        layout.append((degree, degree * degree, 2 * degree + 1, extent, offset))
        offset = offset + (2 * extent + 1) * (2 * degree + 1)
    return layout


def group_places():
    places = {}
    block = 0
    for order in (0, 1, -1, 2, -2):
        for degree in range(abs(order), LMAX + 1):
            places[(degree, order)] = block
            block += 1
    return places


PLACES = group_places()
ROT = len(PLACES)
N0, N1, N2 = LMAX + 1, LMAX, LMAX - 1


def lanes(block, count=1):
    return slice(block * LANES, (block + count) * LANES)


def column(row):
    n = row.shape[1]
    first = lax.broadcasted_iota(jnp.int32, (n, n), 0)
    second = lax.broadcasted_iota(jnp.int32, (n, n), 1)
    picked = jnp.where(first == second, row, 0).astype(F32)
    return jnp.sum(picked, axis=1, keepdims=True).astype(jnp.int32)


def pick_rows(row, count, start=0):
    n = row.shape[1]
    rows = lax.broadcasted_iota(jnp.int32, (n, count), 1) + start
    return (column(row) == rows).astype(F32).astype(BF16)


def sum_rows(row, count, start=0):
    n = row.shape[1]
    rows = lax.broadcasted_iota(jnp.int32, (count, n), 0) + start
    return (row == rows).astype(F32).astype(BF16)


def dot(left, right):
    return jnp.dot(left, right, preferred_element_type=F32)


def dot_t(left, right):
    return lax.dot_general(left, right, (((1,), (1,)), ((), ())), preferred_element_type=F32)


def start(sems, *pairs):
    copies = [pltpu.make_async_copy(*pair, sems.at[i]) for i, pair in enumerate(pairs)]
    for copy in copies:
        copy.start()
    return copies


def load(sems, *pairs):
    for copy in start(sems, *pairs):
        copy.wait()


def both(first, second):
    return jnp.concatenate([first.astype(F32), second.astype(F32)], axis=0).astype(BF16)


def pack_kernel(ghost_hbm, atoms_hbm, down_ref, up_ref, ghost_ref, atoms_ref, sems):
    width = down_ref.shape[1]
    steps = sems.shape[0] - 1
    cuts = [COEF * i // steps for i in range(steps + 1)]
    spans = [pl.ds(low, high - low) for low, high in zip(cuts, cuts[1:])]
    copies = start(
        sems, (ghost_hbm, ghost_ref), *((atoms_hbm.at[span], atoms_ref.at[span]) for span in spans)
    )
    copies[0].wait()
    onehot = pick_rows(ghost_ref[...], atoms_ref.shape[1])
    for i in range(steps):
        copies[1 + i].wait()
        for m in range(cuts[i], cuts[i + 1]):
            rows = dot(onehot, atoms_ref[m])
            down_ref[m] = rows[:width].astype(BF16)
            up_ref[m] = rows[width:].astype(BF16)


def own_send_kernel(
    send_hbm, recv_hbm, atoms_hbm, cot_hbm, out_ref, send_ref, recv_ref, atoms_ref, cot_ref, wide, sems
):
    load(sems, (send_hbm, send_ref), (recv_hbm, recv_ref), (atoms_hbm, atoms_ref), (cot_hbm, cot_ref))
    own = atoms_ref.shape[1]
    slots = send_ref.shape[1]
    from_own = pick_rows(send_ref[...], own)
    from_cot = pick_rows(recv_ref[...], own)
    for m in range(COEF):
        wide[pl.ds(m, slots, stride=PIECE), :] = dot(from_own, atoms_ref[m])
        wide[pl.ds(COEF + m, slots, stride=PIECE), :] = dot(from_cot, cot_ref[m])
    index = jnp.broadcast_to(column(send_ref[...]).astype(F32), (slots, LANES))
    for m in range(2 * COEF, PIECE):
        wide[pl.ds(m, slots, stride=PIECE), :] = index if m == NOTE else jnp.zeros_like(index)
    out_ref[...] = wide[...].astype(BF16)


def send_kernel(own, part_ref, prev_ref, next_ref, out_ref, wide, extra):
    slots = part_ref.shape[0] // PIECE
    ghosts = 2 * prev_ref.shape[1]
    wide[...] = part_ref[...].astype(F32)
    extra[...] = jnp.zeros(extra.shape, F32)
    asked = wide[pl.ds(NOTE, slots, stride=PIECE), 0:1].astype(jnp.int32)
    onehot = (asked == lax.broadcasted_iota(jnp.int32, (slots, ghosts), 1) + own).astype(F32).astype(BF16)
    for m in range(COEF):
        extra[pl.ds(m, slots, stride=PIECE), :] = dot(onehot, both(prev_ref[m], next_ref[m]))
    out_ref[...] = (wide[...] + extra[...]).astype(BF16)


def along(block, k):
    return jnp.broadcast_to(block[:, k : k + 1], (block.shape[0], LANES)).astype(F32)


def fill_spread(turned, spread, step):
    block = turned[pl.ds(pl.multiple_of(step * ROWS, ROWS), ROWS), :]
    for k in range(turned.shape[1]):
        spread[step, k] = along(block, k)


def store_rotated(values, order, degree, refs, step, edges):
    at = pl.ds(pl.multiple_of(step * ROWS, ROWS), ROWS)
    if order < 0:
        at = pl.ds(pl.multiple_of(step * ROWS + edges, ROWS), ROWS)
    refs[abs(order)][at, lanes(degree - abs(order))] = values.astype(BF16)


def remote_marks(src, tgt, own, ext, slots):
    return src >= ext, (tgt >= own) & (tgt < own + slots)


def local_kernel(
    src_ref, tgt_ref, frames_ref, atoms_ref, prev_ref, next_ref, cot_ref,
    near_ups, fwd0, fwd1, fwd2, turned, src_out, tgt_out,
    ups, table, target, xs, us, sems, slots,
):
    own = atoms_ref.shape[1]
    ext = table.shape[0]
    edges = src_ref.shape[1]
    src, tgt = src_ref[...], tgt_ref[...]

    far_src, far_tgt = remote_marks(src, tgt, own, ext, slots)
    kind = jnp.where(far_src, jnp.where(far_tgt, 1, 0), jnp.where(far_tgt, 2, 3))
    key = kind * edges + lax.broadcasted_iota(jnp.int32, (1, edges), 1)
    before = (column(key) < key).astype(F32)
    rank = jnp.sum(before, axis=0, keepdims=True).astype(jnp.int32)
    place = column(rank) == lax.broadcasted_iota(jnp.int32, (edges, edges), 1)

    def reorder(row):
        spots = jnp.where(place, column(row), 0).astype(F32)
        return jnp.sum(spots, axis=0, keepdims=True).astype(jnp.int32)

    src, tgt = reorder(src), reorder(tgt)
    src_out[...] = src
    tgt_out[...] = tgt
    turned[...] = dot(sum_rows(rank, edges), frames_ref[...]).astype(BF16)

    for m in range(COEF):
        table[0:own, lanes(m)] = atoms_ref[m]
        table[own:ext, lanes(m)] = both(prev_ref[m], next_ref[m])
        target[:, lanes(m)] = cot_ref[m]
    pick_src = pick_rows(src, ext)
    pick_tgt = pick_rows(tgt, own)
    for l in range(LMAX + 1):
        span = lanes(l * l, 2 * l + 1)
        xs[:, span] = dot(pick_src, table[:, span])
        us[:, span] = dot(pick_tgt, target[:, span])

    def rotate(step, carry):
        at = pl.ds(pl.multiple_of(step * ROWS, ROWS), ROWS)
        block = turned[at, :]
        for degree, anchor, span, extent, offset in frame_layout():
            orders = range(-extent, extent + 1)
            acc = [None] * len(orders)
            bcc = [None] * len(orders)
            for m in range(span):
                x = xs[at, lanes(anchor + m)]
                u = us[at, lanes(anchor + m)]
                for i in range(len(orders)):
                    k = offset + i * span + m
                    f = along(block, k)
                    acc[i] = f * x if m == 0 else acc[i] + f * x
                    bcc[i] = f * u if m == 0 else bcc[i] + f * u
            for i, order in enumerate(orders):
                store_rotated(acc[i], order, degree, (fwd0, fwd1, fwd2), step, edges)
                ups[at, lanes(PLACES[(degree, order)])] = bcc[i]
        return carry

    lax.fori_loop(0, edges // ROWS, rotate, 0)
    load(sems, (ups, near_ups))


def turn_out(spread, rows, msg, step):
    at = pl.ds(pl.multiple_of(step * ROWS, ROWS), ROWS)
    for degree, anchor, span, extent, offset in frame_layout():
        orders = range(-extent, extent + 1)
        parts = [rows[at, lanes(PLACES[(degree, order)])].astype(F32) for order in orders]
        for m in range(span):
            value = None
            for i in range(len(orders)):
                term = spread[step, offset + i * span + m] * parts[i]
                value = term if value is None else value + term
            msg[at, lanes(anchor + m)] = value.astype(BF16)


def loop(low, high, body):
    def step(i, carry):
        body(i)
        return carry

    lax.fori_loop(low, high, step, 0)


def edge_kernel(
    own, ext,
    recv_ref, src_ref, tgt_ref, turned, near0, near1, near2, near_ups, zero_hbm, one_hbm, two_hbm,
    out_ref, gated_hbm, back_hbm,
    ups, w_zero, w_one, w_two, fwd0, fwd1, fwd2,
    wide, table, target, xs, us, pre, gated, back, msg, spread, sems, sems_out,
):
    first_in = start(
        sems, (zero_hbm, w_zero), (one_hbm, w_one), (two_hbm, w_two),
    )
    edges = src_ref.shape[1]
    slots = table.shape[0]
    groups = edges // ROWS
    msg[...] = jnp.zeros(msg.shape, BF16)
    src, tgt = src_ref[...], tgt_ref[...]
    far_src, far_tgt = remote_marks(src, tgt, own, ext, slots)
    count = lambda mask: jnp.sum(mask.astype(F32)).astype(jnp.int32)
    n_src = count(far_src)
    first = count(far_src & jnp.logical_not(far_tgt))
    last = count(far_src | far_tgt)
    src_end = (n_src + ROWS - 1) // ROWS
    tgt_start, tgt_end = first // ROWS, (last + ROWS - 1) // ROWS

    pick_src = pick_rows(src, slots, ext)
    pick_tgt = pick_rows(tgt, slots, own)
    wide[...] = recv_ref[...].astype(F32)
    for m in range(COEF):
        table[:, lanes(m)] = wide[pl.ds(m, slots, stride=PIECE), :].astype(BF16)
        target[:, lanes(m)] = wide[pl.ds(COEF + m, slots, stride=PIECE), :].astype(BF16)

    for l in range(LMAX + 1):
        span = lanes(l * l, 2 * l + 1)
        xs[:, span] = dot(pick_src, table[:, span])
        us[:, span] = dot(pick_tgt, target[:, span])

    def rotate(step, far, add):
        at = pl.ds(pl.multiple_of(step * ROWS, ROWS), ROWS)
        for degree, anchor, span, extent, offset in frame_layout():
            orders = range(-extent, extent + 1)
            acc = [None] * len(orders)
            for m in range(span):
                row = far[at, lanes(anchor + m)]
                for i in range(len(orders)):
                    term = spread[step, offset + i * span + m] * row
                    acc[i] = term if m == 0 else acc[i] + term
            for i, order in enumerate(orders):
                add(acc[i], order, degree, step)

    def add_ups(value, order, degree, step):
        at = pl.ds(pl.multiple_of(step * ROWS, ROWS), ROWS)
        spot = lanes(PLACES[(degree, order)])
        ups[at, spot] = ups[at, spot] + value

    def add_fwd(value, order, degree, step):
        at = pl.ds(pl.multiple_of(step * ROWS, ROWS), ROWS)
        if order < 0:
            at = pl.ds(pl.multiple_of(step * ROWS + edges, ROWS), ROWS)
        spot = lanes(degree - abs(order))
        near = (near0, near1, near2)[abs(order)][at, spot].astype(F32)
        (fwd0, fwd1, fwd2)[abs(order)][at, spot] = (near + value).astype(BF16)

    def keep_fwd(step):
        at = pl.ds(pl.multiple_of(step * ROWS, ROWS), ROWS)
        low = pl.ds(pl.multiple_of(step * ROWS + edges, ROWS), ROWS)
        fwd0[at, :] = near0[at, :]
        for rows in (at, low):
            fwd1[rows, :] = near1[rows, :]
            fwd2[rows, :] = near2[rows, :]

    def store_fwd(value, order, degree, step):
        store_rotated(value, order, degree, (fwd0, fwd1, fwd2), step, edges)

    loop(0, jnp.maximum(src_end, tgt_end), lambda step: fill_spread(turned, spread, step))
    loop(src_end, groups, keep_fwd)
    ups_in = pltpu.make_async_copy(near_ups, ups, sems.at[3])
    ups_in.start()
    loop(0, src_end, lambda step: rotate(step, xs, add_fwd))

    def mixed(product, sign, to):
        top, low = slice(0, edges), slice(edges, 2 * edges)
        to[:, lanes(0, N0)] = product(fwd0[...], w_zero[...]).astype(to.dtype)
        real = product(fwd1[...], w_one[0])
        imag = product(fwd1[...], w_one[1])
        to[:, lanes(N0, N1)] = (real[top] - sign * imag[low]).astype(to.dtype)
        to[:, lanes(N0 + N1, N1)] = (real[low] + sign * imag[top]).astype(to.dtype)
        real = product(fwd2[...], w_two[0])
        imag = product(fwd2[...], w_two[1])
        to[:, lanes(N0 + 2 * N1, N2)] = (real[top] - sign * imag[low]).astype(to.dtype)
        to[:, lanes(N0 + 2 * N1 + N2, N2)] = (real[low] + sign * imag[top]).astype(to.dtype)

    for copy in first_in:
        copy.wait()
    mixed(dot, 1.0, pre)
    ups_in.wait()
    loop(tgt_start, tgt_end, lambda step: rotate(step, us, add_ups))

    def gating(step):
        at = pl.ds(pl.multiple_of(step * ROWS, ROWS), ROWS)
        scale = jax.nn.sigmoid(pre[at, lanes(0)])
        total = None
        for (degree, order), block in PLACES.items():
            above = ups[at, lanes(block)]
            below = pre[at, lanes(block)] * above
            total = below if total is None else total + below
            gated[at, lanes(block)] = (pre[at, lanes(block)] * scale).astype(BF16)
            if block:
                store_fwd(above * scale, order, degree, step)
        first_row = ups[at, lanes(0)] * scale + total * (scale * (1.0 - scale))
        store_fwd(first_row, 0, 0, step)

    loop(0, groups, gating)
    gated_out, = start(sems_out, (gated, gated_hbm))

    def far_sums(row, start, place):
        onehot = sum_rows(row, slots, start)
        for l in range(LMAX + 1):
            anchor, span = l * l, 2 * l + 1
            sums = dot(onehot, msg[:, lanes(anchor, span)])
            for m in range(span):
                wide[pl.ds(place + anchor + m, slots, stride=PIECE), :] = sums[:, lanes(m)]

    loop(tgt_start, tgt_end, lambda step: turn_out(spread, gated, msg, step))
    far_sums(tgt, own, 0)
    mixed(dot_t, -1.0, back)
    back_out = pltpu.make_async_copy(back, back_hbm, sems_out.at[1])
    back_out.start()
    loop(0, src_end, lambda step: turn_out(spread, back, msg, step))
    far_sums(src, ext, COEF)
    for m in range(2 * COEF, PIECE):
        wide[pl.ds(m, slots, stride=PIECE), :] = jnp.zeros((slots, LANES), F32)
    out_ref[...] = wide[...].astype(BF16)
    gated_out.wait()
    back_out.wait()


def near_kernel(
    src_ref, tgt_ref, turned, gated, back, own_sum_ref, own_grad_ref, ghost_grad_ref, msg, spread
):
    edges = src_ref.shape[1]
    own = own_sum_ref.shape[1]
    ext = own + ghost_grad_ref.shape[1]

    def sums(onehot, store):
        for l in range(LMAX + 1):
            anchor, span = l * l, 2 * l + 1
            rows = dot(onehot, msg[:, lanes(anchor, span)])
            for m in range(span):
                store(anchor + m, rows[:, lanes(m)])

    def store_sum(m, rows):
        own_sum_ref[m] = rows

    def store_grad(m, rows):
        own_grad_ref[m] = rows[:own]
        ghost_grad_ref[m] = rows[own:]

    loop(0, edges // ROWS, lambda step: fill_spread(turned, spread, step))
    loop(0, edges // ROWS, lambda step: turn_out(spread, gated, msg, step))
    sums(sum_rows(tgt_ref[...], own), store_sum)
    loop(0, edges // ROWS, lambda step: turn_out(spread, back, msg, step))
    sums(sum_rows(src_ref[...], ext), store_grad)


def ghost_kernel(own, send_ref, back_ref, ghost_grad_ref, prev_ref, next_ref, wide):
    slots = send_ref.shape[1]
    ghosts = ghost_grad_ref.shape[1]
    wide[...] = back_ref[...].astype(F32)
    onehot = sum_rows(send_ref[...], ghosts, own)
    for m in range(COEF):
        back = wide[pl.ds(COEF + m, slots, stride=PIECE), :].astype(BF16)
        rows = ghost_grad_ref[m] + dot(onehot, back)
        prev_ref[m] = rows[: ghosts // 2].astype(BF16)
        next_ref[m] = rows[ghosts // 2 :].astype(BF16)


def own_kernel(send_ref, recv_ref, back_ref, own_sum_ref, own_grad_ref, update_ref, grad_ref, wide):
    slots = send_ref.shape[1]
    own = own_sum_ref.shape[1]
    wide[...] = back_ref[...].astype(F32)
    from_tgt = sum_rows(recv_ref[...], own)
    from_src = sum_rows(send_ref[...], own)
    for m in range(COEF):
        back = wide[pl.ds(m, slots, stride=PIECE), :].astype(BF16)
        update_ref[m] = (own_sum_ref[m] + dot(from_tgt, back)).astype(BF16)
        back = wide[pl.ds(COEF + m, slots, stride=PIECE), :].astype(BF16)
        grad_ref[m] = own_grad_ref[m] + dot(from_src, back)


def last_kernel(ghost_ref, grad_ref, before_ref, after_ref, out_ref):
    onehot = sum_rows(ghost_ref[...], grad_ref.shape[1])
    for m in range(COEF):
        out_ref[m] = (grad_ref[m] + dot(onehot, both(before_ref[m], after_ref[m]))).astype(BF16)


def shape(*dims, dtype=BF16):
    return jax.ShapeDtypeStruct(dims, dtype)


def call(kernel, out_shape, scratch=(), limit=12, hbm=(), hbm_out=(), cost=(0, 0), inputs=()):
    specs = [
        pl.BlockSpec(memory_space=pltpu.HBM if i in hbm else pltpu.VMEM) for i in range(len(inputs))
    ]
    inputs = [
        pltpu.with_memory_space_constraint(x, pltpu.HBM) if i in hbm else x
        for i, x in enumerate(inputs)
    ]
    return pl.pallas_call(
        kernel,
        out_shape=jax.tree.map(
            lambda s: pltpu.HBM(s.shape, s.dtype) if s in hbm_out else s, out_shape
        ),
        in_specs=specs,
        out_specs=jax.tree.map(
            lambda s: pl.BlockSpec(memory_space=pltpu.HBM if s in hbm_out else pltpu.VMEM), out_shape
        ),
        scratch_shapes=scratch,
        compiler_params=pltpu.CompilerParams(vmem_limit_bytes=limit * MIB),
        cost_estimate=pl.CostEstimate(flops=cost[0], bytes_accessed=cost[1], transcendentals=0),
    )(*inputs)


def local(
    atoms,
    frames,
    w_zero,
    w_one,
    w_two,
    cotangent,
    ghost_rows,
    send_rows,
    recv_rows,
    edge_src,
    edge_tgt,
):
    own = atoms.shape[0]
    half = ghost_rows.shape[0] // 2
    slots = send_rows.shape[0]
    edges = edge_src.shape[0]
    ext = own + 2 * half
    cells = lax.axis_size("cell")
    up = [(i, (i + 1) % cells) for i in range(cells)]
    down = [(j, i) for i, j in up]
    atoms_t = jnp.transpose(atoms, (1, 0, 2))
    cot_t = jnp.transpose(cotangent, (1, 0, 2))
    ghost_l, send_l, recv_l, src_l, tgt_l = (
        row.reshape(1, -1) for row in (ghost_rows, send_rows, recv_rows, edge_src, edge_tgt)
    )
    pack = shape(COEF, half, LANES)
    bundle = shape(slots * PIECE, LANES)
    wide = pltpu.VMEM((slots * PIECE, LANES), F32)
    rows = pltpu.VMEM((COEF, own, LANES), BF16)
    index = shape(1, edges, dtype=jnp.int32)
    coefs = lambda n, dtype: shape(edges, n * LANES, dtype=dtype)
    scratch = lambda s: pltpu.VMEM(s.shape, s.dtype)
    short = lambda x: pltpu.VMEM(x.shape, jnp.int32)
    exchange = lambda x: lax.all_to_all(x, "cell", 0, 0, tiled=True)
    mixing = [coefs(N0, BF16), shape(2 * edges, N1 * LANES), shape(2 * edges, N2 * LANES)]
    every = coefs(COEF, F32)
    turned = coefs(ROT, F32)
    rounded = coefs(ROT, BF16)

    to_down, to_up = call(
        pack_kernel, (pack, pack), (short(ghost_l), rows, pltpu.SemaphoreType.DMA((2,))),
        hbm=(0, 1), cost=(0, MIB), inputs=(ghost_l, atoms_t),
    )
    from_prev = lax.ppermute(to_up, "cell", up)
    from_next = lax.ppermute(to_down, "cell", down)
    part = call(
        own_send_kernel, bundle,
        (short(send_l), short(recv_l), rows, rows, wide, pltpu.SemaphoreType.DMA((4,))),
        hbm=(0, 1, 2, 3), cost=(0, 3 * MIB), inputs=(send_l, recv_l, atoms_t, cot_t),
    )
    outgoing = call(
        lambda *refs: send_kernel(own, *refs), bundle, (wide, wide), cost=(0, MIB),
        inputs=(part, from_prev, from_next),
    )
    received = exchange(outgoing)
    spread = pltpu.VMEM((edges // ROWS, frames.shape[1], ROWS, LANES), F32)
    near = call(
        lambda *refs: local_kernel(*refs, slots),
        [turned] + mixing + [shape(*frames.shape), index, index],
        [
            scratch(turned),
            pltpu.VMEM((ext, COEF * LANES), BF16),
            pltpu.VMEM((own, COEF * LANES), BF16),
            scratch(every),
            scratch(every),
            pltpu.SemaphoreType.DMA((1,)),
        ],
        cost=(1 << 31, 24 * MIB), limit=24, hbm_out=(turned,),
        inputs=(src_l, tgt_l, frames, atoms_t, from_prev, from_next, cot_t),
    )
    near_ups, near0, near1, near2, frames_p, src_p, tgt_p = near
    far_rows = pltpu.VMEM((slots, COEF * LANES), BF16)
    inputs = (
        received, src_p, tgt_p, frames_p, near0, near1, near2, near_ups, w_zero, w_one, w_two
    )
    partial, gated, back = call(
        lambda *refs: edge_kernel(own, ext, *refs),
        (bundle, rounded, rounded),
        [scratch(x) for x in inputs[7:]]
        + [scratch(x) for x in mixing]
        + [wide, far_rows, far_rows, scratch(every), scratch(every), scratch(turned), scratch(rounded), scratch(rounded)]
        + [
            scratch(coefs(COEF, BF16)),
            spread,
            pltpu.SemaphoreType.DMA((4,)),
            pltpu.SemaphoreType.DMA((2,)),
        ],
        cost=(3 << 30, 24 * MIB), limit=44, hbm=range(7, len(inputs)), hbm_out=(rounded,),
        inputs=inputs,
    )
    returned = exchange(partial)
    own_sum, own_grad, ghost_grad = call(
        near_kernel,
        (
            shape(COEF, own, LANES, dtype=F32),
            shape(COEF, own, LANES, dtype=F32),
            shape(COEF, 2 * half, LANES, dtype=F32),
        ),
        [scratch(coefs(COEF, BF16)), spread],
        cost=(1 << 30, 20 * MIB), limit=28,
        inputs=(src_p, tgt_p, frames_p, gated, back),
    )
    to_prev, to_next = call(
        lambda *refs: ghost_kernel(own, *refs), (pack, pack), (wide,), cost=(0, MIB),
        inputs=(send_l, returned, ghost_grad),
    )
    after = lax.ppermute(to_prev, "cell", down)
    before = lax.ppermute(to_next, "cell", up)
    update, grad = call(
        own_kernel,
        (shape(COEF, own, LANES), shape(COEF, own, LANES, dtype=F32)), (wide,), cost=(0, 3 * MIB),
        inputs=(send_l, recv_l, returned, own_sum, own_grad),
    )
    atom_grads = call(
        last_kernel, shape(COEF, own, LANES), cost=(0, 2 * MIB),
        inputs=(ghost_l, grad, before, after),
    )
    return jnp.transpose(update, (1, 0, 2)), jnp.transpose(atom_grads, (1, 0, 2))


def solution(mesh):
    whole = P(("groups", "cell"))
    return jax.shard_map(
        local,
        mesh=mesh,
        in_specs=(whole, whole, P(), P(), P()) + (whole,) * 6,
        out_specs=(whole, whole),
        check_vma=False,
    )
```

```python
import jax
import jax.numpy as jnp
from jax import lax
from jax.experimental import pallas as pl
from jax.experimental.pallas import tpu as pltpu
from jax.sharding import PartitionSpec as P

LMAX = 6
COEF = (LMAX + 1) ** 2
LANES = 128
PIECE = 104
ROWS = 16
MIB = 1024 * 1024
F32 = jnp.float32
BF16 = jnp.bfloat16


def frame_layout():
    layout = []
    offset = 0
    for degree in range(LMAX + 1):
        extent = min(degree, 2)
        layout.append((degree, degree * degree, 2 * degree + 1, extent, offset))
        offset = offset + (2 * extent + 1) * (2 * degree + 1)
    return layout


def group_places():
    places = {}
    block = 0
    for order in (0, 1, -1, 2, -2):
        for degree in range(abs(order), LMAX + 1):
            places[(degree, order)] = block
            block += 1
    return places


PLACES = group_places()
ROT = len(PLACES)
N0, N1, N2 = LMAX + 1, LMAX, LMAX - 1


def lanes(block, count=1):
    return slice(block * LANES, (block + count) * LANES)


def column(row):
    n = row.shape[1]
    first = lax.broadcasted_iota(jnp.int32, (n, n), 0)
    second = lax.broadcasted_iota(jnp.int32, (n, n), 1)
    picked = jnp.where(first == second, row, 0).astype(F32)
    return jnp.sum(picked, axis=1, keepdims=True).astype(jnp.int32)


def pick_rows(row, count, start=0):
    n = row.shape[1]
    rows = lax.broadcasted_iota(jnp.int32, (n, count), 1) + start
    return (column(row) == rows).astype(F32).astype(BF16)


def sum_rows(row, count, start=0):
    n = row.shape[1]
    rows = lax.broadcasted_iota(jnp.int32, (count, n), 0) + start
    return (row == rows).astype(F32).astype(BF16)


def dot(left, right):
    return jnp.dot(left, right, preferred_element_type=F32)


def dot_t(left, right):
    return lax.dot_general(left, right, (((1,), (1,)), ((), ())), preferred_element_type=F32)


def start(sems, *pairs):
    copies = [pltpu.make_async_copy(*pair, sems.at[i]) for i, pair in enumerate(pairs)]
    for copy in copies:
        copy.start()
    return copies


def load(sems, *pairs):
    for copy in start(sems, *pairs):
        copy.wait()


def both(first, second):
    return jnp.concatenate([first.astype(F32), second.astype(F32)], axis=0).astype(BF16)


def pack_kernel(ghost_hbm, atoms_hbm, down_ref, up_ref, ghost_ref, atoms_ref, sems):
    width = down_ref.shape[1]
    steps = sems.shape[0] - 1
    cuts = [COEF * i // steps for i in range(steps + 1)]
    spans = [pl.ds(low, high - low) for low, high in zip(cuts, cuts[1:])]
    copies = start(
        sems, (ghost_hbm, ghost_ref), *((atoms_hbm.at[span], atoms_ref.at[span]) for span in spans)
    )
    copies[0].wait()
    onehot = pick_rows(ghost_ref[...], atoms_ref.shape[1])
    for i in range(steps):
        copies[1 + i].wait()
        for m in range(cuts[i], cuts[i + 1]):
            rows = dot(onehot, atoms_ref[m])
            down_ref[m] = rows[:width].astype(BF16)
            up_ref[m] = rows[width:].astype(BF16)


def own_send_kernel(
    send_hbm, recv_hbm, atoms_hbm, cot_hbm, out_ref, ask_ref, send_ref, recv_ref, atoms_ref, cot_ref, wide, sems
):
    load(sems, (send_hbm, send_ref), (recv_hbm, recv_ref), (atoms_hbm, atoms_ref), (cot_hbm, cot_ref))
    own = atoms_ref.shape[1]
    slots = send_ref.shape[1]
    from_own = pick_rows(send_ref[...], own)
    from_cot = pick_rows(recv_ref[...], own)
    for m in range(COEF):
        wide[pl.ds(m, slots, stride=PIECE), :] = dot(from_own, atoms_ref[m])
        wide[pl.ds(COEF + m, slots, stride=PIECE), :] = dot(from_cot, cot_ref[m])
    for m in range(2 * COEF, PIECE):
        wide[pl.ds(m, slots, stride=PIECE), :] = jnp.zeros((slots, LANES), F32)
    out_ref[...] = wide[...].astype(BF16)
    ask_ref[...] = pick_rows(send_ref[...], ask_ref.shape[1], own)


def send_kernel(ask_ref, part_ref, prev_ref, next_ref, out_ref, extra):
    slots = ask_ref.shape[0]
    extra[...] = jnp.zeros(extra.shape, F32)
    onehot = ask_ref[...]
    for m in range(COEF):
        extra[pl.ds(m, slots, stride=PIECE), :] = dot(onehot, both(prev_ref[m], next_ref[m]))
    out_ref[...] = (part_ref[...].astype(F32) + extra[...]).astype(BF16)


def along(block, k):
    return jnp.broadcast_to(block[:, k : k + 1], (block.shape[0], LANES)).astype(F32)


def fill_spread(turned, spread, step):
    block = turned[pl.ds(pl.multiple_of(step * ROWS, ROWS), ROWS), :]
    for k in range(turned.shape[1]):
        spread[step, k] = along(block, k)


def store_rotated(values, order, degree, refs, step, edges):
    at = pl.ds(pl.multiple_of(step * ROWS, ROWS), ROWS)
    if order < 0:
        at = pl.ds(pl.multiple_of(step * ROWS + edges, ROWS), ROWS)
    refs[abs(order)][at, lanes(degree - abs(order))] = values.astype(BF16)


def remote_marks(src, tgt, own, ext, slots):
    return src >= ext, (tgt >= own) & (tgt < own + slots)


def local_kernel(
    src_ref, tgt_ref, frames_ref, atoms_ref, prev_ref, next_ref, cot_ref,
    near_ups, fwd0, fwd1, fwd2, turned, src_out, tgt_out,
    ups, table, target, xs, us, sems, slots,
):
    own = atoms_ref.shape[1]
    ext = table.shape[0]
    edges = src_ref.shape[1]
    src, tgt = src_ref[...], tgt_ref[...]

    far_src, far_tgt = remote_marks(src, tgt, own, ext, slots)
    kind = jnp.where(far_src, jnp.where(far_tgt, 1, 0), jnp.where(far_tgt, 2, 3))
    key = kind * edges + lax.broadcasted_iota(jnp.int32, (1, edges), 1)
    before = (column(key) < key).astype(F32)
    rank = jnp.sum(before, axis=0, keepdims=True).astype(jnp.int32)
    place = column(rank) == lax.broadcasted_iota(jnp.int32, (edges, edges), 1)

    def reorder(row):
        spots = jnp.where(place, column(row), 0).astype(F32)
        return jnp.sum(spots, axis=0, keepdims=True).astype(jnp.int32)

    src, tgt = reorder(src), reorder(tgt)
    src_out[...] = src
    tgt_out[...] = tgt
    turned[...] = dot(sum_rows(rank, edges), frames_ref[...]).astype(BF16)

    for m in range(COEF):
        table[0:own, lanes(m)] = atoms_ref[m]
        table[own:ext, lanes(m)] = both(prev_ref[m], next_ref[m])
        target[:, lanes(m)] = cot_ref[m]
    pick_src = pick_rows(src, ext)
    pick_tgt = pick_rows(tgt, own)
    for l in range(LMAX + 1):
        span = lanes(l * l, 2 * l + 1)
        xs[:, span] = dot(pick_src, table[:, span])
        us[:, span] = dot(pick_tgt, target[:, span])

    def rotate(step, carry):
        at = pl.ds(pl.multiple_of(step * ROWS, ROWS), ROWS)
        block = turned[at, :]
        for degree, anchor, span, extent, offset in frame_layout():
            orders = range(-extent, extent + 1)
            acc = [None] * len(orders)
            bcc = [None] * len(orders)
            for m in range(span):
                x = xs[at, lanes(anchor + m)]
                u = us[at, lanes(anchor + m)]
                for i in range(len(orders)):
                    k = offset + i * span + m
                    f = along(block, k)
                    acc[i] = f * x if m == 0 else acc[i] + f * x
                    bcc[i] = f * u if m == 0 else bcc[i] + f * u
            for i, order in enumerate(orders):
                store_rotated(acc[i], order, degree, (fwd0, fwd1, fwd2), step, edges)
                ups[at, lanes(PLACES[(degree, order)])] = bcc[i]
        return carry

    lax.fori_loop(0, edges // ROWS, rotate, 0)
    load(sems, (ups, near_ups))


def turn_out(spread, rows, msg, step):
    at = pl.ds(pl.multiple_of(step * ROWS, ROWS), ROWS)
    for degree, anchor, span, extent, offset in frame_layout():
        orders = range(-extent, extent + 1)
        parts = [rows[at, lanes(PLACES[(degree, order)])].astype(F32) for order in orders]
        for m in range(span):
            value = None
            for i in range(len(orders)):
                term = spread[step, offset + i * span + m] * parts[i]
                value = term if value is None else value + term
            msg[at, lanes(anchor + m)] = value.astype(BF16)


def loop(low, high, body):
    def step(i, carry):
        body(i)
        return carry

    lax.fori_loop(low, high, step, 0)


def edge_kernel(
    own, ext,
    recv_ref, src_ref, tgt_ref, turned, near0, near1, near2, near_ups, zero_hbm, one_hbm, two_hbm,
    out_ref, gated_hbm, back_hbm,
    ups, w_zero, w_one, w_two, fwd0, fwd1, fwd2,
    wide, table, target, xs, us, pre, gated, back, msg, spread, sems, sems_out,
):
    first_in = start(
        sems, (zero_hbm, w_zero), (one_hbm, w_one), (two_hbm, w_two),
    )
    edges = src_ref.shape[1]
    slots = table.shape[0]
    groups = edges // ROWS
    msg[...] = jnp.zeros(msg.shape, BF16)
    src, tgt = src_ref[...], tgt_ref[...]
    far_src, far_tgt = remote_marks(src, tgt, own, ext, slots)
    count = lambda mask: jnp.sum(mask.astype(F32)).astype(jnp.int32)
    n_src = count(far_src)
    first = count(far_src & jnp.logical_not(far_tgt))
    last = count(far_src | far_tgt)
    src_end = (n_src + ROWS - 1) // ROWS
    tgt_start, tgt_end = first // ROWS, (last + ROWS - 1) // ROWS

    pick_src = pick_rows(src, slots, ext)
    pick_tgt = pick_rows(tgt, slots, own)
    wide[...] = recv_ref[...].astype(F32)
    for m in range(COEF):
        table[:, lanes(m)] = wide[pl.ds(m, slots, stride=PIECE), :].astype(BF16)
        target[:, lanes(m)] = wide[pl.ds(COEF + m, slots, stride=PIECE), :].astype(BF16)

    for l in range(LMAX + 1):
        span = lanes(l * l, 2 * l + 1)
        xs[:, span] = dot(pick_src, table[:, span])
        us[:, span] = dot(pick_tgt, target[:, span])

    def rotate(step, far, add):
        at = pl.ds(pl.multiple_of(step * ROWS, ROWS), ROWS)
        for degree, anchor, span, extent, offset in frame_layout():
            orders = range(-extent, extent + 1)
            acc = [None] * len(orders)
            for m in range(span):
                row = far[at, lanes(anchor + m)]
                for i in range(len(orders)):
                    term = spread[step, offset + i * span + m] * row
                    acc[i] = term if m == 0 else acc[i] + term
            for i, order in enumerate(orders):
                add(acc[i], order, degree, step)

    def add_ups(value, order, degree, step):
        at = pl.ds(pl.multiple_of(step * ROWS, ROWS), ROWS)
        spot = lanes(PLACES[(degree, order)])
        ups[at, spot] = ups[at, spot] + value

    def add_fwd(value, order, degree, step):
        at = pl.ds(pl.multiple_of(step * ROWS, ROWS), ROWS)
        if order < 0:
            at = pl.ds(pl.multiple_of(step * ROWS + edges, ROWS), ROWS)
        spot = lanes(degree - abs(order))
        near = (near0, near1, near2)[abs(order)][at, spot].astype(F32)
        (fwd0, fwd1, fwd2)[abs(order)][at, spot] = (near + value).astype(BF16)

    def keep_fwd(step):
        at = pl.ds(pl.multiple_of(step * ROWS, ROWS), ROWS)
        low = pl.ds(pl.multiple_of(step * ROWS + edges, ROWS), ROWS)
        fwd0[at, :] = near0[at, :]
        for rows in (at, low):
            fwd1[rows, :] = near1[rows, :]
            fwd2[rows, :] = near2[rows, :]

    def store_fwd(value, order, degree, step):
        store_rotated(value, order, degree, (fwd0, fwd1, fwd2), step, edges)

    loop(0, jnp.maximum(src_end, tgt_end), lambda step: fill_spread(turned, spread, step))
    loop(src_end, groups, keep_fwd)
    ups_in = pltpu.make_async_copy(near_ups, ups, sems.at[3])
    ups_in.start()
    loop(0, src_end, lambda step: rotate(step, xs, add_fwd))

    def mixed(product, sign, to):
        top, low = slice(0, edges), slice(edges, 2 * edges)
        to[:, lanes(0, N0)] = product(fwd0[...], w_zero[...]).astype(to.dtype)
        real = product(fwd1[...], w_one[0])
        imag = product(fwd1[...], w_one[1])
        to[:, lanes(N0, N1)] = (real[top] - sign * imag[low]).astype(to.dtype)
        to[:, lanes(N0 + N1, N1)] = (real[low] + sign * imag[top]).astype(to.dtype)
        real = product(fwd2[...], w_two[0])
        imag = product(fwd2[...], w_two[1])
        to[:, lanes(N0 + 2 * N1, N2)] = (real[top] - sign * imag[low]).astype(to.dtype)
        to[:, lanes(N0 + 2 * N1 + N2, N2)] = (real[low] + sign * imag[top]).astype(to.dtype)

    for copy in first_in:
        copy.wait()
    mixed(dot, 1.0, pre)
    ups_in.wait()
    loop(tgt_start, tgt_end, lambda step: rotate(step, us, add_ups))

    def gating(step):
        at = pl.ds(pl.multiple_of(step * ROWS, ROWS), ROWS)
        scale = jax.nn.sigmoid(pre[at, lanes(0)])
        total = None
        for (degree, order), block in PLACES.items():
            above = ups[at, lanes(block)]
            below = pre[at, lanes(block)] * above
            total = below if total is None else total + below
            gated[at, lanes(block)] = (pre[at, lanes(block)] * scale).astype(BF16)
            if block:
                store_fwd(above * scale, order, degree, step)
        first_row = ups[at, lanes(0)] * scale + total * (scale * (1.0 - scale))
        store_fwd(first_row, 0, 0, step)

    loop(0, groups, gating)
    gated_out, = start(sems_out, (gated, gated_hbm))

    def far_sums(row, start, place):
        onehot = sum_rows(row, slots, start)
        for l in range(LMAX + 1):
            anchor, span = l * l, 2 * l + 1
            sums = dot(onehot, msg[:, lanes(anchor, span)])
            for m in range(span):
                wide[pl.ds(place + anchor + m, slots, stride=PIECE), :] = sums[:, lanes(m)]

    loop(tgt_start, tgt_end, lambda step: turn_out(spread, gated, msg, step))
    far_sums(tgt, own, 0)
    mixed(dot_t, -1.0, back)
    back_out = pltpu.make_async_copy(back, back_hbm, sems_out.at[1])
    back_out.start()
    loop(0, src_end, lambda step: turn_out(spread, back, msg, step))
    far_sums(src, ext, COEF)
    for m in range(2 * COEF, PIECE):
        wide[pl.ds(m, slots, stride=PIECE), :] = jnp.zeros((slots, LANES), F32)
    out_ref[...] = wide[...].astype(BF16)
    gated_out.wait()
    back_out.wait()


def near_kernel(
    src_ref, tgt_ref, turned, gated, back, own_sum_ref, own_grad_ref, ghost_grad_ref, msg, spread
):
    edges = src_ref.shape[1]
    own = own_sum_ref.shape[1]
    ext = own + ghost_grad_ref.shape[1]

    def sums(onehot, store):
        for l in range(LMAX + 1):
            anchor, span = l * l, 2 * l + 1
            rows = dot(onehot, msg[:, lanes(anchor, span)])
            for m in range(span):
                store(anchor + m, rows[:, lanes(m)])

    def store_sum(m, rows):
        own_sum_ref[m] = rows

    def store_grad(m, rows):
        own_grad_ref[m] = rows[:own]
        ghost_grad_ref[m] = rows[own:]

    loop(0, edges // ROWS, lambda step: fill_spread(turned, spread, step))
    loop(0, edges // ROWS, lambda step: turn_out(spread, gated, msg, step))
    sums(sum_rows(tgt_ref[...], own), store_sum)
    loop(0, edges // ROWS, lambda step: turn_out(spread, back, msg, step))
    sums(sum_rows(src_ref[...], ext), store_grad)


def ghost_kernel(own, send_ref, back_ref, ghost_grad_ref, prev_ref, next_ref, wide):
    slots = send_ref.shape[1]
    ghosts = ghost_grad_ref.shape[1]
    wide[...] = back_ref[...].astype(F32)
    onehot = sum_rows(send_ref[...], ghosts, own)
    for m in range(COEF):
        back = wide[pl.ds(COEF + m, slots, stride=PIECE), :].astype(BF16)
        rows = ghost_grad_ref[m] + dot(onehot, back)
        prev_ref[m] = rows[: ghosts // 2].astype(BF16)
        next_ref[m] = rows[ghosts // 2 :].astype(BF16)


def own_kernel(send_ref, recv_ref, back_ref, own_sum_ref, own_grad_ref, update_ref, grad_ref, wide):
    slots = send_ref.shape[1]
    own = own_sum_ref.shape[1]
    wide[...] = back_ref[...].astype(F32)
    from_tgt = sum_rows(recv_ref[...], own)
    from_src = sum_rows(send_ref[...], own)
    for m in range(COEF):
        back = wide[pl.ds(m, slots, stride=PIECE), :].astype(BF16)
        update_ref[m] = (own_sum_ref[m] + dot(from_tgt, back)).astype(BF16)
        back = wide[pl.ds(COEF + m, slots, stride=PIECE), :].astype(BF16)
        grad_ref[m] = own_grad_ref[m] + dot(from_src, back)


def last_kernel(ghost_ref, grad_ref, before_ref, after_ref, out_hbm, out, sems):
    onehot = sum_rows(ghost_ref[...], grad_ref.shape[1])
    parts = sems.shape[0]
    cuts = [COEF * i // parts for i in range(parts + 1)]
    copies = []
    for i in range(parts):
        for m in range(cuts[i], cuts[i + 1]):
            out[m] = (grad_ref[m] + dot(onehot, both(before_ref[m], after_ref[m]))).astype(BF16)
        span = pl.ds(cuts[i], cuts[i + 1] - cuts[i])
        copies.append(pltpu.make_async_copy(out.at[span], out_hbm.at[span], sems.at[i]))
        copies[-1].start()
    for copy in copies:
        copy.wait()


def shape(*dims, dtype=BF16):
    return jax.ShapeDtypeStruct(dims, dtype)


def call(kernel, out_shape, scratch=(), limit=12, hbm=(), hbm_out=(), cost=(0, 0), inputs=()):
    specs = [
        pl.BlockSpec(memory_space=pltpu.HBM if i in hbm else pltpu.VMEM) for i in range(len(inputs))
    ]
    inputs = [
        pltpu.with_memory_space_constraint(x, pltpu.HBM) if i in hbm else x
        for i, x in enumerate(inputs)
    ]
    return pl.pallas_call(
        kernel,
        out_shape=jax.tree.map(
            lambda s: pltpu.HBM(s.shape, s.dtype) if s in hbm_out else s, out_shape
        ),
        in_specs=specs,
        out_specs=jax.tree.map(
            lambda s: pl.BlockSpec(memory_space=pltpu.HBM if s in hbm_out else pltpu.VMEM), out_shape
        ),
        scratch_shapes=scratch,
        compiler_params=pltpu.CompilerParams(vmem_limit_bytes=limit * MIB),
        cost_estimate=pl.CostEstimate(flops=cost[0], bytes_accessed=cost[1], transcendentals=0),
    )(*inputs)


def local(
    atoms,
    frames,
    w_zero,
    w_one,
    w_two,
    cotangent,
    ghost_rows,
    send_rows,
    recv_rows,
    edge_src,
    edge_tgt,
):
    own = atoms.shape[0]
    half = ghost_rows.shape[0] // 2
    slots = send_rows.shape[0]
    edges = edge_src.shape[0]
    ext = own + 2 * half
    cells = lax.axis_size("cell")
    up = [(i, (i + 1) % cells) for i in range(cells)]
    down = [(j, i) for i, j in up]
    atoms_t = jnp.transpose(atoms, (1, 0, 2))
    cot_t = jnp.transpose(cotangent, (1, 0, 2))
    ghost_l, send_l, recv_l, src_l, tgt_l = (
        row.reshape(1, -1) for row in (ghost_rows, send_rows, recv_rows, edge_src, edge_tgt)
    )
    pack = shape(COEF, half, LANES)
    result = shape(COEF, own, LANES)
    bundle = shape(slots * PIECE, LANES)
    wide = pltpu.VMEM((slots * PIECE, LANES), F32)
    rows = pltpu.VMEM((COEF, own, LANES), BF16)
    index = shape(1, edges, dtype=jnp.int32)
    coefs = lambda n, dtype: shape(edges, n * LANES, dtype=dtype)
    scratch = lambda s: pltpu.VMEM(s.shape, s.dtype)
    short = lambda x: pltpu.VMEM(x.shape, jnp.int32)
    exchange = lambda x: lax.all_to_all(x, "cell", 0, 0, tiled=True)
    mixing = [coefs(N0, BF16), shape(2 * edges, N1 * LANES), shape(2 * edges, N2 * LANES)]
    every = coefs(COEF, F32)
    turned = coefs(ROT, F32)
    rounded = coefs(ROT, BF16)

    to_down, to_up = call(
        pack_kernel, (pack, pack), (short(ghost_l), rows, pltpu.SemaphoreType.DMA((2,))),
        hbm=(0, 1), cost=(0, MIB), inputs=(ghost_l, atoms_t),
    )
    from_prev = lax.ppermute(to_up, "cell", up)
    from_next = lax.ppermute(to_down, "cell", down)
    part, ask = call(
        own_send_kernel, (bundle, shape(slots, 2 * half)),
        (short(send_l), short(recv_l), rows, rows, wide, pltpu.SemaphoreType.DMA((4,))),
        hbm=(0, 1, 2, 3), cost=(0, 3 * MIB), inputs=(send_l, recv_l, atoms_t, cot_t),
    )
    outgoing = call(
        send_kernel, bundle, (wide,), cost=(0, MIB),
        inputs=(ask, part, from_prev, from_next),
    )
    received = exchange(outgoing)
    spread = pltpu.VMEM((edges // ROWS, frames.shape[1], ROWS, LANES), F32)
    near = call(
        lambda *refs: local_kernel(*refs, slots),
        [turned] + mixing + [shape(*frames.shape), index, index],
        [
            scratch(turned),
            pltpu.VMEM((ext, COEF * LANES), BF16),
            pltpu.VMEM((own, COEF * LANES), BF16),
            scratch(every),
            scratch(every),
            pltpu.SemaphoreType.DMA((1,)),
        ],
        cost=(1 << 31, 24 * MIB), limit=24, hbm_out=(turned,),
        inputs=(src_l, tgt_l, frames, atoms_t, from_prev, from_next, cot_t),
    )
    near_ups, near0, near1, near2, frames_p, src_p, tgt_p = near
    far_rows = pltpu.VMEM((slots, COEF * LANES), BF16)
    inputs = (
        received, src_p, tgt_p, frames_p, near0, near1, near2, near_ups, w_zero, w_one, w_two
    )
    partial, gated, back = call(
        lambda *refs: edge_kernel(own, ext, *refs),
        (bundle, rounded, rounded),
        [scratch(x) for x in inputs[7:]]
        + [scratch(x) for x in mixing]
        + [wide, far_rows, far_rows, scratch(every), scratch(every), scratch(turned), scratch(rounded), scratch(rounded)]
        + [
            scratch(coefs(COEF, BF16)),
            spread,
            pltpu.SemaphoreType.DMA((4,)),
            pltpu.SemaphoreType.DMA((2,)),
        ],
        cost=(3 << 30, 24 * MIB), limit=44, hbm=range(7, len(inputs)), hbm_out=(rounded,),
        inputs=inputs,
    )
    returned = exchange(partial)
    own_sum, own_grad, ghost_grad = call(
        near_kernel,
        (
            shape(COEF, own, LANES, dtype=F32),
            shape(COEF, own, LANES, dtype=F32),
            shape(COEF, 2 * half, LANES, dtype=F32),
        ),
        [scratch(coefs(COEF, BF16)), spread],
        cost=(1 << 30, 20 * MIB), limit=28,
        inputs=(src_p, tgt_p, frames_p, gated, back),
    )
    to_prev, to_next = call(
        lambda *refs: ghost_kernel(own, *refs), (pack, pack), (wide,), cost=(0, MIB),
        inputs=(send_l, returned, ghost_grad),
    )
    after = lax.ppermute(to_prev, "cell", down)
    before = lax.ppermute(to_next, "cell", up)
    update, grad = call(
        own_kernel,
        (shape(COEF, own, LANES), shape(COEF, own, LANES, dtype=F32)), (wide,), cost=(0, 3 * MIB),
        inputs=(send_l, recv_l, returned, own_sum, own_grad),
    )
    atom_grads = call(
        last_kernel, result, (scratch(result), pltpu.SemaphoreType.DMA((4,))),
        hbm_out=(result,), cost=(0, 2 * MIB),
        inputs=(ghost_l, grad, before, after),
    )
    return jnp.transpose(update, (1, 0, 2)), jnp.transpose(atom_grads, (1, 0, 2))


def solution(mesh):
    whole = P(("groups", "cell"))
    return jax.shard_map(
        local,
        mesh=mesh,
        in_specs=(whole, whole, P(), P(), P()) + (whole,) * 6,
        out_specs=(whole, whole),
        check_vma=False,
    )
```

```python
import jax
import jax.numpy as jnp
from jax import lax
from jax.experimental import pallas as pl
from jax.experimental.pallas import tpu as pltpu
from jax.sharding import PartitionSpec as P

LMAX = 6
COEF = (LMAX + 1) ** 2
LANES = 128
PIECE = 104
ROWS = 16
MIB = 1024 * 1024
F32 = jnp.float32
BF16 = jnp.bfloat16


def frame_layout():
    layout = []
    offset = 0
    for degree in range(LMAX + 1):
        extent = min(degree, 2)
        layout.append((degree, degree * degree, 2 * degree + 1, extent, offset))
        offset = offset + (2 * extent + 1) * (2 * degree + 1)
    return layout


def group_places():
    places = {}
    block = 0
    for order in (0, 1, -1, 2, -2):
        for degree in range(abs(order), LMAX + 1):
            places[(degree, order)] = block
            block += 1
    return places


PLACES = group_places()
ROT = len(PLACES)
N0, N1, N2 = LMAX + 1, LMAX, LMAX - 1


def lanes(block, count=1):
    return slice(block * LANES, (block + count) * LANES)


def column(row):
    n = row.shape[1]
    first = lax.broadcasted_iota(jnp.int32, (n, n), 0)
    second = lax.broadcasted_iota(jnp.int32, (n, n), 1)
    picked = jnp.where(first == second, row, 0).astype(F32)
    return jnp.sum(picked, axis=1, keepdims=True).astype(jnp.int32)


def pick_rows(row, count, start=0):
    n = row.shape[1]
    rows = lax.broadcasted_iota(jnp.int32, (n, count), 1) + start
    return (column(row) == rows).astype(F32).astype(BF16)


def sum_rows(row, count, start=0):
    n = row.shape[1]
    rows = lax.broadcasted_iota(jnp.int32, (count, n), 0) + start
    return (row == rows).astype(F32).astype(BF16)


def dot(left, right):
    return jnp.dot(left, right, preferred_element_type=F32)


def dot_t(left, right):
    return lax.dot_general(left, right, (((1,), (1,)), ((), ())), preferred_element_type=F32)


def start(sems, *pairs):
    copies = [pltpu.make_async_copy(*pair, sems.at[i]) for i, pair in enumerate(pairs)]
    for copy in copies:
        copy.start()
    return copies


def load(sems, *pairs):
    for copy in start(sems, *pairs):
        copy.wait()


def both(first, second):
    return jnp.concatenate([first.astype(F32), second.astype(F32)], axis=0).astype(BF16)


def pack_kernel(ghost_hbm, atoms_hbm, down_ref, up_ref, ghost_ref, atoms_ref, sems):
    width = down_ref.shape[1]
    steps = sems.shape[0] - 1
    cuts = [COEF * i // steps for i in range(steps + 1)]
    spans = [pl.ds(low, high - low) for low, high in zip(cuts, cuts[1:])]
    copies = start(
        sems, (ghost_hbm, ghost_ref), *((atoms_hbm.at[span], atoms_ref.at[span]) for span in spans)
    )
    copies[0].wait()
    onehot = pick_rows(ghost_ref[...], atoms_ref.shape[1])
    for i in range(steps):
        copies[1 + i].wait()
        for m in range(cuts[i], cuts[i + 1]):
            rows = dot(onehot, atoms_ref[m])
            down_ref[m] = rows[:width].astype(BF16)
            up_ref[m] = rows[width:].astype(BF16)


def own_send_kernel(
    send_hbm, recv_hbm, atoms_hbm, cot_hbm, out_ref, ask_ref, send_ref, recv_ref, atoms_ref, cot_ref, wide, sems
):
    load(sems, (send_hbm, send_ref), (recv_hbm, recv_ref), (atoms_hbm, atoms_ref), (cot_hbm, cot_ref))
    own = atoms_ref.shape[1]
    slots = send_ref.shape[1]
    from_own = pick_rows(send_ref[...], own)
    from_cot = pick_rows(recv_ref[...], own)
    for m in range(COEF):
        wide[pl.ds(m, slots, stride=PIECE), :] = dot(from_own, atoms_ref[m])
        wide[pl.ds(COEF + m, slots, stride=PIECE), :] = dot(from_cot, cot_ref[m])
    for m in range(2 * COEF, PIECE):
        wide[pl.ds(m, slots, stride=PIECE), :] = jnp.zeros((slots, LANES), F32)
    out_ref[...] = wide[...].astype(BF16)
    ask_ref[...] = pick_rows(send_ref[...], ask_ref.shape[1], own)


def send_kernel(ask_ref, part_ref, prev_ref, next_ref, out_ref, extra):
    slots = ask_ref.shape[0]
    extra[...] = jnp.zeros(extra.shape, F32)
    onehot = ask_ref[...]
    for m in range(COEF):
        extra[pl.ds(m, slots, stride=PIECE), :] = dot(onehot, both(prev_ref[m], next_ref[m]))
    out_ref[...] = (part_ref[...].astype(F32) + extra[...]).astype(BF16)


def along(block, k):
    return jnp.broadcast_to(block[:, k : k + 1], (block.shape[0], LANES)).astype(F32)


def fill_spread(turned, spread, step):
    block = turned[pl.ds(pl.multiple_of(step * ROWS, ROWS), ROWS), :]
    for k in range(turned.shape[1]):
        spread[step, k] = along(block, k)


def store_rotated(values, order, degree, refs, step, edges):
    at = pl.ds(pl.multiple_of(step * ROWS, ROWS), ROWS)
    if order < 0:
        at = pl.ds(pl.multiple_of(step * ROWS + edges, ROWS), ROWS)
    refs[abs(order)][at, lanes(degree - abs(order))] = values.astype(BF16)


def remote_marks(src, tgt, own, ext, slots):
    return src >= ext, (tgt >= own) & (tgt < own + slots)


def local_kernel(
    src_ref, tgt_ref, frames_ref, atoms_ref, prev_ref, next_ref, cot_ref,
    near_ups, fwd0, fwd1, fwd2, turned, src_out, tgt_out, far_src_ref, far_tgt_ref,
    ups, table, target, xs, us, sems, slots,
):
    own = atoms_ref.shape[1]
    ext = table.shape[0]
    edges = src_ref.shape[1]
    src, tgt = src_ref[...], tgt_ref[...]

    far_src, far_tgt = remote_marks(src, tgt, own, ext, slots)
    kind = jnp.where(far_src, jnp.where(far_tgt, 1, 0), jnp.where(far_tgt, 2, 3))
    key = kind * edges + lax.broadcasted_iota(jnp.int32, (1, edges), 1)
    before = (column(key) < key).astype(F32)
    rank = jnp.sum(before, axis=0, keepdims=True).astype(jnp.int32)
    place = column(rank) == lax.broadcasted_iota(jnp.int32, (edges, edges), 1)

    def reorder(row):
        spots = jnp.where(place, column(row), 0).astype(F32)
        return jnp.sum(spots, axis=0, keepdims=True).astype(jnp.int32)

    src, tgt = reorder(src), reorder(tgt)
    src_out[...] = src
    tgt_out[...] = tgt
    far_src_ref[...] = pick_rows(src, slots, ext)
    far_tgt_ref[...] = pick_rows(tgt, slots, own)
    turned[...] = dot(sum_rows(rank, edges), frames_ref[...]).astype(BF16)

    for m in range(COEF):
        table[0:own, lanes(m)] = atoms_ref[m]
        table[own:ext, lanes(m)] = both(prev_ref[m], next_ref[m])
        target[:, lanes(m)] = cot_ref[m]
    pick_src = pick_rows(src, ext)
    pick_tgt = pick_rows(tgt, own)
    for l in range(LMAX + 1):
        span = lanes(l * l, 2 * l + 1)
        xs[:, span] = dot(pick_src, table[:, span])
        us[:, span] = dot(pick_tgt, target[:, span])

    def rotate(step, carry):
        at = pl.ds(pl.multiple_of(step * ROWS, ROWS), ROWS)
        block = turned[at, :]
        for degree, anchor, span, extent, offset in frame_layout():
            orders = range(-extent, extent + 1)
            acc = [None] * len(orders)
            bcc = [None] * len(orders)
            for m in range(span):
                x = xs[at, lanes(anchor + m)]
                u = us[at, lanes(anchor + m)]
                for i in range(len(orders)):
                    k = offset + i * span + m
                    f = along(block, k)
                    acc[i] = f * x if m == 0 else acc[i] + f * x
                    bcc[i] = f * u if m == 0 else bcc[i] + f * u
            for i, order in enumerate(orders):
                store_rotated(acc[i], order, degree, (fwd0, fwd1, fwd2), step, edges)
                ups[at, lanes(PLACES[(degree, order)])] = bcc[i]
        return carry

    lax.fori_loop(0, edges // ROWS, rotate, 0)
    load(sems, (ups, near_ups))


def turn_out(spread, rows, msg, step):
    at = pl.ds(pl.multiple_of(step * ROWS, ROWS), ROWS)
    for degree, anchor, span, extent, offset in frame_layout():
        orders = range(-extent, extent + 1)
        parts = [rows[at, lanes(PLACES[(degree, order)])].astype(F32) for order in orders]
        for m in range(span):
            value = None
            for i in range(len(orders)):
                term = spread[step, offset + i * span + m] * parts[i]
                value = term if value is None else value + term
            msg[at, lanes(anchor + m)] = value.astype(BF16)


def loop(low, high, body):
    def step(i, carry):
        body(i)
        return carry

    lax.fori_loop(low, high, step, 0)


def edge_kernel(
    own, ext,
    recv_ref, far_src_ref, far_tgt_ref, src_ref, tgt_ref, turned, near0, near1, near2, near_ups, zero_hbm, one_hbm, two_hbm,
    out_ref, gated_hbm, back_hbm,
    ups, w_zero, w_one, w_two, fwd0, fwd1, fwd2,
    wide, table, target, xs, us, pre, gated, back, msg, spread, sems, sems_out,
):
    first_in = start(
        sems, (zero_hbm, w_zero), (one_hbm, w_one), (two_hbm, w_two),
    )
    edges = src_ref.shape[1]
    slots = table.shape[0]
    groups = edges // ROWS
    msg[...] = jnp.zeros(msg.shape, BF16)
    src, tgt = src_ref[...], tgt_ref[...]
    far_src, far_tgt = remote_marks(src, tgt, own, ext, slots)
    only_src = far_src & jnp.logical_not(far_tgt)
    marks = jnp.where(far_src, 1.0, 0.0) + jnp.where(only_src, 256.0, 0.0)
    marks = marks + jnp.where(far_src | far_tgt, 65536.0, 0.0)
    counts = jnp.sum(marks).astype(jnp.int32)
    n_src, first, last = counts & 255, (counts >> 8) & 255, counts >> 16
    src_end = (n_src + ROWS - 1) // ROWS
    tgt_start, tgt_end = first // ROWS, (last + ROWS - 1) // ROWS

    pick_src, pick_tgt = far_src_ref[...], far_tgt_ref[...]
    wide[...] = recv_ref[...].astype(F32)
    for m in range(COEF):
        table[:, lanes(m)] = wide[pl.ds(m, slots, stride=PIECE), :].astype(BF16)
        target[:, lanes(m)] = wide[pl.ds(COEF + m, slots, stride=PIECE), :].astype(BF16)

    for l in range(LMAX + 1):
        span = lanes(l * l, 2 * l + 1)
        xs[:, span] = dot(pick_src, table[:, span])
        us[:, span] = dot(pick_tgt, target[:, span])

    def rotate(step, far, add):
        at = pl.ds(pl.multiple_of(step * ROWS, ROWS), ROWS)
        for degree, anchor, span, extent, offset in frame_layout():
            orders = range(-extent, extent + 1)
            acc = [None] * len(orders)
            for m in range(span):
                row = far[at, lanes(anchor + m)]
                for i in range(len(orders)):
                    term = spread[step, offset + i * span + m] * row
                    acc[i] = term if m == 0 else acc[i] + term
            for i, order in enumerate(orders):
                add(acc[i], order, degree, step)

    def add_ups(value, order, degree, step):
        at = pl.ds(pl.multiple_of(step * ROWS, ROWS), ROWS)
        spot = lanes(PLACES[(degree, order)])
        ups[at, spot] = ups[at, spot] + value

    def add_fwd(value, order, degree, step):
        at = pl.ds(pl.multiple_of(step * ROWS, ROWS), ROWS)
        if order < 0:
            at = pl.ds(pl.multiple_of(step * ROWS + edges, ROWS), ROWS)
        spot = lanes(degree - abs(order))
        near = (near0, near1, near2)[abs(order)][at, spot].astype(F32)
        (fwd0, fwd1, fwd2)[abs(order)][at, spot] = (near + value).astype(BF16)

    def keep_fwd(step):
        at = pl.ds(pl.multiple_of(step * ROWS, ROWS), ROWS)
        low = pl.ds(pl.multiple_of(step * ROWS + edges, ROWS), ROWS)
        fwd0[at, :] = near0[at, :]
        for rows in (at, low):
            fwd1[rows, :] = near1[rows, :]
            fwd2[rows, :] = near2[rows, :]

    def store_fwd(value, order, degree, step):
        store_rotated(value, order, degree, (fwd0, fwd1, fwd2), step, edges)

    loop(0, jnp.maximum(src_end, tgt_end), lambda step: fill_spread(turned, spread, step))
    loop(src_end, groups, keep_fwd)
    ups_in = pltpu.make_async_copy(near_ups, ups, sems.at[3])
    ups_in.start()
    loop(0, src_end, lambda step: rotate(step, xs, add_fwd))

    def mixed(product, sign, to):
        top, low = slice(0, edges), slice(edges, 2 * edges)
        to[:, lanes(0, N0)] = product(fwd0[...], w_zero[...]).astype(to.dtype)
        real = product(fwd1[...], w_one[0])
        imag = product(fwd1[...], w_one[1])
        to[:, lanes(N0, N1)] = (real[top] - sign * imag[low]).astype(to.dtype)
        to[:, lanes(N0 + N1, N1)] = (real[low] + sign * imag[top]).astype(to.dtype)
        real = product(fwd2[...], w_two[0])
        imag = product(fwd2[...], w_two[1])
        to[:, lanes(N0 + 2 * N1, N2)] = (real[top] - sign * imag[low]).astype(to.dtype)
        to[:, lanes(N0 + 2 * N1 + N2, N2)] = (real[low] + sign * imag[top]).astype(to.dtype)

    for copy in first_in:
        copy.wait()
    mixed(dot, 1.0, pre)
    ups_in.wait()
    loop(tgt_start, tgt_end, lambda step: rotate(step, us, add_ups))

    def gating(step):
        at = pl.ds(pl.multiple_of(step * ROWS, ROWS), ROWS)
        scale = jax.nn.sigmoid(pre[at, lanes(0)])
        total = None
        for (degree, order), block in PLACES.items():
            above = ups[at, lanes(block)]
            below = pre[at, lanes(block)] * above
            total = below if total is None else total + below
            gated[at, lanes(block)] = (pre[at, lanes(block)] * scale).astype(BF16)
            if block:
                store_fwd(above * scale, order, degree, step)
        first_row = ups[at, lanes(0)] * scale + total * (scale * (1.0 - scale))
        store_fwd(first_row, 0, 0, step)

    loop(0, groups, gating)
    gated_out, = start(sems_out, (gated, gated_hbm))

    def far_sums(row, start, place):
        onehot = sum_rows(row, slots, start)
        for l in range(LMAX + 1):
            anchor, span = l * l, 2 * l + 1
            sums = dot(onehot, msg[:, lanes(anchor, span)])
            for m in range(span):
                wide[pl.ds(place + anchor + m, slots, stride=PIECE), :] = sums[:, lanes(m)]

    loop(tgt_start, tgt_end, lambda step: turn_out(spread, gated, msg, step))
    far_sums(tgt, own, 0)
    mixed(dot_t, -1.0, back)
    back_out = pltpu.make_async_copy(back, back_hbm, sems_out.at[1])
    back_out.start()
    loop(0, src_end, lambda step: turn_out(spread, back, msg, step))
    far_sums(src, ext, COEF)
    for m in range(2 * COEF, PIECE):
        wide[pl.ds(m, slots, stride=PIECE), :] = jnp.zeros((slots, LANES), F32)
    out_ref[...] = wide[...].astype(BF16)
    gated_out.wait()
    back_out.wait()


def near_kernel(
    src_ref, tgt_ref, turned, gated, back, own_sum_ref, own_grad_ref, ghost_grad_ref, msg, spread
):
    edges = src_ref.shape[1]
    own = own_sum_ref.shape[1]
    ext = own + ghost_grad_ref.shape[1]

    def sums(onehot, store):
        for l in range(LMAX + 1):
            anchor, span = l * l, 2 * l + 1
            rows = dot(onehot, msg[:, lanes(anchor, span)])
            for m in range(span):
                store(anchor + m, rows[:, lanes(m)])

    def store_sum(m, rows):
        own_sum_ref[m] = rows

    def store_grad(m, rows):
        own_grad_ref[m] = rows[:own]
        ghost_grad_ref[m] = rows[own:]

    loop(0, edges // ROWS, lambda step: fill_spread(turned, spread, step))
    loop(0, edges // ROWS, lambda step: turn_out(spread, gated, msg, step))
    sums(sum_rows(tgt_ref[...], own), store_sum)
    loop(0, edges // ROWS, lambda step: turn_out(spread, back, msg, step))
    sums(sum_rows(src_ref[...], ext), store_grad)


def ghost_kernel(own, send_ref, back_ref, ghost_grad_ref, prev_ref, next_ref, wide):
    slots = send_ref.shape[1]
    ghosts = ghost_grad_ref.shape[1]
    wide[...] = back_ref[...].astype(F32)
    onehot = sum_rows(send_ref[...], ghosts, own)
    for m in range(COEF):
        back = wide[pl.ds(COEF + m, slots, stride=PIECE), :].astype(BF16)
        rows = ghost_grad_ref[m] + dot(onehot, back)
        prev_ref[m] = rows[: ghosts // 2].astype(BF16)
        next_ref[m] = rows[ghosts // 2 :].astype(BF16)


def own_kernel(send_ref, recv_ref, back_ref, own_sum_ref, own_grad_ref, update_ref, grad_ref, wide):
    slots = send_ref.shape[1]
    own = own_sum_ref.shape[1]
    wide[...] = back_ref[...].astype(F32)
    from_tgt = sum_rows(recv_ref[...], own)
    from_src = sum_rows(send_ref[...], own)
    for m in range(COEF):
        back = wide[pl.ds(m, slots, stride=PIECE), :].astype(BF16)
        update_ref[m] = (own_sum_ref[m] + dot(from_tgt, back)).astype(BF16)
        back = wide[pl.ds(COEF + m, slots, stride=PIECE), :].astype(BF16)
        grad_ref[m] = own_grad_ref[m] + dot(from_src, back)


def last_kernel(ghost_ref, grad_ref, before_ref, after_ref, out_hbm, out, sems):
    onehot = sum_rows(ghost_ref[...], grad_ref.shape[1])
    parts = sems.shape[0]
    cuts = [COEF * i // parts for i in range(parts + 1)]
    copies = []
    for i in range(parts):
        for m in range(cuts[i], cuts[i + 1]):
            out[m] = (grad_ref[m] + dot(onehot, both(before_ref[m], after_ref[m]))).astype(BF16)
        span = pl.ds(cuts[i], cuts[i + 1] - cuts[i])
        copies.append(pltpu.make_async_copy(out.at[span], out_hbm.at[span], sems.at[i]))
        copies[-1].start()
    for copy in copies:
        copy.wait()


def shape(*dims, dtype=BF16):
    return jax.ShapeDtypeStruct(dims, dtype)


def call(kernel, out_shape, scratch=(), limit=12, hbm=(), hbm_out=(), cost=(0, 0), inputs=()):
    specs = [
        pl.BlockSpec(memory_space=pltpu.HBM if i in hbm else pltpu.VMEM) for i in range(len(inputs))
    ]
    inputs = [
        pltpu.with_memory_space_constraint(x, pltpu.HBM) if i in hbm else x
        for i, x in enumerate(inputs)
    ]
    return pl.pallas_call(
        kernel,
        out_shape=jax.tree.map(
            lambda s: pltpu.HBM(s.shape, s.dtype) if s in hbm_out else s, out_shape
        ),
        in_specs=specs,
        out_specs=jax.tree.map(
            lambda s: pl.BlockSpec(memory_space=pltpu.HBM if s in hbm_out else pltpu.VMEM), out_shape
        ),
        scratch_shapes=scratch,
        compiler_params=pltpu.CompilerParams(vmem_limit_bytes=limit * MIB),
        cost_estimate=pl.CostEstimate(flops=cost[0], bytes_accessed=cost[1], transcendentals=0),
    )(*inputs)


def local(
    atoms,
    frames,
    w_zero,
    w_one,
    w_two,
    cotangent,
    ghost_rows,
    send_rows,
    recv_rows,
    edge_src,
    edge_tgt,
):
    own = atoms.shape[0]
    half = ghost_rows.shape[0] // 2
    slots = send_rows.shape[0]
    edges = edge_src.shape[0]
    ext = own + 2 * half
    cells = lax.axis_size("cell")
    up = [(i, (i + 1) % cells) for i in range(cells)]
    down = [(j, i) for i, j in up]
    atoms_t = jnp.transpose(atoms, (1, 0, 2))
    cot_t = jnp.transpose(cotangent, (1, 0, 2))
    ghost_l, send_l, recv_l, src_l, tgt_l = (
        row.reshape(1, -1) for row in (ghost_rows, send_rows, recv_rows, edge_src, edge_tgt)
    )
    pack = shape(COEF, half, LANES)
    result = shape(COEF, own, LANES)
    bundle = shape(slots * PIECE, LANES)
    wide = pltpu.VMEM((slots * PIECE, LANES), F32)
    rows = pltpu.VMEM((COEF, own, LANES), BF16)
    index = shape(1, edges, dtype=jnp.int32)
    coefs = lambda n, dtype: shape(edges, n * LANES, dtype=dtype)
    scratch = lambda s: pltpu.VMEM(s.shape, s.dtype)
    short = lambda x: pltpu.VMEM(x.shape, jnp.int32)
    exchange = lambda x: lax.all_to_all(x, "cell", 0, 0, tiled=True)
    mixing = [coefs(N0, BF16), shape(2 * edges, N1 * LANES), shape(2 * edges, N2 * LANES)]
    every = coefs(COEF, F32)
    turned = coefs(ROT, F32)
    rounded = coefs(ROT, BF16)

    to_down, to_up = call(
        pack_kernel, (pack, pack), (short(ghost_l), rows, pltpu.SemaphoreType.DMA((2,))),
        hbm=(0, 1), cost=(0, MIB), inputs=(ghost_l, atoms_t),
    )
    from_prev = lax.ppermute(to_up, "cell", up)
    from_next = lax.ppermute(to_down, "cell", down)
    part, ask = call(
        own_send_kernel, (bundle, shape(slots, 2 * half)),
        (short(send_l), short(recv_l), rows, rows, wide, pltpu.SemaphoreType.DMA((4,))),
        hbm=(0, 1, 2, 3), cost=(0, 3 * MIB), inputs=(send_l, recv_l, atoms_t, cot_t),
    )
    outgoing = call(
        send_kernel, bundle, (wide,), cost=(0, MIB),
        inputs=(ask, part, from_prev, from_next),
    )
    received = exchange(outgoing)
    spread = pltpu.VMEM((edges // ROWS, frames.shape[1], ROWS, LANES), F32)
    near = call(
        lambda *refs: local_kernel(*refs, slots),
        [turned] + mixing + [shape(*frames.shape), index, index] + [shape(edges, slots)] * 2,
        [
            scratch(turned),
            pltpu.VMEM((ext, COEF * LANES), BF16),
            pltpu.VMEM((own, COEF * LANES), BF16),
            scratch(every),
            scratch(every),
            pltpu.SemaphoreType.DMA((1,)),
        ],
        cost=(1 << 31, 24 * MIB), limit=24, hbm_out=(turned,),
        inputs=(src_l, tgt_l, frames, atoms_t, from_prev, from_next, cot_t),
    )
    near_ups, near0, near1, near2, frames_p, src_p, tgt_p, far_src, far_tgt = near
    far_rows = pltpu.VMEM((slots, COEF * LANES), BF16)
    inputs = (
        received, far_src, far_tgt, src_p, tgt_p, frames_p, near0, near1, near2, near_ups, w_zero, w_one, w_two
    )
    partial, gated, back = call(
        lambda *refs: edge_kernel(own, ext, *refs),
        (bundle, rounded, rounded),
        [scratch(x) for x in inputs[9:]]
        + [scratch(x) for x in mixing]
        + [wide, far_rows, far_rows, scratch(every), scratch(every), scratch(turned), scratch(rounded), scratch(rounded)]
        + [
            scratch(coefs(COEF, BF16)),
            spread,
            pltpu.SemaphoreType.DMA((4,)),
            pltpu.SemaphoreType.DMA((2,)),
        ],
        cost=(3 << 30, 24 * MIB), limit=44, hbm=range(9, len(inputs)), hbm_out=(rounded,),
        inputs=inputs,
    )
    returned = exchange(partial)
    own_sum, own_grad, ghost_grad = call(
        near_kernel,
        (
            shape(COEF, own, LANES, dtype=F32),
            shape(COEF, own, LANES, dtype=F32),
            shape(COEF, 2 * half, LANES, dtype=F32),
        ),
        [scratch(coefs(COEF, BF16)), spread],
        cost=(1 << 30, 20 * MIB), limit=28,
        inputs=(src_p, tgt_p, frames_p, gated, back),
    )
    to_prev, to_next = call(
        lambda *refs: ghost_kernel(own, *refs), (pack, pack), (wide,), cost=(0, MIB),
        inputs=(send_l, returned, ghost_grad),
    )
    after = lax.ppermute(to_prev, "cell", down)
    before = lax.ppermute(to_next, "cell", up)
    update, grad = call(
        own_kernel,
        (shape(COEF, own, LANES), shape(COEF, own, LANES, dtype=F32)), (wide,), cost=(0, 3 * MIB),
        inputs=(send_l, recv_l, returned, own_sum, own_grad),
    )
    atom_grads = call(
        last_kernel, result, (scratch(result), pltpu.SemaphoreType.DMA((4,))),
        hbm_out=(result,), cost=(0, 2 * MIB),
        inputs=(ghost_l, grad, before, after),
    )
    return jnp.transpose(update, (1, 0, 2)), jnp.transpose(atom_grads, (1, 0, 2))


def solution(mesh):
    whole = P(("groups", "cell"))
    return jax.shard_map(
        local,
        mesh=mesh,
        in_specs=(whole, whole, P(), P(), P()) + (whole,) * 6,
        out_specs=(whole, whole),
        check_vma=False,
    )
```

```python
import jax
import jax.numpy as jnp
from jax import lax
from jax.experimental import pallas as pl
from jax.experimental.pallas import tpu as pltpu
from jax.sharding import PartitionSpec as P

LMAX = 6
COEF = (LMAX + 1) ** 2
LANES = 128
PIECE = 104
ROWS = 16
MIB = 1024 * 1024
F32 = jnp.float32
BF16 = jnp.bfloat16


def frame_layout():
    layout = []
    offset = 0
    for degree in range(LMAX + 1):
        extent = min(degree, 2)
        layout.append((degree, degree * degree, 2 * degree + 1, extent, offset))
        offset = offset + (2 * extent + 1) * (2 * degree + 1)
    return layout


def group_places():
    places = {}
    block = 0
    for order in (0, 1, -1, 2, -2):
        for degree in range(abs(order), LMAX + 1):
            places[(degree, order)] = block
            block += 1
    return places


PLACES = group_places()
ROT = len(PLACES)
N0, N1, N2 = LMAX + 1, LMAX, LMAX - 1


def lanes(block, count=1):
    return slice(block * LANES, (block + count) * LANES)


def column(row):
    n = row.shape[1]
    first = lax.broadcasted_iota(jnp.int32, (n, n), 0)
    second = lax.broadcasted_iota(jnp.int32, (n, n), 1)
    picked = jnp.where(first == second, row, 0).astype(F32)
    return jnp.sum(picked, axis=1, keepdims=True).astype(jnp.int32)


def pick_rows(row, count, start=0):
    n = row.shape[1]
    rows = lax.broadcasted_iota(jnp.int32, (n, count), 1) + start
    return (column(row) == rows).astype(F32).astype(BF16)


def sum_rows(row, count, start=0):
    n = row.shape[1]
    rows = lax.broadcasted_iota(jnp.int32, (count, n), 0) + start
    return (row == rows).astype(F32).astype(BF16)


def dot(left, right):
    return jnp.dot(left, right, preferred_element_type=F32)


def dot_t(left, right):
    return lax.dot_general(left, right, (((1,), (1,)), ((), ())), preferred_element_type=F32)


def start(sems, *pairs):
    copies = [pltpu.make_async_copy(*pair, sems.at[i]) for i, pair in enumerate(pairs)]
    for copy in copies:
        copy.start()
    return copies


def load(sems, *pairs):
    for copy in start(sems, *pairs):
        copy.wait()


def both(first, second):
    return jnp.concatenate([first.astype(F32), second.astype(F32)], axis=0).astype(BF16)


def pack_kernel(ghost_hbm, atoms_hbm, down_ref, up_ref, ghost_ref, atoms_ref, sems):
    width = down_ref.shape[1]
    steps = sems.shape[0] - 1
    cuts = [COEF * i // steps for i in range(steps + 1)]
    spans = [pl.ds(low, high - low) for low, high in zip(cuts, cuts[1:])]
    copies = start(
        sems, (ghost_hbm, ghost_ref), *((atoms_hbm.at[span], atoms_ref.at[span]) for span in spans)
    )
    copies[0].wait()
    onehot = pick_rows(ghost_ref[...], atoms_ref.shape[1])
    for i in range(steps):
        copies[1 + i].wait()
        for m in range(cuts[i], cuts[i + 1]):
            rows = dot(onehot, atoms_ref[m])
            down_ref[m] = rows[:width].astype(BF16)
            up_ref[m] = rows[width:].astype(BF16)


def own_send_kernel(
    send_hbm, recv_hbm, atoms_hbm, cot_hbm, out_ref, ask_ref, send_ref, recv_ref, atoms_ref, cot_ref, wide, sems
):
    load(sems, (send_hbm, send_ref), (recv_hbm, recv_ref), (atoms_hbm, atoms_ref), (cot_hbm, cot_ref))
    own = atoms_ref.shape[1]
    slots = send_ref.shape[1]
    from_own = pick_rows(send_ref[...], own)
    from_cot = pick_rows(recv_ref[...], own)
    for m in range(COEF):
        wide[pl.ds(m, slots, stride=PIECE), :] = dot(from_own, atoms_ref[m])
        wide[pl.ds(COEF + m, slots, stride=PIECE), :] = dot(from_cot, cot_ref[m])
    for m in range(2 * COEF, PIECE):
        wide[pl.ds(m, slots, stride=PIECE), :] = jnp.zeros((slots, LANES), F32)
    out_ref[...] = wide[...].astype(BF16)
    ask_ref[...] = pick_rows(send_ref[...], ask_ref.shape[1], own)


def send_kernel(ask_ref, part_ref, prev_ref, next_ref, out_ref, extra):
    slots = ask_ref.shape[0]
    extra[...] = jnp.zeros(extra.shape, F32)
    onehot = ask_ref[...]
    for m in range(COEF):
        extra[pl.ds(m, slots, stride=PIECE), :] = dot(onehot, both(prev_ref[m], next_ref[m]))
    out_ref[...] = (part_ref[...].astype(F32) + extra[...]).astype(BF16)


def along(block, k):
    return jnp.broadcast_to(block[:, k : k + 1], (block.shape[0], LANES)).astype(F32)


def fill_spread(turned, spread, step):
    block = turned[pl.ds(pl.multiple_of(step * ROWS, ROWS), ROWS), :]
    for k in range(turned.shape[1]):
        spread[step, k] = along(block, k)


def store_rotated(values, order, degree, refs, step, edges):
    at = pl.ds(pl.multiple_of(step * ROWS, ROWS), ROWS)
    if order < 0:
        at = pl.ds(pl.multiple_of(step * ROWS + edges, ROWS), ROWS)
    refs[abs(order)][at, lanes(degree - abs(order))] = values.astype(BF16)


def remote_marks(src, tgt, own, ext, slots):
    return src >= ext, (tgt >= own) & (tgt < own + slots)


def local_kernel(
    src_ref, tgt_ref, frames_ref, atoms_ref, prev_ref, next_ref, cot_ref,
    near_ups, fwd0, fwd1, fwd2, turned, src_out, tgt_out, far_src_ref, far_tgt_ref,
    ups, table, target, xs, us, sems, slots,
):
    own = atoms_ref.shape[1]
    ext = table.shape[0]
    edges = src_ref.shape[1]
    src, tgt = src_ref[...], tgt_ref[...]

    far_src, far_tgt = remote_marks(src, tgt, own, ext, slots)
    kind = jnp.where(far_src, jnp.where(far_tgt, 1, 0), jnp.where(far_tgt, 2, 3))
    key = kind * edges + lax.broadcasted_iota(jnp.int32, (1, edges), 1)
    before = (column(key) < key).astype(F32)
    rank = jnp.sum(before, axis=0, keepdims=True).astype(jnp.int32)
    place = column(rank) == lax.broadcasted_iota(jnp.int32, (edges, edges), 1)

    def reorder(row):
        spots = jnp.where(place, column(row), 0).astype(F32)
        return jnp.sum(spots, axis=0, keepdims=True).astype(jnp.int32)

    src, tgt = reorder(src), reorder(tgt)
    src_out[...] = src
    tgt_out[...] = tgt
    far_src_ref[...] = pick_rows(src, slots, ext)
    far_tgt_ref[...] = pick_rows(tgt, slots, own)
    turned[...] = dot(sum_rows(rank, edges), frames_ref[...]).astype(BF16)

    for m in range(COEF):
        table[0:own, lanes(m)] = atoms_ref[m]
        table[own:ext, lanes(m)] = both(prev_ref[m], next_ref[m])
        target[:, lanes(m)] = cot_ref[m]
    pick_src = pick_rows(src, ext)
    pick_tgt = pick_rows(tgt, own)
    for l in range(LMAX + 1):
        span = lanes(l * l, 2 * l + 1)
        xs[:, span] = dot(pick_src, table[:, span])
        us[:, span] = dot(pick_tgt, target[:, span])

    def rotate(step, carry):
        at = pl.ds(pl.multiple_of(step * ROWS, ROWS), ROWS)
        block = turned[at, :]
        for degree, anchor, span, extent, offset in frame_layout():
            orders = range(-extent, extent + 1)
            acc = [None] * len(orders)
            bcc = [None] * len(orders)
            for m in range(span):
                x = xs[at, lanes(anchor + m)]
                u = us[at, lanes(anchor + m)]
                for i in range(len(orders)):
                    k = offset + i * span + m
                    f = along(block, k)
                    acc[i] = f * x if m == 0 else acc[i] + f * x
                    bcc[i] = f * u if m == 0 else bcc[i] + f * u
            for i, order in enumerate(orders):
                store_rotated(acc[i], order, degree, (fwd0, fwd1, fwd2), step, edges)
                ups[at, lanes(PLACES[(degree, order)])] = bcc[i]
        return carry

    lax.fori_loop(0, edges // ROWS, rotate, 0)
    load(sems, (ups, near_ups))


def turn_out(spread, rows, msg, step):
    at = pl.ds(pl.multiple_of(step * ROWS, ROWS), ROWS)
    for degree, anchor, span, extent, offset in frame_layout():
        orders = range(-extent, extent + 1)
        parts = [rows[at, lanes(PLACES[(degree, order)])].astype(F32) for order in orders]
        for m in range(span):
            value = None
            for i in range(len(orders)):
                term = spread[step, offset + i * span + m] * parts[i]
                value = term if value is None else value + term
            msg[at, lanes(anchor + m)] = value.astype(BF16)


def loop(low, high, body):
    def step(i, carry):
        body(i)
        return carry

    lax.fori_loop(low, high, step, 0)


def edge_kernel(
    own, ext,
    recv_ref, far_src_ref, far_tgt_ref, src_ref, tgt_ref, turned, near0, near1, near2, near_ups, zero_hbm, one_hbm, two_hbm,
    out_ref, gated_hbm, back_hbm,
    ups, w_zero, w_one, w_two, fwd0, fwd1, fwd2,
    wide, table, target, xs, us, pre, gated, back, msg, spread, sems, sems_out,
):
    first_in = start(
        sems, (zero_hbm, w_zero), (one_hbm, w_one), (two_hbm, w_two),
    )
    edges = src_ref.shape[1]
    slots = table.shape[0]
    groups = edges // ROWS
    src, tgt = src_ref[...], tgt_ref[...]
    far_src, far_tgt = remote_marks(src, tgt, own, ext, slots)
    only_src = far_src & jnp.logical_not(far_tgt)
    marks = jnp.where(far_src, 1.0, 0.0) + jnp.where(only_src, 256.0, 0.0)
    marks = marks + jnp.where(far_src | far_tgt, 65536.0, 0.0)
    counts = jnp.sum(marks).astype(jnp.int32)
    n_src, first, last = counts & 255, (counts >> 8) & 255, counts >> 16
    src_end = (n_src + ROWS - 1) // ROWS
    tgt_start, tgt_end = first // ROWS, (last + ROWS - 1) // ROWS

    pick_src, pick_tgt = far_src_ref[...], far_tgt_ref[...]
    wide[...] = recv_ref[...].astype(F32)
    for m in range(COEF):
        table[:, lanes(m)] = wide[pl.ds(m, slots, stride=PIECE), :].astype(BF16)
        target[:, lanes(m)] = wide[pl.ds(COEF + m, slots, stride=PIECE), :].astype(BF16)

    for l in range(LMAX + 1):
        span = lanes(l * l, 2 * l + 1)
        xs[:, span] = dot(pick_src, table[:, span])
        us[:, span] = dot(pick_tgt, target[:, span])

    def rotate(step, far, add):
        at = pl.ds(pl.multiple_of(step * ROWS, ROWS), ROWS)
        for degree, anchor, span, extent, offset in frame_layout():
            orders = range(-extent, extent + 1)
            acc = [None] * len(orders)
            for m in range(span):
                row = far[at, lanes(anchor + m)]
                for i in range(len(orders)):
                    term = spread[step, offset + i * span + m] * row
                    acc[i] = term if m == 0 else acc[i] + term
            for i, order in enumerate(orders):
                add(acc[i], order, degree, step)

    def add_ups(value, order, degree, step):
        at = pl.ds(pl.multiple_of(step * ROWS, ROWS), ROWS)
        spot = lanes(PLACES[(degree, order)])
        ups[at, spot] = ups[at, spot] + value

    def add_fwd(value, order, degree, step):
        at = pl.ds(pl.multiple_of(step * ROWS, ROWS), ROWS)
        if order < 0:
            at = pl.ds(pl.multiple_of(step * ROWS + edges, ROWS), ROWS)
        spot = lanes(degree - abs(order))
        near = (near0, near1, near2)[abs(order)][at, spot].astype(F32)
        (fwd0, fwd1, fwd2)[abs(order)][at, spot] = (near + value).astype(BF16)

    def keep_fwd(step):
        at = pl.ds(pl.multiple_of(step * ROWS, ROWS), ROWS)
        low = pl.ds(pl.multiple_of(step * ROWS + edges, ROWS), ROWS)
        fwd0[at, :] = near0[at, :]
        for rows in (at, low):
            fwd1[rows, :] = near1[rows, :]
            fwd2[rows, :] = near2[rows, :]

    def store_fwd(value, order, degree, step):
        store_rotated(value, order, degree, (fwd0, fwd1, fwd2), step, edges)

    loop(0, jnp.maximum(src_end, tgt_end), lambda step: fill_spread(turned, spread, step))
    loop(src_end, groups, keep_fwd)
    ups_in = pltpu.make_async_copy(near_ups, ups, sems.at[3])
    ups_in.start()
    loop(0, src_end, lambda step: rotate(step, xs, add_fwd))

    def mixed(product, sign, to):
        top, low = slice(0, edges), slice(edges, 2 * edges)
        to[:, lanes(0, N0)] = product(fwd0[...], w_zero[...]).astype(to.dtype)
        real = product(fwd1[...], w_one[0])
        imag = product(fwd1[...], w_one[1])
        to[:, lanes(N0, N1)] = (real[top] - sign * imag[low]).astype(to.dtype)
        to[:, lanes(N0 + N1, N1)] = (real[low] + sign * imag[top]).astype(to.dtype)
        real = product(fwd2[...], w_two[0])
        imag = product(fwd2[...], w_two[1])
        to[:, lanes(N0 + 2 * N1, N2)] = (real[top] - sign * imag[low]).astype(to.dtype)
        to[:, lanes(N0 + 2 * N1 + N2, N2)] = (real[low] + sign * imag[top]).astype(to.dtype)

    for copy in first_in:
        copy.wait()
    mixed(dot, 1.0, pre)
    ups_in.wait()
    loop(tgt_start, tgt_end, lambda step: rotate(step, us, add_ups))

    def gating(step):
        at = pl.ds(pl.multiple_of(step * ROWS, ROWS), ROWS)
        scale = jax.nn.sigmoid(pre[at, lanes(0)])
        total = None
        for (degree, order), block in PLACES.items():
            above = ups[at, lanes(block)]
            below = pre[at, lanes(block)] * above
            total = below if total is None else total + below
            gated[at, lanes(block)] = (pre[at, lanes(block)] * scale).astype(BF16)
            if block:
                store_fwd(above * scale, order, degree, step)
        first_row = ups[at, lanes(0)] * scale + total * (scale * (1.0 - scale))
        store_fwd(first_row, 0, 0, step)

    lax.fori_loop(0, groups, lambda step, carry: (gating(step), carry)[1], 0, unroll=2)
    gated_out, = start(sems_out, (gated, gated_hbm))

    def far_sums(row, start, place):
        onehot = sum_rows(row, slots, start)
        for l in range(LMAX + 1):
            anchor, span = l * l, 2 * l + 1
            sums = dot(onehot, msg[:, lanes(anchor, span)])
            for m in range(span):
                wide[pl.ds(place + anchor + m, slots, stride=PIECE), :] = sums[:, lanes(m)]

    def clear(step):
        at = pl.ds(pl.multiple_of(step * ROWS, ROWS), ROWS)
        msg[at, :] = jnp.zeros((ROWS, msg.shape[1]), BF16)

    loop(0, tgt_start, clear)
    loop(tgt_end, groups, clear)
    loop(tgt_start, tgt_end, lambda step: turn_out(spread, gated, msg, step))
    far_sums(tgt, own, 0)
    mixed(dot_t, -1.0, back)
    back_out = pltpu.make_async_copy(back, back_hbm, sems_out.at[1])
    back_out.start()
    loop(0, src_end, lambda step: turn_out(spread, back, msg, step))
    far_sums(src, ext, COEF)
    for m in range(2 * COEF, PIECE):
        wide[pl.ds(m, slots, stride=PIECE), :] = jnp.zeros((slots, LANES), F32)
    out_ref[...] = wide[...].astype(BF16)
    gated_out.wait()
    back_out.wait()


def near_kernel(
    src_ref, tgt_ref, turned, gated, back, own_sum_ref, own_grad_ref, ghost_grad_ref, msg, spread
):
    edges = src_ref.shape[1]
    own = own_sum_ref.shape[1]
    ext = own + ghost_grad_ref.shape[1]

    def sums(onehot, store):
        for l in range(LMAX + 1):
            anchor, span = l * l, 2 * l + 1
            rows = dot(onehot, msg[:, lanes(anchor, span)])
            for m in range(span):
                store(anchor + m, rows[:, lanes(m)])

    def store_sum(m, rows):
        own_sum_ref[m] = rows

    def store_grad(m, rows):
        own_grad_ref[m] = rows[:own]
        ghost_grad_ref[m] = rows[own:]

    loop(0, edges // ROWS, lambda step: fill_spread(turned, spread, step))
    loop(0, edges // ROWS, lambda step: turn_out(spread, gated, msg, step))
    sums(sum_rows(tgt_ref[...], own), store_sum)
    loop(0, edges // ROWS, lambda step: turn_out(spread, back, msg, step))
    sums(sum_rows(src_ref[...], ext), store_grad)


def ghost_kernel(own, send_ref, back_ref, ghost_grad_ref, prev_ref, next_ref, wide):
    slots = send_ref.shape[1]
    ghosts = ghost_grad_ref.shape[1]
    wide[...] = back_ref[...].astype(F32)
    onehot = sum_rows(send_ref[...], ghosts, own)
    for m in range(COEF):
        back = wide[pl.ds(COEF + m, slots, stride=PIECE), :].astype(BF16)
        rows = ghost_grad_ref[m] + dot(onehot, back)
        prev_ref[m] = rows[: ghosts // 2].astype(BF16)
        next_ref[m] = rows[ghosts // 2 :].astype(BF16)


def own_kernel(send_ref, recv_ref, back_ref, own_sum_ref, own_grad_ref, update_ref, grad_ref, wide):
    slots = send_ref.shape[1]
    own = own_sum_ref.shape[1]
    wide[...] = back_ref[...].astype(F32)
    from_tgt = sum_rows(recv_ref[...], own)
    from_src = sum_rows(send_ref[...], own)
    for m in range(COEF):
        back = wide[pl.ds(m, slots, stride=PIECE), :].astype(BF16)
        update_ref[m] = (own_sum_ref[m] + dot(from_tgt, back)).astype(BF16)
        back = wide[pl.ds(COEF + m, slots, stride=PIECE), :].astype(BF16)
        grad_ref[m] = own_grad_ref[m] + dot(from_src, back)


def last_kernel(ghost_ref, grad_ref, before_ref, after_ref, out_hbm, out, sems):
    onehot = sum_rows(ghost_ref[...], grad_ref.shape[1])
    parts = sems.shape[0]
    cuts = [COEF * i // parts for i in range(parts + 1)]
    copies = []
    for i in range(parts):
        for m in range(cuts[i], cuts[i + 1]):
            out[m] = (grad_ref[m] + dot(onehot, both(before_ref[m], after_ref[m]))).astype(BF16)
        span = pl.ds(cuts[i], cuts[i + 1] - cuts[i])
        copies.append(pltpu.make_async_copy(out.at[span], out_hbm.at[span], sems.at[i]))
        copies[-1].start()
    for copy in copies:
        copy.wait()


def shape(*dims, dtype=BF16):
    return jax.ShapeDtypeStruct(dims, dtype)


def call(kernel, out_shape, scratch=(), limit=12, hbm=(), hbm_out=(), cost=(0, 0), inputs=()):
    specs = [
        pl.BlockSpec(memory_space=pltpu.HBM if i in hbm else pltpu.VMEM) for i in range(len(inputs))
    ]
    inputs = [
        pltpu.with_memory_space_constraint(x, pltpu.HBM) if i in hbm else x
        for i, x in enumerate(inputs)
    ]
    return pl.pallas_call(
        kernel,
        out_shape=jax.tree.map(
            lambda s: pltpu.HBM(s.shape, s.dtype) if s in hbm_out else s, out_shape
        ),
        in_specs=specs,
        out_specs=jax.tree.map(
            lambda s: pl.BlockSpec(memory_space=pltpu.HBM if s in hbm_out else pltpu.VMEM), out_shape
        ),
        scratch_shapes=scratch,
        compiler_params=pltpu.CompilerParams(vmem_limit_bytes=limit * MIB),
        cost_estimate=pl.CostEstimate(flops=cost[0], bytes_accessed=cost[1], transcendentals=0),
    )(*inputs)


def local(
    atoms,
    frames,
    w_zero,
    w_one,
    w_two,
    cotangent,
    ghost_rows,
    send_rows,
    recv_rows,
    edge_src,
    edge_tgt,
):
    own = atoms.shape[0]
    half = ghost_rows.shape[0] // 2
    slots = send_rows.shape[0]
    edges = edge_src.shape[0]
    ext = own + 2 * half
    cells = lax.axis_size("cell")
    up = [(i, (i + 1) % cells) for i in range(cells)]
    down = [(j, i) for i, j in up]
    atoms_t = jnp.transpose(atoms, (1, 0, 2))
    cot_t = jnp.transpose(cotangent, (1, 0, 2))
    ghost_l, send_l, recv_l, src_l, tgt_l = (
        row.reshape(1, -1) for row in (ghost_rows, send_rows, recv_rows, edge_src, edge_tgt)
    )
    pack = shape(COEF, half, LANES)
    result = shape(COEF, own, LANES)
    bundle = shape(slots * PIECE, LANES)
    wide = pltpu.VMEM((slots * PIECE, LANES), F32)
    rows = pltpu.VMEM((COEF, own, LANES), BF16)
    index = shape(1, edges, dtype=jnp.int32)
    coefs = lambda n, dtype: shape(edges, n * LANES, dtype=dtype)
    scratch = lambda s: pltpu.VMEM(s.shape, s.dtype)
    short = lambda x: pltpu.VMEM(x.shape, jnp.int32)
    exchange = lambda x: lax.all_to_all(x, "cell", 0, 0, tiled=True)
    mixing = [coefs(N0, BF16), shape(2 * edges, N1 * LANES), shape(2 * edges, N2 * LANES)]
    every = coefs(COEF, F32)
    turned = coefs(ROT, F32)
    rounded = coefs(ROT, BF16)

    to_down, to_up = call(
        pack_kernel, (pack, pack), (short(ghost_l), rows, pltpu.SemaphoreType.DMA((2,))),
        hbm=(0, 1), cost=(0, MIB), inputs=(ghost_l, atoms_t),
    )
    from_prev = lax.ppermute(to_up, "cell", up)
    from_next = lax.ppermute(to_down, "cell", down)
    part, ask = call(
        own_send_kernel, (bundle, shape(slots, 2 * half)),
        (short(send_l), short(recv_l), rows, rows, wide, pltpu.SemaphoreType.DMA((4,))),
        hbm=(0, 1, 2, 3), cost=(0, 3 * MIB), inputs=(send_l, recv_l, atoms_t, cot_t),
    )
    outgoing = call(
        send_kernel, bundle, (wide,), cost=(0, MIB),
        inputs=(ask, part, from_prev, from_next),
    )
    received = exchange(outgoing)
    spread = pltpu.VMEM((edges // ROWS, frames.shape[1], ROWS, LANES), F32)
    near = call(
        lambda *refs: local_kernel(*refs, slots),
        [turned] + mixing + [shape(*frames.shape), index, index] + [shape(edges, slots)] * 2,
        [
            scratch(turned),
            pltpu.VMEM((ext, COEF * LANES), BF16),
            pltpu.VMEM((own, COEF * LANES), BF16),
            scratch(every),
            scratch(every),
            pltpu.SemaphoreType.DMA((1,)),
        ],
        cost=(1 << 31, 24 * MIB), limit=24, hbm_out=(turned,),
        inputs=(src_l, tgt_l, frames, atoms_t, from_prev, from_next, cot_t),
    )
    near_ups, near0, near1, near2, frames_p, src_p, tgt_p, far_src, far_tgt = near
    far_rows = pltpu.VMEM((slots, COEF * LANES), BF16)
    inputs = (
        received, far_src, far_tgt, src_p, tgt_p, frames_p, near0, near1, near2, near_ups, w_zero, w_one, w_two
    )
    partial, gated, back = call(
        lambda *refs: edge_kernel(own, ext, *refs),
        (bundle, rounded, rounded),
        [scratch(x) for x in inputs[9:]]
        + [scratch(x) for x in mixing]
        + [wide, far_rows, far_rows, scratch(every), scratch(every), scratch(turned), scratch(rounded), scratch(rounded)]
        + [
            scratch(coefs(COEF, BF16)),
            spread,
            pltpu.SemaphoreType.DMA((4,)),
            pltpu.SemaphoreType.DMA((2,)),
        ],
        cost=(3 << 30, 24 * MIB), limit=44, hbm=range(9, len(inputs)), hbm_out=(rounded,),
        inputs=inputs,
    )
    returned = exchange(partial)
    own_sum, own_grad, ghost_grad = call(
        near_kernel,
        (
            shape(COEF, own, LANES, dtype=F32),
            shape(COEF, own, LANES, dtype=F32),
            shape(COEF, 2 * half, LANES, dtype=F32),
        ),
        [scratch(coefs(COEF, BF16)), spread],
        cost=(1 << 30, 20 * MIB), limit=28,
        inputs=(src_p, tgt_p, frames_p, gated, back),
    )
    to_prev, to_next = call(
        lambda *refs: ghost_kernel(own, *refs), (pack, pack), (wide,), cost=(0, MIB),
        inputs=(send_l, returned, ghost_grad),
    )
    after = lax.ppermute(to_prev, "cell", down)
    before = lax.ppermute(to_next, "cell", up)
    update, grad = call(
        own_kernel,
        (shape(COEF, own, LANES), shape(COEF, own, LANES, dtype=F32)), (wide,), cost=(0, 3 * MIB),
        inputs=(send_l, recv_l, returned, own_sum, own_grad),
    )
    atom_grads = call(
        last_kernel, result, (scratch(result), pltpu.SemaphoreType.DMA((4,))),
        hbm_out=(result,), cost=(0, 2 * MIB),
        inputs=(ghost_l, grad, before, after),
    )
    return jnp.transpose(update, (1, 0, 2)), jnp.transpose(atom_grads, (1, 0, 2))


def solution(mesh):
    whole = P(("groups", "cell"))
    return jax.shard_map(
        local,
        mesh=mesh,
        in_specs=(whole, whole, P(), P(), P()) + (whole,) * 6,
        out_specs=(whole, whole),
        check_vma=False,
    )
```
